256 devices in a mesh: dp: 4 (over x), latent: 64 (over z, y, core).
Axes of the slice: x: 4, y: 4, z: 8, core: 2. Of those that a mesh axis runs over, the one named last changes fastest.
Arguments:
- activations: bfloat16 [1024, 4608], P('dp', 'latent'), may hold values from -6 to 6
- latent_codes: bfloat16 [1024, 256], P('dp'), may hold values from 0 to 2
- active_blocks: int32 [1024, 4], P('dp'), may hold values from 0 to 2047, all different within a row; in each aligned block of 1024 rows (0 to 1023, 1024 to 2047, ...) at most 8 rows name the same one
- decoder: bfloat16 [131072, 4608], P(('dp', 'latent')), may hold values from -0.375 to 0.375
- decoder_bias: float32 [4608], P('latent'), may hold values from -3 to 3
Outputs:
- recon_error: bfloat16 [1024, 4608], P('dp', 'latent')
- decoder_grad: bfloat16 [131072, 4608], P(('dp', 'latent'))
- codes_grad: bfloat16 [1024, 256], P('dp')
The draws below stay inside these ranges and needn't reach their ends.
Inputs may be any that keep to these rules, and one draw needn't show every extreme that they name: `active_blocks`: each token names 4 different blocks; every block is named by at least one token and by at most 8 tokens, and some block by exactly 8.
All inputs are finite; a program needn't handle non-finite values.
Results may differ from the reference program's by a relative error of at most 0.0045.
Values may be sent and summed in bfloat16 or wider, within the bound.
A program may use at most 128 MiB of HBM per device.

```python
import math
import jax
import jax.numpy as jnp
import numpy as np
from jax import lax

D = 4608
LAT_BLOCK = 64
K_BLK = 4
TOKENS = 1024
NBLK = 2048
NLAT = 131072
MOST = 8


def block_levels(key, dims, split, smallest, top_value):
    loudness, own = 1.0, jax.random.fold_in(key, 6)
    for axis_at, blocks in split:
        steps = jnp.exp(jax.random.uniform(jax.random.fold_in(own, axis_at), (blocks,), jnp.float32, smallest / len(split), top_value / len(split)))
        loudness = loudness * jnp.repeat(steps, dims[axis_at] // blocks).reshape([-1 if axis == axis_at else 1 for axis in range(len(dims))])
    return loudness


def shared_out(own_key, own, number, rows, number_of, top, reach, skew):
    sequence = jax.random.permutation(own_key, number_of)
    crowded, usual = shares(number_of, rows * top, reach, skew, True), shares(number_of, rows * top, reach, skew, False)
    places = jnp.arange(number_of)

    def named(sizes, rotation):
        used = int((sizes > 0).sum())
        fixed = max(1, used // 4)
        shifted = fixed + (places - fixed + rotation * (used - fixed)) % max(1, number_of - fixed)
        return jnp.zeros((number_of,), jnp.int32).at[sequence[jnp.where(places < fixed, places, shifted)]].set(jnp.asarray(sizes, jnp.int32))

    sizes = jnp.where(number % 4 == 0, named(crowded, number // 4), named(usual, number - number // 4 - 1))
    mixed = jax.random.permutation(jax.random.fold_in(own, 3), number_of)
    giver, taker = mixed[0:number_of // 2 * 2:2], mixed[1:number_of // 2 * 2:2]
    slack = jnp.minimum(sizes[giver] - 1, reach - sizes[taker]) // 2
    slack = jnp.where((giver == sequence[0]) | (taker == sequence[0]) | (sizes[taker] == 0), 0, jnp.maximum(slack, 0))
    shifted = jax.random.randint(jax.random.fold_in(own, 4), (number_of // 2,), 0, 1 << 20) % (slack + 1)
    sizes = sizes.at[giver].add(-shifted).at[taker].add(shifted)
    items = jnp.searchsorted(jnp.cumsum(sizes), jnp.arange(rows * top), side="right").astype(jnp.int32)
    table = items.reshape(top, rows).T
    table = table[jax.random.permutation(jax.random.fold_in(own, 1), rows)]
    rotation = jax.random.randint(jax.random.fold_in(own, 2), (rows, 1), 0, top)
    return jnp.take_along_axis(table, (jnp.arange(top)[None, :] + rotation) % top, axis=1)


def shares(count, total, reach, lean, full):
    weights = [(1 << 20) // math.isqrt(rank ** lean) + 1 for rank in range(1, count + 1)]
    largest = reach if full else min(reach, max(-(-total // count), total * weights[0] // sum(weights)))
    least = 1 if total - largest >= count - 1 else 0
    counts, rest = [largest] + [least] * (count - 1), total - largest - least * (count - 1)
    while rest > 0:
        free = [i for i in range(1, count) if counts[i] < largest] or [i for i in range(1, count) if counts[i] < reach]
        pool, left = sum([weights[i] for i in free]), rest
        for i in free:
            extra = min(reach - counts[i], max(1, left * weights[i] // pool), rest)
            counts[i] = counts[i] + extra
            rest = rest - extra
    return np.array(counts)


def gaussian(stream_key, shape, scale, limit, cuts=(), kind=jnp.bfloat16):
    array = scale * jax.random.normal(stream_key, shape, jnp.float32)
    if cuts:
        array = array * block_levels(stream_key, shape, cuts, -0.22, 0.18)
    return jnp.clip(array, -limit, limit).astype(kind)


def setup_inputs(seed: int = 0) -> dict:
    arg_keys = jax.random.split(jax.random.key(seed), 6)
    activations = gaussian(arg_keys[0], (TOKENS, D), 1.0, 6.0, ((0, 4), (1, 64)))
    latent_codes = jnp.clip(2.0 * jax.random.uniform(arg_keys[1], (TOKENS, K_BLK * LAT_BLOCK), jnp.float32) ** block_levels(arg_keys[1], (TOKENS, K_BLK * LAT_BLOCK), ((0, 4),), -0.2, 0.2), 0.0, 2.0).astype(jnp.bfloat16)
    active_blocks_keys = jax.random.split(jax.random.fold_in(arg_keys[2], 1), TOKENS // TOKENS)
    active_blocks_turns = jax.random.permutation(jax.random.fold_in(arg_keys[2], 3), TOKENS // TOKENS)
    active_blocks = jax.vmap(lambda own, number: shared_out(jax.random.fold_in(arg_keys[2], 2), own, number, TOKENS, NBLK, K_BLK, MOST, 2))(active_blocks_keys, active_blocks_turns).reshape((TOKENS, K_BLK))
    decoder = gaussian(arg_keys[3], (NLAT, D), (K_BLK * LAT_BLOCK) ** -0.5, 0.375, ((0, 256),))
    decoder_bias = gaussian(arg_keys[4], (D,), 0.5, 3.0, ((0, 64),), jnp.float32)
    return {"activations": activations, "latent_codes": latent_codes, "active_blocks": active_blocks, "decoder": decoder, "decoder_bias": decoder_bias}


def reference(activations, latent_codes, active_blocks, decoder, decoder_bias):
    pair_count = TOKENS * K_BLK
    weight_blocks = decoder.reshape(NBLK, LAT_BLOCK, D)
    group_rows = 16
    starts = jnp.arange(0, TOKENS, group_rows, dtype=jnp.int32)

    def per_group(start):
        rows = lax.dynamic_slice_in_dim(activations, start, group_rows, 0)
        codes = lax.dynamic_slice_in_dim(latent_codes, start, group_rows, 0)
        codes = codes.reshape(group_rows, K_BLK, LAT_BLOCK).astype(jnp.float32)
        blocks = lax.dynamic_slice_in_dim(active_blocks, start, group_rows, 0)
        chosen = weight_blocks[blocks].astype(jnp.float32)
        summed = jnp.einsum("tkl,tkld->td", codes, chosen, precision=lax.Precision.HIGHEST)
        errors = (summed + decoder_bias[None, :] - rows.astype(jnp.float32)).astype(jnp.bfloat16)
        grads = jnp.einsum("td,tkld->tkl", errors.astype(jnp.float32), chosen, precision=lax.Precision.HIGHEST)
        return errors, grads.astype(jnp.bfloat16).reshape(group_rows, K_BLK * LAT_BLOCK)

    error_groups, grad_groups = lax.map(per_group, starts)
    recon_error = error_groups.reshape(TOKENS, D)
    codes_grad = grad_groups.reshape(TOKENS, K_BLK * LAT_BLOCK)

    flat_blocks = active_blocks.reshape(pair_count).astype(jnp.int32)
    pair_index = jnp.arange(pair_count, dtype=jnp.int32)
    order = jnp.argsort(flat_blocks, stable=True).astype(jnp.int32)
    ordered = flat_blocks[order]
    first = jnp.searchsorted(ordered, ordered, side="left").astype(jnp.int32)
    rank = jnp.zeros((pair_count,), jnp.int32).at[order].set(pair_index - first)
    slot_pair = jnp.full((NBLK * MOST,), pair_count, jnp.int32).at[flat_blocks * MOST + rank].set(pair_index)
    slot_token = (slot_pair // K_BLK).astype(jnp.int32)
    error_padded = jnp.concatenate([recon_error, jnp.zeros((1, D), recon_error.dtype)], axis=0)
    codes_padded = jnp.concatenate([latent_codes.reshape(pair_count, LAT_BLOCK), jnp.zeros((1, LAT_BLOCK), latent_codes.dtype)], axis=0)
    slot_grad = error_padded[slot_token].reshape(NBLK // 32, 32, MOST, D)
    slot_codes = codes_padded[slot_pair].reshape(NBLK // 32, 32, MOST, LAT_BLOCK)

    def per_blocks(pieces):
        codes, grads = pieces
        outer = jnp.einsum("bsl,bsd->bld", codes.astype(jnp.float32), grads.astype(jnp.float32), precision=lax.Precision.HIGHEST)
        return outer.astype(jnp.bfloat16)

    decoder_grad = lax.map(per_blocks, (slot_codes, slot_grad)).reshape(NLAT, D)
    return recon_error, decoder_grad, codes_grad
```

```python
import functools
import math

import jax
import jax.numpy as jnp
from jax import lax
from jax.experimental import pallas as pl
from jax.experimental.pallas import tpu as pltpu
from jax.sharding import PartitionSpec as P

MESH = pl.DeviceIdType.MESH
F32 = jnp.float32
BF16 = jnp.bfloat16
LAT_BLOCK = 64
BLK_DEV = 8
K_BLK = 4
MOST = 8
SLOTS = BLK_DEV * MOST
LATS = BLK_DEV * LAT_BLOCK
CODES = K_BLK * LAT_BLOCK


def dot(a, b, ca=1, cb=0):
    return lax.dot_general(a, b, (((ca,), (cb,)), ((), ())), preferred_element_type=F32)


def onehot(place, rows, first=0):
    ids = lax.broadcasted_iota(jnp.int32, (rows, place.shape[1]), 0) + first
    return jnp.where(ids == place, 1.0, 0.0).astype(BF16)


def exchange_kernel(
    X, Z, J, cap,
    ab_ref, codes_ref, act_ref, bias_ref, dec_hbm,
    recon_ref, rows_ref, own_ref, grad_ref, load_ref,
    dec, ab_all, place, c_all, q_all, zt, ecodes, codes_out, codes_in,
    part, a_out, a_in, gpt, b_out, b_in, dense, x_out, x_in, recon_all,
    b2_out, b2_in, a2_out, a2_in, yt, w_out, w_in, d_in, dense2, x2_out, x2_in, g_in,
    send_sem, recv_sem, dec_sem,
):
    T = ab_ref.shape[1]
    NT = X * T
    cw = act_ref.shape[1]
    span = Z * cw
    cs = CODES // J
    D = rows_ref.shape[1]
    d = lax.axis_index("dp")
    lat = lax.axis_index("latent")
    z = lax.div(lat, J)
    j = lax.rem(lat, J)

    def x_dev(i):
        return (i, lat)

    def z_dev(i):
        return (d, i * J + j)

    def j_dev(i):
        return (d, z * J + i)

    def to(me, n, r):
        return lax.rem(me + r, n)

    def frm(me, n, r):
        return lax.rem(me + n - r, n)

    load_dec = pltpu.make_async_copy(dec_hbm, dec, dec_sem)
    load_dec.start()

    barrier = pltpu.get_barrier_semaphore()
    peers = (
        [x_dev(to(d, X, r)) for r in range(1, X)]
        + [z_dev(to(z, Z, r)) for r in range(1, Z)]
        + [j_dev(to(j, J, r)) for r in range(1, J)]
    )
    for peer in peers:
        pl.semaphore_signal(barrier, inc=1, device_id=peer, device_id_type=MESH)
    pl.semaphore_wait(barrier, len(peers))

    sent = []

    def put(src, dst, device):
        at = len(sent)
        copy = pltpu.make_async_remote_copy(
            src_ref=src,
            dst_ref=dst,
            send_sem=send_sem.at[at],
            recv_sem=recv_sem.at[at],
            device_id=device,
            device_id_type=MESH,
        )
        copy.start()
        sent.append(copy)
        return copy

    ab_all[d] = ab_ref[...]
    copies = [put(ab_ref, ab_all.at[d], x_dev(to(d, X, r))) for r in range(1, X)]
    for copy in copies:
        copy.wait_recv()
    ab = jnp.concatenate([ab_all[i] for i in range(X)], axis=1)
    owner = ab >> int(math.log2(BLK_DEV))
    group = owner >> int(math.log2(J))

    def member(key, ids):
        named = key[0:1] == ids
        for k in range(1, K_BLK):
            named = named | (key[k : k + 1] == ids)
        return jnp.where(named, 1.0, 0.0)

    def column(n):
        return lax.broadcasted_iota(jnp.int32, (n, 1), 0)

    counts = jnp.sum(member(group, column(X * Z)), axis=1, keepdims=True)
    load_ref[...] = jnp.broadcast_to(
        jnp.max(counts, axis=0, keepdims=True), load_ref.shape
    ).astype(jnp.int32)

    pad = (-X) % 8
    row = column(X + pad)
    mem = jnp.concatenate(
        [
            member(owner, (row * Z + z) * J + j),
            member(owner, (d * Z + z) * J + column(J)),
            member(group, d * Z + column(Z)),
        ],
        axis=0,
    )
    lanes = min(128, NT)
    chunks = NT // lanes
    upto = jnp.where(
        lax.broadcasted_iota(jnp.int32, (lanes, lanes), 0)
        <= lax.broadcasted_iota(jnp.int32, (lanes, lanes), 1),
        1.0,
        0.0,
    ).astype(BF16)
    n_rows = mem.shape[0]
    stacked = jnp.concatenate(
        [mem[:, c * lanes : (c + 1) * lanes] for c in range(chunks)], axis=0
    )
    run = dot(stacked.astype(BF16), upto)
    base = jnp.zeros((n_rows, 1), F32)
    for c in range(chunks):
        here = run[c * n_rows : (c + 1) * n_rows]
        named = stacked[c * n_rows : (c + 1) * n_rows]
        place[:, c * lanes : (c + 1) * lanes] = jnp.where(
            named > 0.5, here - 1.0 + base, -1.0
        ).astype(jnp.int32)
        base = base + here[:, lanes - 1 : lanes]
    own_j = X + pad
    own_z = X + pad + J

    codes = codes_ref[...]
    for i in range(X):
        pick = onehot(place[i : i + 1, pl.ds(pl.multiple_of(d * T, T), T)], SLOTS)
        codes_out[i] = dot(pick, codes).astype(BF16)
    copies = []
    for r in range(1, X):
        i = to(d, X, r)
        copies.append(put(codes_out.at[i], codes_in.at[d], x_dev(i)))
    codes_in[d] = codes_out[d]

    def fill_q(i, carry):
        q_all[i] = onehot(place[pl.ds(own_j + i, 1), :], SLOTS)
        return carry

    lax.fori_loop(0, J, fill_q, 0)
    step = min(64, cap)
    per = cap // step

    def fill_c(n, carry):
        i = lax.div(n, per)
        first = pl.multiple_of(lax.rem(n, per) * step, step)
        c_all[i, pl.ds(first, step), :] = onehot(
            place[pl.ds(own_z + i, 1), :], step, first
        )
        return carry

    me = (d * Z + z) * J + j
    named = jnp.where(owner == me, (ab & (BLK_DEV - 1)) + 1, 0).astype(F32).astype(BF16)
    own_q = q_all[j]
    by_row = dot(own_q, named, 1, 1)
    by_col = dot(named, own_q, 1, 1)

    for copy in copies:
        copy.wait_recv()
    mine = codes_in[0].astype(F32)
    for i in range(1, X):
        mine = mine + codes_in[i].astype(F32)
    half = lax.broadcasted_iota(jnp.int32, (SLOTS, 2 * LAT_BLOCK), 1) >= LAT_BLOCK
    wide = []
    for k in range(K_BLK):
        one = mine[:, k * LAT_BLOCK : (k + 1) * LAT_BLOCK]
        wide.append(jnp.concatenate([one, one], axis=1))
    for m in range(BLK_DEV // 2):
        target = jnp.where(half, 2.0 * m + 2.0, 2.0 * m + 1.0)
        total = jnp.zeros((SLOTS, 2 * LAT_BLOCK), F32)
        for k in range(K_BLK):
            total = total + jnp.where(by_row[:, k : k + 1] == target, wide[k], 0.0)
        own_ref[:, m * 2 * LAT_BLOCK : (m + 1) * 2 * LAT_BLOCK] = total.astype(BF16)

    load_dec.wait()
    tile = 512 if D % 512 == 0 else D
    own = own_ref[...]

    def reconstruct(n, carry):
        at = pl.ds(pl.multiple_of(n * tile, tile), tile)
        part[:, at] = dot(own, dec[:, at])
        return carry

    lax.fori_loop(0, D // tile, reconstruct, 0)
    for i in range(J):
        a_out[i] = jnp.concatenate(
            [part[:, (n * J + i) * cw : (n * J + i + 1) * cw] for n in range(Z)], axis=1
        ).astype(BF16)
    copies = []
    for r in range(1, J):
        i = to(j, J, r)
        copies.append(put(a_out.at[i], a_in.at[j], j_dev(i)))
    a_in[j] = a_out[j]
    lax.fori_loop(0, Z * per, fill_c, 0)

    def fill_z(i, carry):
        zt[pl.ds(pl.multiple_of(i * SLOTS, SLOTS), SLOTS), :] = dot(
            q_all[i], c_all[z], 1, 1
        ).astype(BF16)
        return carry

    lax.fori_loop(0, J, fill_z, 0)
    for copy in copies:
        copy.wait_recv()

    arrived = a_in[...].reshape(J * SLOTS, span)
    gpt[...] = dot(arrived, zt[...], 0, 0)
    for n in range(Z):
        b_out[n] = gpt[n * cw : (n + 1) * cw, :].astype(BF16)
    copies = []
    for r in range(1, Z):
        i = to(z, Z, r)
        copies.append(put(b_out.at[i], b_in.at[z], z_dev(i)))
    b_in[z] = b_out[z]
    dense[...] = dot(b_in[z], c_all[z])
    for r in range(1, Z):
        copies[r - 1].wait_recv()
        i = frm(z, Z, r)
        dense[...] += dot(b_in[i], c_all[i])
    for i in range(X):
        x_out[i] = dense[:, i * T : (i + 1) * T]
    copies = []
    for r in range(1, X):
        i = to(d, X, r)
        copies.append(put(x_out.at[i], x_in.at[d], x_dev(i)))
    total = (bias_ref[...] - act_ref[...].astype(F32)).T + x_out[d]
    for r in range(1, X):
        copies[r - 1].wait_recv()
        total = total + x_in[frm(d, X, r)]
    recon = total.astype(BF16)
    recon_ref[...] = recon
    recon_all[d] = recon
    copies = [put(recon_ref, recon_all.at[d], x_dev(to(d, X, r))) for r in range(1, X)]
    for copy in copies:
        copy.wait_recv()

    whole = jnp.concatenate([recon_all[i] for i in range(X)], axis=1)
    copies = []
    for r in range(1, Z):
        i = to(z, Z, r)
        b2_out[i] = dot(whole, c_all[i], 1, 1).astype(BF16)
        copies.append(put(b2_out.at[i], b2_in.at[z], z_dev(i)))
    b2_in[z] = dot(whole, c_all[z], 1, 1).astype(BF16)
    for copy in copies:
        copy.wait_recv()
    flat = b2_in[...].astype(F32).reshape(span, cap).astype(BF16)
    a2_out[...] = dot(zt[...], flat, 1, 1).astype(BF16).reshape(J, SLOTS, span)
    copies = []
    for r in range(1, J):
        i = to(j, J, r)
        copies.append(put(a2_out.at[i], a2_in.at[j], j_dev(i)))
    a2_in[j] = a2_out[j]
    for copy in copies:
        copy.wait_recv()
    for m in range(Z // 2):
        pieces = [
            a2_in[i, :, n * cw : (n + 1) * cw].astype(F32)
            for n in (2 * m, 2 * m + 1)
            for i in range(J)
        ]
        width = 2 * J * cw
        rows_ref[:, m * width : (m + 1) * width] = jnp.concatenate(pieces, axis=1).astype(BF16)

    yt[...] = jnp.zeros_like(yt)

    def back(n, carry):
        at = pl.ds(pl.multiple_of(n * tile, tile), tile)
        yt[...] += dot(dec[:, at], rows_ref[:, at], 1, 1)
        return carry

    lax.fori_loop(0, D // tile, back, 0)
    for k in range(K_BLK):
        total = jnp.zeros((LAT_BLOCK, SLOTS), F32)
        for b in range(BLK_DEV):
            total = total + jnp.where(
                by_col[k : k + 1, :] == b + 1.0, yt[b * LAT_BLOCK : (b + 1) * LAT_BLOCK, :], 0.0
            )
        total = total.astype(BF16)
        for n in range(LAT_BLOCK // cs):
            w_out[k * (LAT_BLOCK // cs) + n] = total[n * cs : (n + 1) * cs]
    copies = []
    for r in range(1, J):
        i = to(j, J, r)
        copies.append(put(w_out.at[i], w_in.at[j], j_dev(i)))
    w_in[j] = w_out[j]
    for copy in copies:
        copy.wait_recv()
    merged = dot(w_in[0], zt[0:SLOTS, :])
    for i in range(1, J):
        merged = merged + dot(w_in[i], zt[i * SLOTS : (i + 1) * SLOTS, :])
    d_in[z] = merged.astype(BF16)
    copies = []
    for r in range(1, Z):
        copies.append(put(d_in.at[z], d_in.at[z], z_dev(to(z, Z, r))))
    dense2[...] = dot(d_in[z], c_all[z])
    for r in range(1, Z):
        copies[r - 1].wait_recv()
        i = frm(z, Z, r)
        dense2[...] += dot(d_in[i], c_all[i])
    for i in range(X):
        x2_out[i] = dense2[:, i * T : (i + 1) * T].astype(BF16)
    copies = []
    for r in range(1, X):
        i = to(d, X, r)
        copies.append(put(x2_out.at[i], x2_in.at[d], x_dev(i)))
    total = x2_out[d].astype(F32)
    for r in range(1, X):
        copies[r - 1].wait_recv()
        total = total + x2_in[frm(d, X, r)].astype(F32)
    g_in[j] = total.astype(BF16)
    copies = []
    for r in range(1, J):
        copies.append(put(g_in.at[j], g_in.at[j], j_dev(to(j, J, r))))
    for copy in copies:
        copy.wait_recv()
    grad_ref[...] = g_in[...].reshape(CODES, T)
    for copy in sent:
        copy.wait_send()


def exchange(X, Z, J, cap, collective_id, ab, codes, act, bias, decoder):
    T, cw = act.shape
    D = decoder.shape[1]
    NT = X * T
    span = Z * cw
    cs = CODES // J
    n_copies = 5 * (X - 1) + 3 * (Z - 1) + 4 * (J - 1)
    vmem = pltpu.VMEM
    whole = pl.BlockSpec(memory_space=pltpu.VMEM)
    rows = X + (-X) % 8 + J + Z
    return pl.pallas_call(
        functools.partial(exchange_kernel, X, Z, J, cap),
        out_shape=(
            jax.ShapeDtypeStruct((cw, T), BF16),
            jax.ShapeDtypeStruct((SLOTS, D), BF16),
            jax.ShapeDtypeStruct((SLOTS, LATS), BF16),
            jax.ShapeDtypeStruct((CODES, T), BF16),
            jax.ShapeDtypeStruct((8, 128), jnp.int32),
        ),
        in_specs=[whole] * 4 + [pl.BlockSpec(memory_space=pl.ANY)],
        out_specs=[whole] * 5,
        scratch_shapes=[
            vmem((LATS, D), BF16),
            vmem((X, 8, T), jnp.int32),
            vmem((rows, NT), jnp.int32),
            vmem((Z, cap, NT), BF16),
            vmem((J, SLOTS, NT), BF16),
            vmem((J * SLOTS, cap), BF16),
            vmem((SLOTS, CODES), BF16),
            vmem((X, SLOTS, CODES), BF16),
            vmem((X, SLOTS, CODES), BF16),
            vmem((SLOTS, D), F32),
            vmem((J, SLOTS, span), BF16),
            vmem((J, SLOTS, span), BF16),
            vmem((span, cap), F32),
            vmem((Z, cw, cap), BF16),
            vmem((Z, cw, cap), BF16),
            vmem((cw, NT), F32),
            vmem((X, cw, T), F32),
            vmem((X, cw, T), F32),
            vmem((X, cw, T), BF16),
            vmem((Z, cw, cap), BF16),
            vmem((Z, cw, cap), BF16),
            vmem((J, SLOTS, span), BF16),
            vmem((J, SLOTS, span), BF16),
            vmem((LATS, SLOTS), F32),
            vmem((J, cs, SLOTS), BF16),
            vmem((J, cs, SLOTS), BF16),
            vmem((Z, cs, cap), BF16),
            vmem((cs, NT), F32),
            vmem((X, cs, T), BF16),
            vmem((X, cs, T), BF16),
            vmem((J, cs, T), BF16),
            pltpu.SemaphoreType.DMA((n_copies,)),
            pltpu.SemaphoreType.DMA((n_copies,)),
            pltpu.SemaphoreType.DMA,
        ],
        compiler_params=pltpu.CompilerParams(
            collective_id=collective_id,
            has_side_effects=True,
            vmem_limit_bytes=52 * 2**20,
        ),
        name="exchange",
    )(ab, codes, act, bias, decoder)


def per_device(J, activations, latent_codes, active_blocks, decoder, decoder_bias):
    X = lax.axis_size("dp")
    Z = lax.axis_size("latent") // J
    ab = jnp.pad(active_blocks.T, ((0, 8 - K_BLK), (0, 0)), constant_values=-1)
    cap = min(J * SLOTS, X * activations.shape[0])
    recon, rows, own, grad, load = exchange(
        X, Z, J, cap, 0, ab, latent_codes, activations, decoder_bias[None, :], decoder
    )
    decoder_grad = dot(own, rows, 0, 0).astype(BF16)
    return recon.T, decoder_grad, grad.T


def solution(mesh):
    in_specs = (
        P("dp", "latent"),
        P("dp", None),
        P("dp", None),
        P(("dp", "latent"), None),
        P("latent"),
    )
    out_specs = (P("dp", "latent"), P(("dp", "latent"), None), P("dp", None))
    J = 8 if mesh.shape["latent"] >= 16 else 4
    return jax.shard_map(
        functools.partial(per_device, J),
        mesh=mesh, in_specs=in_specs, out_specs=out_specs, check_vma=False,
    )
```

```python
import functools
import math

import jax
import jax.numpy as jnp
from jax import lax
from jax.experimental import pallas as pl
from jax.experimental.pallas import tpu as pltpu
from jax.sharding import PartitionSpec as P

MESH = pl.DeviceIdType.MESH
F32 = jnp.float32
BF16 = jnp.bfloat16
LAT_BLOCK = 64
BLK_DEV = 8
K_BLK = 4
MOST = 8
MOST_DEV = BLK_DEV * MOST
LATS = BLK_DEV * LAT_BLOCK
CODES = K_BLK * LAT_BLOCK


def dot(a, b, ca=1, cb=0):
    return lax.dot_general(a, b, (((ca,), (cb,)), ((), ())), preferred_element_type=F32)


def iota(shape, axis):
    return lax.broadcasted_iota(jnp.int32, shape, axis)


def ones(where):
    return jnp.where(where, 1.0, 0.0)


def onehot(place, rows):
    return ones(iota((rows, place.shape[1]), 0) == place).astype(BF16)


def onehot_twice(place, rows, pack):
    ids = iota((rows * pack, place.shape[1]), 0)
    if pack == 2:
        ids = jnp.where(ids >= rows, ids - rows, ids)
    return ones(ids == place).astype(BF16)


def member(key, ids):
    named = key[0:1] == ids
    for k in range(1, K_BLK):
        named = named | (key[k : k + 1] == ids)
    return ones(named)


def exchange_kernel(
    X, Z, J, slots, cell,
    ab_hbm, codes_hbm, act_hbm, bias_hbm, dec_hbm,
    recon_ref, rows_ref, own_ref, grad_ref, over_ref,
    ab_my, codes, act, bias, dec, ab_all, c_all, q_all, zt, places, codes_out, codes_in,
    part, a_out, a_in, gpt, b_out, b_in, packed, recon_bf, b2_out, b2_in,
    a2_out, a2_in, yt, w_out, w_in, d_out, d_in, packed_d, g_in,
    send_sem, recv_sem, in_sem,
):
    T = ab_my.shape[1]
    NT = X * T
    G = X * Z
    pack = 128 // cell if cell < 128 else 1
    wide = cell * pack
    cw = act.shape[0]
    span = Z * cw
    cs = CODES // J
    D = dec.shape[1]
    top = b_out.shape[1]
    top_d = d_out.shape[1]
    d = lax.axis_index("dp")
    lat = lax.axis_index("latent")
    z = lax.div(lat, J)
    j = lax.rem(lat, J)
    g = d * Z + z

    def to(me, n, r):
        return lax.rem(me + r, n)

    def frm(me, n, r):
        return lax.rem(me + n - r, n)

    def near(n, r):
        return min(r, n - r)

    loads = [
        pltpu.make_async_copy(src, dst, in_sem.at[n])
        for n, (src, dst) in enumerate(
            ((ab_hbm, ab_my), (codes_hbm, codes), (act_hbm, act), (bias_hbm, bias), (dec_hbm, dec))
        )
    ]
    for load in loads:
        load.start()

    x_steps = sorted(range(1, X), key=lambda r: -near(X, r))
    j_steps = sorted(range(1, J), key=lambda r: -near(J, r))
    xz_steps = sorted(
        [(a, b) for a in range(X) for b in range(Z) if a + b > 0],
        key=lambda s: -near(X, s[0]) - near(Z, s[1]),
    )
    x_peers = [(to(d, X, r), lat) for r in x_steps]
    j_peers = [(d, z * J + to(j, J, r)) for r in j_steps]
    xz_peers = [(to(d, X, a), to(z, Z, b) * J + j) for a, b in xz_steps]
    barrier = pltpu.get_barrier_semaphore()
    for peer in j_peers + xz_peers:
        pl.semaphore_signal(barrier, inc=1, device_id=peer, device_id_type=MESH)

    sent = []

    def put(src, dst, device):
        at = len(sent)
        copy = pltpu.make_async_remote_copy(
            src_ref=src,
            dst_ref=dst,
            send_sem=send_sem.at[at],
            recv_sem=recv_sem.at[at],
            device_id=device,
            device_id_type=MESH,
        )
        copy.start()
        sent.append(copy)
        return copy

    lanes = min(128, T)
    per = T // lanes
    upto = ones(iota((lanes, lanes), 0) <= iota((lanes, lanes), 1)).astype(BF16)

    def running(mem):
        n = mem.shape[0]
        chunks = mem.shape[1] // lanes
        stacked = jnp.concatenate(
            [mem[:, c * lanes : (c + 1) * lanes] for c in range(chunks)], axis=0
        )
        run = dot(stacked.astype(BF16), upto)
        return [run[c * n : (c + 1) * n] for c in range(chunks)]

    def placed(mem, run, restart):
        pieces = []
        base = jnp.zeros((mem.shape[0], 1), F32)
        for c, here in enumerate(run):
            if c % restart == 0:
                base = jnp.zeros_like(base)
            named = mem[:, c * lanes : (c + 1) * lanes]
            pieces.append(jnp.where(named > 0.5, here - 1.0 + base, -1.0))
            base = base + here[:, lanes - 1 : lanes]
        return jnp.concatenate(pieces, axis=1).astype(jnp.int32)

    to_owner = int(math.log2(BLK_DEV))
    to_group = int(math.log2(J))
    for load in loads[:2]:
        load.wait()
    ab_here = ab_my[...]
    owner_here = ab_here >> to_owner
    pad_x = X + (-X) % 8
    mem = jnp.concatenate(
        [
            member(owner_here >> to_group, iota((G, 1), 0)),
            member(owner_here, (iota((pad_x, 1), 0) * Z + z) * J + j),
        ],
        axis=0,
    )
    places[...] = placed(mem, running(mem), per)
    for i in range(X):
        pick = onehot(places[G + i : G + i + 1, :], slots)
        codes_out[i] = dot(pick, codes[...]).astype(BF16)
    ab_all[d] = ab_here
    codes_in[d] = codes_out[d]
    pl.semaphore_wait(barrier, len(j_peers) + len(xz_peers))

    copies = []
    for r, peer in zip(x_steps, x_peers):
        copies.append(put(ab_my, ab_all.at[d], peer))
        copies.append(put(codes_out.at[to(d, X, r)], codes_in.at[d], peer))

    def fill_c(i, carry):
        c_all[i] = onehot_twice(places[pl.ds(i, 1), :], cell, pack)
        return carry

    lax.fori_loop(0, G, fill_c, 0)
    loads[2].wait()
    loads[3].wait()
    column = jnp.broadcast_to(bias[...], (8, cw)).T[:, 0:1]
    offset = column - act[...].astype(F32)
    for copy in copies:
        copy.wait_recv()

    ab = jnp.concatenate([ab_all[i] for i in range(X)], axis=1)
    owner = ab >> to_owner
    group = owner >> to_group
    mem_j = member(owner, g * J + iota((J + (-J) % 8, 1), 0))
    mem_own = member(owner, g * J + j + 0 * iota((8, 1), 0))
    mem_group = member(group, g + 0 * iota((8, 1), 0))
    n_j = mem_j.shape[0]
    mem = jnp.concatenate([mem_j, mem_own, mem_group], axis=0)
    run = running(mem)
    in_owner = placed(mem, run, NT // lanes)
    anew = placed(mem, run, per)
    for i in range(J):
        q_all[i] = onehot(in_owner[i : i + 1], slots)
    own_q = q_all[j]
    named = jnp.where(owner == g * J + j, (ab & (BLK_DEV - 1)) + 1, 0)
    named = jnp.concatenate([named.astype(F32), jnp.zeros((8 - K_BLK, NT), F32)], axis=0)
    named = named.astype(BF16)
    by_row = dot(own_q, named, 1, 1)
    by_col = dot(named, own_q, 1, 1)
    mine = jnp.zeros((slots, CODES), F32)
    for i in range(X):
        at = slice(i * T, (i + 1) * T)
        pick = onehot(anew[n_j : n_j + 1, at], slots)
        mine = mine + dot(dot(own_q[:, at], pick, 1, 1).astype(BF16), codes_in[i])
    half = iota((slots, 2 * LAT_BLOCK), 1) >= LAT_BLOCK
    twice = []
    for k in range(K_BLK):
        one = mine[:, k * LAT_BLOCK : (k + 1) * LAT_BLOCK]
        twice.append(jnp.concatenate([one, one], axis=1))
    for m in range(BLK_DEV // 2):
        target = jnp.where(half, 2.0 * m + 2.0, 2.0 * m + 1.0)
        total = jnp.zeros((slots, 2 * LAT_BLOCK), F32)
        for k in range(K_BLK):
            total = total + jnp.where(by_row[:, k : k + 1] == target, twice[k], 0.0)
        own_ref[:, m * 2 * LAT_BLOCK : (m + 1) * 2 * LAT_BLOCK] = total.astype(BF16)

    loads[4].wait()
    tile = 512 if D % 512 == 0 else D
    own = own_ref[...]

    def reconstruct(n, carry):
        at = pl.ds(pl.multiple_of(n * tile, tile), tile)
        part[:, at] = dot(own, dec[:, at])
        return carry

    lax.fori_loop(0, D // tile, reconstruct, 0)
    for i in range(J):
        a_out[i] = jnp.concatenate(
            [part[:, (n * J + i) * cw : (n * J + i + 1) * cw] for n in range(Z)], axis=1
        ).astype(BF16)
    copies = []
    for r, peer in zip(j_steps, j_peers):
        copies.append(put(a_out.at[to(j, J, r)], a_in.at[j], peer))
    a_in[j] = a_out[j]
    for i in range(X):
        at = slice(i * T, (i + 1) * T)
        pick = onehot_twice(anew[n_j + 8 : n_j + 9, at], cell, pack)
        zt[:, i * wide : (i + 1) * wide] = dot(
            q_all[...].reshape(J * slots, NT)[:, at], pick, 1, 1
        ).astype(BF16)
    over = jnp.zeros((1, 1), F32)
    for i in range(G * J // 64):
        count = jnp.sum(member(owner, i * 64 + iota((64, 1), 0)), axis=1, keepdims=True)
        over = over + jnp.max(ones(count > slots), axis=0, keepdims=True)
    count = member(group, iota((G, 1), 0))
    for i in range(X):
        here = jnp.sum(count[:, i * T : (i + 1) * T], axis=1, keepdims=True)
        over = over + jnp.max(ones(here > cell), axis=0, keepdims=True)
    over_ref[...] = jnp.broadcast_to(over, over_ref.shape).astype(jnp.int32)
    for copy in copies:
        copy.wait_recv()

    left = lax.rem(iota((8, wide), 1), 128) < 64
    left_row = left[0:1]

    def packs(x, rows):
        if pack == 1:
            return x
        rest = x[rows:]
        if rest.shape[0] < rows:
            rest = jnp.concatenate([rest, rest[: rows - rest.shape[0]]], axis=0)
        return jnp.where(left_row, x[:rows], rest)

    def unpacks(x, rows):
        if pack == 1:
            return x
        x = x.astype(F32)
        first = jnp.where(left_row, x, 0.0)
        rest = jnp.where(left_row, 0.0, x[: rows - x.shape[0]])
        return jnp.concatenate([first, rest], axis=0).astype(BF16)

    arrived = a_in[...].reshape(J * slots, span)
    gpt[...] = dot(arrived, zt[...], 0, 0)
    for i in range(X):
        for n in range(Z):
            b_out[i * Z + n] = packs(
                gpt[n * cw : (n + 1) * cw, i * wide : (i + 1) * wide], top
            ).astype(BF16)
    copies = []
    for (a, b), peer in zip(xz_steps, xz_peers):
        copies.append(put(b_out.at[to(d, X, a) * Z + to(z, Z, b)], b_in.at[g], peer))
    b_in[g] = b_out[g]
    for copy in copies:
        copy.wait_recv()
    for i in range(G):
        packed[:, i * wide : (i + 1) * wide] = unpacks(b_in[i], cw)
    flat_c = c_all[...].reshape(G * wide, T)
    recon = (dot(packed[...], flat_c) + offset).astype(BF16)
    recon_ref[...] = recon
    recon_bf[...] = recon

    copies = []
    for a in sorted(range(X), key=lambda r: -near(X, r)):
        x = to(d, X, a)
        back_c = c_all[pl.ds(x * Z, Z)].reshape(Z * wide, T)
        sends = dot(recon_bf[...], back_c, 1, 1)
        for n in range(Z):
            b2_out[x * Z + n] = packs(sends[:, n * wide : (n + 1) * wide], top).astype(BF16)
        for (a2, b), peer in zip(xz_steps, xz_peers):
            if a2 == a:
                copies.append(put(b2_out.at[x * Z + to(z, Z, b)], b2_in.at[g], peer))
    b2_in[g] = b2_out[g]
    for copy in copies:
        copy.wait_recv()
    pieces = []
    for n in range(Z):
        pieces.append(
            jnp.concatenate([unpacks(b2_in[i * Z + n], cw) for i in range(X)], axis=1).astype(F32)
        )
    flat = jnp.concatenate(pieces, axis=0).astype(BF16)
    a2_out[...] = dot(zt[...], flat, 1, 1).astype(BF16).reshape(J, slots, span)
    copies = []
    for r, peer in zip(j_steps, j_peers):
        copies.append(put(a2_out.at[to(j, J, r)], a2_in.at[j], peer))
    a2_in[j] = a2_out[j]
    for copy in copies:
        copy.wait_recv()
    for m in range(Z // 2):
        pieces = [
            a2_in[i, :, n * cw : (n + 1) * cw].astype(F32)
            for n in (2 * m, 2 * m + 1)
            for i in range(J)
        ]
        width = 2 * J * cw
        rows_ref[:, m * width : (m + 1) * width] = jnp.concatenate(pieces, axis=1).astype(BF16)

    yt[...] = jnp.zeros_like(yt)

    def back(n, carry):
        at = pl.ds(pl.multiple_of(n * tile, tile), tile)
        yt[...] += dot(dec[:, at], rows_ref[:, at], 1, 1)
        return carry

    lax.fori_loop(0, D // tile, back, 0)
    for k in range(K_BLK):
        total = jnp.zeros((LAT_BLOCK, slots), F32)
        for b in range(BLK_DEV):
            total = total + jnp.where(
                by_col[k : k + 1, :] == b + 1.0, yt[b * LAT_BLOCK : (b + 1) * LAT_BLOCK, :], 0.0
            )
        total = total.astype(BF16)
        for n in range(LAT_BLOCK // cs):
            w_out[k * (LAT_BLOCK // cs) + n] = total[n * cs : (n + 1) * cs]
    copies = []
    for r, peer in zip(j_steps, j_peers):
        copies.append(put(w_out.at[to(j, J, r)], w_in.at[j], peer))
    w_in[j] = w_out[j]
    for copy in copies:
        copy.wait_recv()
    merged = dot(w_in[0], zt[0:slots, :])
    for i in range(1, J):
        merged = merged + dot(w_in[i], zt[i * slots : (i + 1) * slots, :])
    for i in range(X):
        d_out[i] = packs(merged[:, i * wide : (i + 1) * wide], top_d).astype(BF16)
    copies = []
    for (a, b), peer in zip(xz_steps, xz_peers):
        copies.append(put(d_out.at[to(d, X, a)], d_in.at[g], peer))
    d_in[g] = d_out[d]
    for copy in copies:
        copy.wait_recv()
    for i in range(G):
        packed_d[:, i * wide : (i + 1) * wide] = unpacks(d_in[i], cs)
    g_in[j] = dot(packed_d[...], c_all[...].reshape(G * wide, T)).astype(BF16)
    copies = []
    for r, peer in zip(j_steps, j_peers):
        copies.append(put(g_in.at[j], g_in.at[j], peer))
    for copy in copies:
        copy.wait_recv()
    grad_ref[...] = g_in[...].reshape(CODES, T)
    for copy in sent:
        copy.wait_send()


def exchange(X, Z, J, slots, cell, collective_id, ab, codes, act, bias, decoder):
    cw, T = act.shape
    D = decoder.shape[1]
    NT = X * T
    G = X * Z
    span = Z * cw
    cs = CODES // J
    pack = 128 // cell if cell < 128 else 1
    wide = cell * pack
    top = cw if pack == 1 else -(-cw // 16) * 8
    top_d = cs if pack == 1 else cs // 2
    n_copies = 2 * (X - 1) + 3 * (G - 1) + 4 * (J - 1)
    vmem = pltpu.VMEM
    whole = pl.BlockSpec(memory_space=pltpu.VMEM)
    far = pl.BlockSpec(memory_space=pl.ANY)
    return pl.pallas_call(
        functools.partial(exchange_kernel, X, Z, J, slots, cell),
        out_shape=(
            jax.ShapeDtypeStruct((cw, T), BF16),
            jax.ShapeDtypeStruct((slots, D), BF16),
            jax.ShapeDtypeStruct((slots, LATS), BF16),
            jax.ShapeDtypeStruct((CODES, T), BF16),
            jax.ShapeDtypeStruct((8, 128), jnp.int32),
        ),
        in_specs=[far] * 5,
        out_specs=[whole] * 5,
        scratch_shapes=[
            vmem((K_BLK, T), jnp.int32),
            vmem((T, CODES), BF16),
            vmem((cw, T), BF16),
            vmem((1, cw), F32),
            vmem((LATS, D), BF16),
            vmem((X, K_BLK, T), jnp.int32),
            vmem((G, wide, T), BF16),
            vmem((J, slots, NT), BF16),
            vmem((J * slots, X * wide), BF16),
            vmem((G + X + (-X) % 8, T), jnp.int32),
            vmem((X, slots, CODES), BF16),
            vmem((X, slots, CODES), BF16),
            vmem((slots, D), F32),
            vmem((J, slots, span), BF16),
            vmem((J, slots, span), BF16),
            vmem((span, X * wide), F32),
            vmem((G, top, wide), BF16),
            vmem((G, top, wide), BF16),
            vmem((cw, G * wide), BF16),
            vmem((cw, T), BF16),
            vmem((G, top, wide), BF16),
            vmem((G, top, wide), BF16),
            vmem((J, slots, span), BF16),
            vmem((J, slots, span), BF16),
            vmem((LATS, slots), F32),
            vmem((J, cs, slots), BF16),
            vmem((J, cs, slots), BF16),
            vmem((X, top_d, wide), BF16),
            vmem((G, top_d, wide), BF16),
            vmem((cs, G * wide), BF16),
            vmem((J, cs, T), BF16),
            pltpu.SemaphoreType.DMA((n_copies,)),
            pltpu.SemaphoreType.DMA((n_copies,)),
            pltpu.SemaphoreType.DMA((5,)),
        ],
        compiler_params=pltpu.CompilerParams(
            collective_id=collective_id,
            has_side_effects=True,
            vmem_limit_bytes=52 * 2**20,
        ),
        name="exchange_%d_%d" % (slots, cell),
    )(ab, codes, act, bias, decoder)


def per_device(J, activations, latent_codes, active_blocks, decoder, decoder_bias):
    X = lax.axis_size("dp")
    Z = lax.axis_size("latent") // J
    T = activations.shape[0]
    args = (active_blocks.T, latent_codes, activations.T, decoder_bias[None, :], decoder)
    *fast, over = exchange(X, Z, J, 48, 64, 0, *args)

    def finish(recon, rows, own, grad):
        return recon.T, dot(own, rows, 0, 0).astype(BF16), grad.T

    def roomy():
        return finish(*exchange(X, Z, J, MOST_DEV, T, 1, *args)[:4])

    return lax.cond(over[0, 0] > 0, roomy, lambda: finish(*fast))


def solution(mesh):
    in_specs = (
        P("dp", "latent"),
        P("dp", None),
        P("dp", None),
        P(("dp", "latent"), None),
        P("latent"),
    )
    out_specs = (P("dp", "latent"), P(("dp", "latent"), None), P("dp", None))
    J = 8 if mesh.shape["latent"] >= 16 else 4
    return jax.shard_map(
        functools.partial(per_device, J),
        mesh=mesh, in_specs=in_specs, out_specs=out_specs, check_vma=False,
    )
```

```python
import functools
import math

import jax
import jax.numpy as jnp
from jax import lax
from jax.experimental import pallas as pl
from jax.experimental.pallas import tpu as pltpu
from jax.sharding import PartitionSpec as P

MESH = pl.DeviceIdType.MESH
F32 = jnp.float32
BF16 = jnp.bfloat16
LAT_BLOCK = 64
BLK_DEV = 8
K_BLK = 4
MOST = 8
MOST_DEV = BLK_DEV * MOST
LATS = BLK_DEV * LAT_BLOCK
CODES = K_BLK * LAT_BLOCK


def dot(a, b, ca=1, cb=0):
    return lax.dot_general(a, b, (((ca,), (cb,)), ((), ())), preferred_element_type=F32)


def iota(shape, axis):
    return lax.broadcasted_iota(jnp.int32, shape, axis)


def ones(where):
    return jnp.where(where, 1.0, 0.0)


def onehot(place, rows):
    return ones(iota((rows, place.shape[1]), 0) == place).astype(BF16)


def onehot_twice(place, rows, pack):
    ids = iota((rows * pack, place.shape[1]), 0)
    if pack == 2:
        ids = jnp.where(ids >= rows, ids - rows, ids)
    return ones(ids == place).astype(BF16)


def member(key, ids):
    named = key[0:1] == ids
    for k in range(1, K_BLK):
        named = named | (key[k : k + 1] == ids)
    return ones(named)


def exchange_kernel(
    X, Z, J, slots, cell,
    ab_hbm, codes_hbm, act_hbm, bias_hbm, dec_hbm,
    recon_ref, rows, own, grad_ref, over_ref,
    ab_my, codes, act, bias, dec, ab_all, c_all, q_all, zt, places, codes_out, codes_in,
    part, a_out, a_in, gpt, b_out, b_in, packed, recon_bf, b2_out, b2_in,
    a2_out, a2_in, yt, w_out, w_in, d_out, d_in, packed_d, g_in,
    send_sem, recv_sem, in_sem,
):
    T = ab_my.shape[1]
    NT = X * T
    G = X * Z
    pack = 128 // cell if cell < 128 else 1
    wide = cell * pack
    cw = act.shape[0]
    span = Z * cw
    cs = CODES // J
    D = dec.shape[1]
    top = b_out.shape[1]
    top_d = d_out.shape[1]
    d = lax.axis_index("dp")
    lat = lax.axis_index("latent")
    z = lax.div(lat, J)
    j = lax.rem(lat, J)
    g = d * Z + z

    def to(me, n, r):
        return lax.rem(me + r, n)

    def frm(me, n, r):
        return lax.rem(me + n - r, n)

    def near(n, r):
        return min(r, n - r)

    loads = [
        pltpu.make_async_copy(src, dst, in_sem.at[n])
        for n, (src, dst) in enumerate(
            ((ab_hbm, ab_my), (codes_hbm, codes), (act_hbm, act), (bias_hbm, bias), (dec_hbm, dec))
        )
    ]
    for load in loads:
        load.start()

    x_steps = sorted(range(1, X), key=lambda r: -near(X, r))
    j_steps = sorted(range(1, J), key=lambda r: -near(J, r))
    xz_steps = sorted(
        [(a, b) for a in range(X) for b in range(Z) if a + b > 0],
        key=lambda s: -near(X, s[0]) - near(Z, s[1]),
    )
    x_peers = [(to(d, X, r), lat) for r in x_steps]
    j_peers = [(d, z * J + to(j, J, r)) for r in j_steps]
    xz_peers = [(to(d, X, a), to(z, Z, b) * J + j) for a, b in xz_steps]
    barrier = pltpu.get_barrier_semaphore()
    for peer in j_peers + xz_peers:
        pl.semaphore_signal(barrier, inc=1, device_id=peer, device_id_type=MESH)

    sent = []

    def put(src, dst, device):
        at = len(sent)
        copy = pltpu.make_async_remote_copy(
            src_ref=src,
            dst_ref=dst,
            send_sem=send_sem.at[at],
            recv_sem=recv_sem.at[at],
            device_id=device,
            device_id_type=MESH,
        )
        copy.start()
        sent.append(copy)
        return copy

    lanes = min(128, T)
    per = T // lanes
    upto = ones(iota((lanes, lanes), 0) <= iota((lanes, lanes), 1)).astype(BF16)

    def running(mem):
        n = mem.shape[0]
        chunks = mem.shape[1] // lanes
        stacked = jnp.concatenate(
            [mem[:, c * lanes : (c + 1) * lanes] for c in range(chunks)], axis=0
        )
        run = dot(stacked.astype(BF16), upto)
        return [run[c * n : (c + 1) * n] for c in range(chunks)]

    def placed(mem, run, restart):
        pieces = []
        base = jnp.zeros((mem.shape[0], 1), F32)
        for c, here in enumerate(run):
            if c % restart == 0:
                base = jnp.zeros_like(base)
            named = mem[:, c * lanes : (c + 1) * lanes]
            pieces.append(jnp.where(named > 0.5, here - 1.0 + base, -1.0))
            base = base + here[:, lanes - 1 : lanes]
        return jnp.concatenate(pieces, axis=1).astype(jnp.int32)

    to_owner = int(math.log2(BLK_DEV))
    to_group = int(math.log2(J))
    for load in loads[:2]:
        load.wait()
    ab_here = ab_my[...]
    owner_here = ab_here >> to_owner
    mem = member(owner_here, (iota((X + (-X) % 8, 1), 0) * Z + z) * J + j)
    along = placed(mem, running(mem), per)
    for i in range(X):
        codes_out[i] = dot(onehot(along[i : i + 1], slots), codes[...]).astype(BF16)
    ab_all[d] = ab_here
    codes_in[d] = codes_out[d]
    pl.semaphore_wait(barrier, len(j_peers) + len(xz_peers))

    copies = []
    for r, peer in zip(x_steps, x_peers):
        copies.append(put(ab_my, ab_all.at[d], peer))
        copies.append(put(codes_out.at[to(d, X, r)], codes_in.at[d], peer))

    mem = member(owner_here >> to_group, iota((G, 1), 0))
    places[...] = placed(mem, running(mem), per)
    loads[2].wait()
    loads[3].wait()
    column = jnp.broadcast_to(bias[...], (8, cw)).T[:, 0:1]
    offset = column - act[...].astype(F32)
    for copy in copies:
        copy.wait_recv()

    ab = jnp.concatenate([ab_all[i] for i in range(X)], axis=1)
    owner = ab >> to_owner
    group = owner >> to_group
    mem_j = member(owner, g * J + iota((J + (-J) % 8, 1), 0))
    mem_own = member(owner, g * J + j + 0 * iota((8, 1), 0))
    mem_group = member(group, g + 0 * iota((8, 1), 0))
    n_j = mem_j.shape[0]
    mem = jnp.concatenate([mem_j, mem_own, mem_group], axis=0)
    run = running(mem)
    in_owner = placed(mem, run, NT // lanes)
    anew = placed(mem, run, per)
    for i in range(J):
        q_all[i] = onehot(in_owner[i : i + 1], slots)
    own_q = q_all[j]
    named = jnp.where(owner == g * J + j, (ab & (BLK_DEV - 1)) + 1, 0)
    named = jnp.concatenate([named.astype(F32), jnp.zeros((8 - K_BLK, NT), F32)], axis=0)
    named = named.astype(BF16)
    by_row = dot(own_q, named, 1, 1)
    by_col = dot(named, own_q, 1, 1)
    mine = jnp.zeros((slots, CODES), F32)
    for i in range(X):
        at = slice(i * T, (i + 1) * T)
        pick = onehot(anew[n_j : n_j + 1, at], slots)
        mine = mine + dot(dot(own_q[:, at], pick, 1, 1).astype(BF16), codes_in[i])
    half = iota((slots, 2 * LAT_BLOCK), 1) >= LAT_BLOCK
    twice = []
    for k in range(K_BLK):
        one = mine[:, k * LAT_BLOCK : (k + 1) * LAT_BLOCK]
        twice.append(jnp.concatenate([one, one], axis=1))
    for m in range(BLK_DEV // 2):
        target = jnp.where(half, 2.0 * m + 2.0, 2.0 * m + 1.0)
        total = jnp.zeros((slots, 2 * LAT_BLOCK), F32)
        for k in range(K_BLK):
            total = total + jnp.where(by_row[:, k : k + 1] == target, twice[k], 0.0)
        own[:, m * 2 * LAT_BLOCK : (m + 1) * 2 * LAT_BLOCK] = total.astype(BF16)

    loads[4].wait()
    tile = 512 if D % 512 == 0 else D
    own_codes = own[...]

    for n in range(D // tile):
        at = slice(n * tile, (n + 1) * tile)
        part[:, at] = dot(own_codes, dec[:, at]).astype(BF16)
    for i in range(J):
        a_out[i] = jnp.concatenate(
            [part[:, (n * J + i) * cw : (n * J + i + 1) * cw] for n in range(Z)], axis=1
        )
    copies = []
    for r, peer in zip(j_steps, j_peers):
        copies.append(put(a_out.at[to(j, J, r)], a_in.at[j], peer))
    a_in[j] = a_out[j]

    def fill_c(i, carry):
        c_all[i] = onehot_twice(places[pl.ds(i, 1), :], cell, pack)
        return carry

    lax.fori_loop(0, G, fill_c, 0)
    for i in range(X):
        at = slice(i * T, (i + 1) * T)
        pick = onehot_twice(anew[n_j + 8 : n_j + 9, at], cell, pack)
        zt[:, i * wide : (i + 1) * wide] = dot(
            q_all[...].reshape(J * slots, NT)[:, at], pick, 1, 1
        ).astype(BF16)
    over = jnp.zeros((1, 1), F32)
    part_of = min(64, G * J)
    for i in range(G * J // part_of):
        count = jnp.sum(member(owner, i * part_of + iota((part_of, 1), 0)), axis=1, keepdims=True)
        over = over + jnp.max(ones(count > slots), axis=0, keepdims=True)
    count = member(group, iota((G, 1), 0))
    for i in range(X):
        here = jnp.sum(count[:, i * T : (i + 1) * T], axis=1, keepdims=True)
        over = over + jnp.max(ones(here > cell), axis=0, keepdims=True)
    over_ref[0, 0] = jnp.max(over).astype(jnp.int32)
    for copy in copies:
        copy.wait_recv()

    left = lax.rem(iota((8, wide), 1), 128) < 64
    left_row = left[0:1]

    def packs(x, rows):
        if pack == 1:
            return x
        rest = x[rows:]
        if rest.shape[0] < rows:
            rest = jnp.concatenate([rest, rest[: rows - rest.shape[0]]], axis=0)
        return jnp.where(left_row, x[:rows], rest)

    def unpacks(x, rows):
        if pack == 1:
            return x
        x = x.astype(F32)
        first = jnp.where(left_row, x, 0.0)
        rest = jnp.where(left_row, 0.0, x[: rows - x.shape[0]])
        return jnp.concatenate([first, rest], axis=0).astype(BF16)

    arrived = a_in[...].reshape(J * slots, span)
    gpt[...] = dot(arrived, zt[...], 0, 0)
    for i in range(X):
        for n in range(Z):
            b_out[i * Z + n] = packs(
                gpt[n * cw : (n + 1) * cw, i * wide : (i + 1) * wide], top
            ).astype(BF16)
    copies = []
    for (a, b), peer in zip(xz_steps, xz_peers):
        copies.append(put(b_out.at[to(d, X, a) * Z + to(z, Z, b)], b_in.at[g], peer))
    b_in[g] = b_out[g]
    for copy in copies:
        copy.wait_recv()
    for i in range(G):
        packed[:, i * wide : (i + 1) * wide] = unpacks(b_in[i], cw)
    flat_c = c_all[...].reshape(G * wide, T)
    recon = (dot(packed[...], flat_c) + offset).astype(BF16)
    recon_ref[...] = recon
    recon_bf[...] = recon

    copies = []
    for a in sorted(range(X), key=lambda r: -near(X, r)):
        x = to(d, X, a)
        back_c = c_all[pl.ds(x * Z, Z)].reshape(Z * wide, T)
        sends = dot(recon_bf[...], back_c, 1, 1)
        for n in range(Z):
            b2_out[x * Z + n] = packs(sends[:, n * wide : (n + 1) * wide], top).astype(BF16)
        for (a2, b), peer in zip(xz_steps, xz_peers):
            if a2 == a:
                copies.append(put(b2_out.at[x * Z + to(z, Z, b)], b2_in.at[g], peer))
    b2_in[g] = b2_out[g]
    for copy in copies:
        copy.wait_recv()
    pieces = []
    for n in range(Z):
        pieces.append(
            jnp.concatenate([unpacks(b2_in[i * Z + n], cw) for i in range(X)], axis=1).astype(F32)
        )
    flat = jnp.concatenate(pieces, axis=0).astype(BF16)
    a2_out[...] = dot(zt[...], flat, 1, 1).astype(BF16).reshape(J, slots, span)
    copies = []
    for r, peer in zip(j_steps, j_peers):
        copies.append(put(a2_out.at[to(j, J, r)], a2_in.at[j], peer))
    a2_in[j] = a2_out[j]
    for copy in copies:
        copy.wait_recv()
    for m in range(Z // 2):
        pieces = [
            a2_in[i, :, n * cw : (n + 1) * cw]
            for n in (2 * m, 2 * m + 1)
            for i in range(J)
        ]
        width = 2 * J * cw
        rows[:, m * width : (m + 1) * width] = jnp.concatenate(pieces, axis=1)

    yt[...] = dot(dec[...], rows[...], 1, 1)
    for k in range(K_BLK):
        total = jnp.zeros((LAT_BLOCK, slots), F32)
        for b in range(BLK_DEV):
            total = total + jnp.where(
                by_col[k : k + 1, :] == b + 1.0, yt[b * LAT_BLOCK : (b + 1) * LAT_BLOCK, :], 0.0
            )
        total = total.astype(BF16)
        for n in range(LAT_BLOCK // cs):
            w_out[k * (LAT_BLOCK // cs) + n] = total[n * cs : (n + 1) * cs]
    copies = []
    for r, peer in zip(j_steps, j_peers):
        copies.append(put(w_out.at[to(j, J, r)], w_in.at[j], peer))
    w_in[j] = w_out[j]
    for copy in copies:
        copy.wait_recv()
    merged = dot(w_in[0], zt[0:slots, :])
    for i in range(1, J):
        merged = merged + dot(w_in[i], zt[i * slots : (i + 1) * slots, :])
    for i in range(X):
        d_out[i] = packs(merged[:, i * wide : (i + 1) * wide], top_d).astype(BF16)
    copies = []
    for (a, b), peer in zip(xz_steps, xz_peers):
        copies.append(put(d_out.at[to(d, X, a)], d_in.at[g], peer))
    d_in[g] = d_out[d]
    for copy in copies:
        copy.wait_recv()
    for i in range(G):
        packed_d[:, i * wide : (i + 1) * wide] = unpacks(d_in[i], cs)
    g_in[j] = dot(packed_d[...], c_all[...].reshape(G * wide, T)).astype(BF16)
    copies = []
    for r, peer in zip(j_steps, j_peers):
        copies.append(put(g_in.at[j], g_in.at[j], peer))
    for copy in copies:
        copy.wait_recv()
    grad_ref[...] = g_in[...].reshape(CODES, T)
    for copy in sent:
        copy.wait_send()


def exchange(X, Z, J, slots, cell, collective_id, ab, codes, act, bias, decoder):
    cw, T = act.shape
    D = decoder.shape[1]
    NT = X * T
    G = X * Z
    span = Z * cw
    cs = CODES // J
    pack = 128 // cell if cell < 128 else 1
    wide = cell * pack
    top = cw if pack == 1 else -(-cw // 16) * 8
    top_d = cs if pack == 1 else cs // 2
    n_copies = 2 * (X - 1) + 3 * (G - 1) + 4 * (J - 1)
    vmem = pltpu.VMEM
    whole = pl.BlockSpec(memory_space=pltpu.VMEM)
    far = pl.BlockSpec(memory_space=pl.ANY)
    return pl.pallas_call(
        functools.partial(exchange_kernel, X, Z, J, slots, cell),
        out_shape=(
            jax.ShapeDtypeStruct((cw, T), BF16),
            jax.ShapeDtypeStruct((slots, D), BF16),
            jax.ShapeDtypeStruct((slots, LATS), BF16),
            jax.ShapeDtypeStruct((CODES, T), BF16),
            jax.ShapeDtypeStruct((1, 1), jnp.int32),
        ),
        in_specs=[far] * 5,
        out_specs=[whole] * 4 + [pl.BlockSpec(memory_space=pltpu.SMEM)],
        scratch_shapes=[
            vmem((K_BLK, T), jnp.int32),
            vmem((T, CODES), BF16),
            vmem((cw, T), BF16),
            vmem((1, cw), F32),
            vmem((LATS, D), BF16),
            vmem((X, K_BLK, T), jnp.int32),
            vmem((G, wide, T), BF16),
            vmem((J, slots, NT), BF16),
            vmem((J * slots, X * wide), BF16),
            vmem((G, T), jnp.int32),
            vmem((X, slots, CODES), BF16),
            vmem((X, slots, CODES), BF16),
            vmem((slots, D), BF16),
            vmem((J, slots, span), BF16),
            vmem((J, slots, span), BF16),
            vmem((span, X * wide), F32),
            vmem((G, top, wide), BF16),
            vmem((G, top, wide), BF16),
            vmem((cw, G * wide), BF16),
            vmem((cw, T), BF16),
            vmem((G, top, wide), BF16),
            vmem((G, top, wide), BF16),
            vmem((J, slots, span), BF16),
            vmem((J, slots, span), BF16),
            vmem((LATS, slots), F32),
            vmem((J, cs, slots), BF16),
            vmem((J, cs, slots), BF16),
            vmem((X, top_d, wide), BF16),
            vmem((G, top_d, wide), BF16),
            vmem((cs, G * wide), BF16),
            vmem((J, cs, T), BF16),
            pltpu.SemaphoreType.DMA((n_copies,)),
            pltpu.SemaphoreType.DMA((n_copies,)),
            pltpu.SemaphoreType.DMA((5,)),
        ],
        compiler_params=pltpu.CompilerParams(
            collective_id=collective_id,
            has_side_effects=True,
            vmem_limit_bytes=52 * 2**20,
        ),
        name="exchange_%d_%d" % (slots, cell),
    )(ab, codes, act, bias, decoder)


def finish_kernel(recon_in, rows_ref, own_ref, grad_in, recon_out, dgrad_ref, grad_out):
    @pl.when(pl.program_id(0) == 0)
    def _():
        recon_out[...] = recon_in[...]
        grad_out[...] = grad_in[...].T

    dgrad_ref[...] = dot(own_ref[...], rows_ref[...], 0, 0).astype(BF16)


def finish(recon, rows, own, grad):
    slots, D = rows.shape
    tile = 512 if D % 512 == 0 else D
    CO, T = grad.shape

    def fixed(shape):
        return pl.BlockSpec(shape, lambda n: (0, 0))

    recon, decoder_grad, grad = pl.pallas_call(
        finish_kernel,
        grid=(D // tile,),
        out_shape=(
            jax.ShapeDtypeStruct(recon.shape, BF16),
            jax.ShapeDtypeStruct((LATS, D), BF16),
            jax.ShapeDtypeStruct((T, CO), BF16),
        ),
        in_specs=[
            fixed(recon.shape),
            pl.BlockSpec((slots, tile), lambda n: (0, n)),
            fixed(own.shape),
            fixed(grad.shape),
        ],
        out_specs=[
            fixed(recon.shape),
            pl.BlockSpec((LATS, tile), lambda n: (0, n)),
            fixed((T, CO)),
        ],
        cost_estimate=pl.CostEstimate(
            flops=2 * slots * LATS * D, bytes_accessed=2 * LATS * D, transcendentals=0
        ),
        name="finish_%d" % slots,
    )(recon, rows, own, grad)
    return recon, decoder_grad, grad


def per_device(J, activations, latent_codes, active_blocks, decoder, decoder_bias):
    X = lax.axis_size("dp")
    Z = lax.axis_size("latent") // J
    T = activations.shape[0]
    args = (active_blocks.T, latent_codes, activations.T, decoder_bias[None, :], decoder)
    *fast, over = exchange(X, Z, J, 40, 64, 0, *args)

    def roomy():
        return finish(*exchange(X, Z, J, MOST_DEV, T, 1, *args)[:4])

    recon, decoder_grad, grad = lax.cond(over[0, 0] > 0, roomy, lambda: finish(*fast))
    return recon.T, decoder_grad, grad


def solution(mesh):
    in_specs = (
        P("dp", "latent"),
        P("dp", None),
        P("dp", None),
        P(("dp", "latent"), None),
        P("latent"),
    )
    out_specs = (P("dp", "latent"), P(("dp", "latent"), None), P("dp", None))
    J = 8 if mesh.shape["latent"] >= 16 else 4
    return jax.shard_map(
        functools.partial(per_device, J),
        mesh=mesh, in_specs=in_specs, out_specs=out_specs, check_vma=False,
    )
```

```python
import functools
import math

import jax
import jax.numpy as jnp
from jax import lax
from jax.experimental import pallas as pl
from jax.experimental.pallas import tpu as pltpu
from jax.sharding import PartitionSpec as P

MESH = pl.DeviceIdType.MESH
F32 = jnp.float32
BF16 = jnp.bfloat16
LAT_BLOCK = 64
BLK_DEV = 8
K_BLK = 4
MOST = 8
MOST_DEV = BLK_DEV * MOST
LATS = BLK_DEV * LAT_BLOCK
CODES = K_BLK * LAT_BLOCK


def dot(a, b, ca=1, cb=0):
    return lax.dot_general(a, b, (((ca,), (cb,)), ((), ())), preferred_element_type=F32)


def iota(shape, axis):
    return lax.broadcasted_iota(jnp.int32, shape, axis)


def ones(where):
    return jnp.where(where, 1.0, 0.0)


def onehot(place, rows):
    return ones(iota((rows, place.shape[1]), 0) == place).astype(BF16)


def onehot_twice(place, rows, pack):
    ids = iota((rows * pack, place.shape[1]), 0)
    if pack == 2:
        ids = jnp.where(ids >= rows, ids - rows, ids)
    return ones(ids == place).astype(BF16)


def member(key, ids):
    named = key[0:1] == ids
    for k in range(1, K_BLK):
        named = named | (key[k : k + 1] == ids)
    return ones(named)


def exchange_kernel(
    X, Z, J, slots, cell,
    ab_hbm, codes_hbm, act_hbm, bias_hbm, dec_hbm,
    recon_ref, rows, own, grad_ref, over_ref,
    ab_my, codes, act, bias, dec, ab_all, c_all, q_all, zt, places, codes_out, codes_in,
    part, a_out, a_in, gpt, b_out, b_in, packed, recon_bf, b2_out, b2_in,
    a2_out, a2_in, yt, w_out, w_in, d_out, d_in, packed_d, g_in,
    send_sem, recv_sem, in_sem,
):
    T = ab_my.shape[1]
    NT = X * T
    G = X * Z
    pack = 128 // cell if cell < 128 else 1
    wide = cell * pack
    cw = act.shape[0]
    span = Z * cw
    cs = CODES // J
    D = dec.shape[1]
    top = b_out.shape[1]
    top_d = d_out.shape[1]
    d = lax.axis_index("dp")
    lat = lax.axis_index("latent")
    z = lax.div(lat, J)
    j = lax.rem(lat, J)
    g = d * Z + z

    def to(me, n, r):
        return lax.rem(me + r, n)

    def frm(me, n, r):
        return lax.rem(me + n - r, n)

    def near(n, r):
        return min(r, n - r)

    loads = [
        pltpu.make_async_copy(src, dst, in_sem.at[n])
        for n, (src, dst) in enumerate(
            ((ab_hbm, ab_my), (codes_hbm, codes), (act_hbm, act), (bias_hbm, bias), (dec_hbm, dec))
        )
    ]
    for load in loads:
        load.start()

    x_steps = sorted(range(1, X), key=lambda r: -near(X, r))
    j_steps = sorted(range(1, J), key=lambda r: -near(J, r))
    xz_steps = sorted(
        [(a, b) for a in range(X) for b in range(Z) if a + b > 0],
        key=lambda s: -near(X, s[0]) - near(Z, s[1]),
    )
    x_peers = [(to(d, X, r), lat) for r in x_steps]
    j_peers = [(d, z * J + to(j, J, r)) for r in j_steps]
    xz_peers = [(to(d, X, a), to(z, Z, b) * J + j) for a, b in xz_steps]
    barrier = pltpu.get_barrier_semaphore()
    for peer in j_peers + xz_peers:
        pl.semaphore_signal(barrier, inc=1, device_id=peer, device_id_type=MESH)

    sent = []

    def put(src, dst, device):
        at = len(sent)
        copy = pltpu.make_async_remote_copy(
            src_ref=src,
            dst_ref=dst,
            send_sem=send_sem.at[at],
            recv_sem=recv_sem.at[at],
            device_id=device,
            device_id_type=MESH,
        )
        copy.start()
        sent.append(copy)
        return copy

    lanes = min(128, T)
    per = T // lanes
    upto = ones(iota((lanes, lanes), 0) <= iota((lanes, lanes), 1)).astype(BF16)

    def running(mem):
        n = mem.shape[0]
        chunks = mem.shape[1] // lanes
        stacked = jnp.concatenate(
            [mem[:, c * lanes : (c + 1) * lanes] for c in range(chunks)], axis=0
        )
        run = dot(stacked.astype(BF16), upto)
        return [run[c * n : (c + 1) * n] for c in range(chunks)]

    def placed(mem, run, restart):
        pieces = []
        base = jnp.zeros((mem.shape[0], 1), F32)
        for c, here in enumerate(run):
            if c % restart == 0:
                base = jnp.zeros_like(base)
            named = mem[:, c * lanes : (c + 1) * lanes]
            pieces.append(jnp.where(named > 0.5, here - 1.0 + base, -1.0))
            base = base + here[:, lanes - 1 : lanes]
        return jnp.concatenate(pieces, axis=1).astype(jnp.int32)

    to_owner = int(math.log2(BLK_DEV))
    to_group = int(math.log2(J))
    for load in loads[:2]:
        load.wait()
    ab_here = ab_my[...]
    owner_here = ab_here >> to_owner
    mem = member(owner_here, (iota((X + (-X) % 8, 1), 0) * Z + z) * J + j)
    along = placed(mem, running(mem), per)
    for i in range(X):
        codes_out[i] = dot(onehot(along[i : i + 1], slots), codes[...]).astype(BF16)
    ab_all[d] = ab_here
    codes_in[d] = codes_out[d]
    pl.semaphore_wait(barrier, len(j_peers) + len(xz_peers))

    copies = []
    for r, peer in zip(x_steps, x_peers):
        copies.append(put(ab_my, ab_all.at[d], peer))
        copies.append(put(codes_out.at[to(d, X, r)], codes_in.at[d], peer))

    mem = member(owner_here >> to_group, iota((G, 1), 0))
    places[...] = placed(mem, running(mem), per)
    loads[2].wait()
    loads[3].wait()
    column = jnp.broadcast_to(bias[...], (8, cw)).T[:, 0:1]
    offset = column - act[...].astype(F32)
    for copy in copies:
        copy.wait_recv()

    ab = jnp.concatenate([ab_all[i] for i in range(X)], axis=1)
    owner = ab >> to_owner
    group = owner >> to_group
    mem_j = member(owner, g * J + iota((J + (-J) % 8, 1), 0))
    mem_own = member(owner, g * J + j + 0 * iota((8, 1), 0))
    mem_group = member(group, g + 0 * iota((8, 1), 0))
    n_j = mem_j.shape[0]
    mem = jnp.concatenate([mem_j, mem_own, mem_group], axis=0)
    run = running(mem)
    in_owner = placed(mem, run, NT // lanes)
    anew = placed(mem, run, per)
    for i in range(J):
        q_all[i] = onehot(in_owner[i : i + 1], slots)
    own_q = q_all[j]
    named = jnp.where(owner == g * J + j, (ab & (BLK_DEV - 1)) + 1, 0)
    named = jnp.concatenate([named.astype(F32), jnp.zeros((8 - K_BLK, NT), F32)], axis=0)
    named = named.astype(BF16)
    by_row = dot(own_q, named, 1, 1)
    by_col = dot(named, own_q, 1, 1)
    mine = jnp.zeros((slots, CODES), F32)
    for i in range(X):
        at = slice(i * T, (i + 1) * T)
        pick = onehot(anew[n_j : n_j + 1, at], slots)
        mine = mine + dot(dot(own_q[:, at], pick, 1, 1).astype(BF16), codes_in[i])
    half = iota((slots, 2 * LAT_BLOCK), 1) >= LAT_BLOCK
    twice = []
    for k in range(K_BLK):
        one = mine[:, k * LAT_BLOCK : (k + 1) * LAT_BLOCK]
        twice.append(jnp.concatenate([one, one], axis=1))
    for m in range(BLK_DEV // 2):
        target = jnp.where(half, 2.0 * m + 2.0, 2.0 * m + 1.0)
        total = jnp.zeros((slots, 2 * LAT_BLOCK), F32)
        for k in range(K_BLK):
            total = total + jnp.where(by_row[:, k : k + 1] == target, twice[k], 0.0)
        own[:, m * 2 * LAT_BLOCK : (m + 1) * 2 * LAT_BLOCK] = total.astype(BF16)

    loads[4].wait()
    tile = 512 if D % 512 == 0 else D
    own_codes = own[...]

    for n in range(D // tile):
        at = slice(n * tile, (n + 1) * tile)
        part[:, at] = dot(own_codes, dec[:, at]).astype(BF16)
    for i in range(J):
        a_out[i] = jnp.concatenate(
            [part[:, (n * J + i) * cw : (n * J + i + 1) * cw] for n in range(Z)], axis=1
        )
    copies = []
    for r, peer in zip(j_steps, j_peers):
        copies.append(put(a_out.at[to(j, J, r)], a_in.at[j], peer))
    a_in[j] = a_out[j]

    def fill_c(i, carry):
        c_all[i] = onehot_twice(places[pl.ds(i, 1), :], cell, pack)
        return carry

    lax.fori_loop(0, G, fill_c, 0)
    for i in range(X):
        at = slice(i * T, (i + 1) * T)
        pick = onehot_twice(anew[n_j + 8 : n_j + 9, at], cell, pack)
        zt[:, i * wide : (i + 1) * wide] = dot(
            q_all[...].reshape(J * slots, NT)[:, at], pick, 1, 1
        ).astype(BF16)
    over = jnp.zeros((1, 1), F32)
    part_of = min(64, G * J)
    for i in range(G * J // part_of):
        count = jnp.sum(member(owner, i * part_of + iota((part_of, 1), 0)), axis=1, keepdims=True)
        over = over + jnp.max(ones(count > slots), axis=0, keepdims=True)
    count = member(group, iota((G, 1), 0))
    for i in range(X):
        here = jnp.sum(count[:, i * T : (i + 1) * T], axis=1, keepdims=True)
        over = over + jnp.max(ones(here > cell), axis=0, keepdims=True)
    over_ref[0, 0] = jnp.max(over).astype(jnp.int32)
    for copy in copies:
        copy.wait_recv()

    left = lax.rem(iota((8, wide), 1), 128) < 64
    left_row = left[0:1]

    def packs(x, rows):
        if pack == 1:
            return x
        rest = x[rows:]
        if rest.shape[0] < rows:
            rest = jnp.concatenate([rest, rest[: rows - rest.shape[0]]], axis=0)
        return jnp.where(left_row, x[:rows], rest)

    def unpacks(x, rows):
        if pack == 1:
            return x
        x = x.astype(F32)
        first = jnp.where(left_row, x, 0.0)
        rest = jnp.where(left_row, 0.0, x[: rows - x.shape[0]])
        return jnp.concatenate([first, rest], axis=0).astype(BF16)

    arrived = a_in[...].reshape(J * slots, span)
    gpt[...] = dot(arrived, zt[...], 0, 0)
    for i in range(X):
        for n in range(Z):
            b_out[i * Z + n] = packs(
                gpt[n * cw : (n + 1) * cw, i * wide : (i + 1) * wide], top
            ).astype(BF16)
    copies = []
    for (a, b), peer in zip(xz_steps, xz_peers):
        copies.append(put(b_out.at[to(d, X, a) * Z + to(z, Z, b)], b_in.at[g], peer))
    b_in[g] = b_out[g]
    for copy in copies:
        copy.wait_recv()
    for i in range(G):
        packed[:, i * wide : (i + 1) * wide] = unpacks(b_in[i], cw)
    flat_c = c_all[...].reshape(G * wide, T)
    recon = (dot(packed[...], flat_c) + offset).astype(BF16)
    recon_ref[...] = recon
    recon_bf[...] = recon

    copies = []
    for a in sorted(range(X), key=lambda r: -near(X, r)):
        x = to(d, X, a)
        back_c = c_all[pl.ds(x * Z, Z)].reshape(Z * wide, T)
        sends = dot(recon_bf[...], back_c, 1, 1)
        for n in range(Z):
            b2_out[x * Z + n] = packs(sends[:, n * wide : (n + 1) * wide], top).astype(BF16)
        for (a2, b), peer in zip(xz_steps, xz_peers):
            if a2 == a:
                copies.append(put(b2_out.at[x * Z + to(z, Z, b)], b2_in.at[g], peer))
    b2_in[g] = b2_out[g]
    for copy in copies:
        copy.wait_recv()
    pieces = []
    for n in range(Z):
        pieces.append(
            jnp.concatenate([unpacks(b2_in[i * Z + n], cw) for i in range(X)], axis=1).astype(F32)
        )
    flat = jnp.concatenate(pieces, axis=0).astype(BF16)
    a2_out[...] = dot(zt[...], flat, 1, 1).astype(BF16).reshape(J, slots, span)
    copies = []
    for r, peer in zip(j_steps, j_peers):
        copies.append(put(a2_out.at[to(j, J, r)], a2_in.at[j], peer))
    a2_in[j] = a2_out[j]
    for copy in copies:
        copy.wait_recv()
    for m in range(Z // 2):
        pieces = [
            a2_in[i, :, n * cw : (n + 1) * cw]
            for n in (2 * m, 2 * m + 1)
            for i in range(J)
        ]
        width = 2 * J * cw
        rows[:, m * width : (m + 1) * width] = jnp.concatenate(pieces, axis=1)

    yt[...] = dot(dec[...], rows[...], 1, 1)
    for k in range(K_BLK):
        total = jnp.zeros((LAT_BLOCK, slots), F32)
        for b in range(BLK_DEV):
            total = total + jnp.where(
                by_col[k : k + 1, :] == b + 1.0, yt[b * LAT_BLOCK : (b + 1) * LAT_BLOCK, :], 0.0
            )
        total = total.astype(BF16)
        for n in range(LAT_BLOCK // cs):
            w_out[k * (LAT_BLOCK // cs) + n] = total[n * cs : (n + 1) * cs]
    copies = []
    for r, peer in zip(j_steps, j_peers):
        copies.append(put(w_out.at[to(j, J, r)], w_in.at[j], peer))
    w_in[j] = w_out[j]
    for copy in copies:
        copy.wait_recv()
    merged = dot(w_in[0], zt[0:slots, :])
    for i in range(1, J):
        merged = merged + dot(w_in[i], zt[i * slots : (i + 1) * slots, :])
    for i in range(X):
        d_out[i] = packs(merged[:, i * wide : (i + 1) * wide], top_d).astype(BF16)
    copies = []
    for (a, b), peer in zip(xz_steps, xz_peers):
        copies.append(put(d_out.at[to(d, X, a)], d_in.at[g], peer))
    d_in[g] = d_out[d]
    for copy in copies:
        copy.wait_recv()
    for i in range(G):
        packed_d[:, i * wide : (i + 1) * wide] = unpacks(d_in[i], cs)
    g_in[j] = dot(packed_d[...], c_all[...].reshape(G * wide, T)).astype(BF16)
    copies = []
    for r, peer in zip(j_steps, j_peers):
        copies.append(put(g_in.at[j], g_in.at[j], peer))
    for copy in copies:
        copy.wait_recv()
    grad_ref[...] = g_in[...].reshape(CODES, T)
    for copy in sent:
        copy.wait_send()


def exchange(X, Z, J, slots, cell, collective_id, ab, codes, act, bias, decoder):
    cw, T = act.shape
    D = decoder.shape[1]
    NT = X * T
    G = X * Z
    span = Z * cw
    cs = CODES // J
    pack = 128 // cell if cell < 128 else 1
    wide = cell * pack
    top = cw if pack == 1 else -(-cw // 16) * 8
    top_d = cs if pack == 1 else cs // 2
    n_copies = 2 * (X - 1) + 3 * (G - 1) + 4 * (J - 1)
    vmem = pltpu.VMEM
    whole = pl.BlockSpec(memory_space=pltpu.VMEM)
    far = pl.BlockSpec(memory_space=pl.ANY)
    return pl.pallas_call(
        functools.partial(exchange_kernel, X, Z, J, slots, cell),
        out_shape=(
            jax.ShapeDtypeStruct((cw, T), BF16),
            jax.ShapeDtypeStruct((slots, D), BF16),
            jax.ShapeDtypeStruct((slots, LATS), BF16),
            jax.ShapeDtypeStruct((CODES, T), BF16),
            jax.ShapeDtypeStruct((1, 1), jnp.int32),
        ),
        in_specs=[far] * 5,
        out_specs=[whole] * 4 + [pl.BlockSpec(memory_space=pltpu.SMEM)],
        scratch_shapes=[
            vmem((K_BLK, T), jnp.int32),
            vmem((T, CODES), BF16),
            vmem((cw, T), BF16),
            vmem((1, cw), F32),
            vmem((LATS, D), BF16),
            vmem((X, K_BLK, T), jnp.int32),
            vmem((G, wide, T), BF16),
            vmem((J, slots, NT), BF16),
            vmem((J * slots, X * wide), BF16),
            vmem((G, T), jnp.int32),
            vmem((X, slots, CODES), BF16),
            vmem((X, slots, CODES), BF16),
            vmem((slots, D), BF16),
            vmem((J, slots, span), BF16),
            vmem((J, slots, span), BF16),
            vmem((span, X * wide), F32),
            vmem((G, top, wide), BF16),
            vmem((G, top, wide), BF16),
            vmem((cw, G * wide), BF16),
            vmem((cw, T), BF16),
            vmem((G, top, wide), BF16),
            vmem((G, top, wide), BF16),
            vmem((J, slots, span), BF16),
            vmem((J, slots, span), BF16),
            vmem((LATS, slots), F32),
            vmem((J, cs, slots), BF16),
            vmem((J, cs, slots), BF16),
            vmem((X, top_d, wide), BF16),
            vmem((G, top_d, wide), BF16),
            vmem((cs, G * wide), BF16),
            vmem((J, cs, T), BF16),
            pltpu.SemaphoreType.DMA((n_copies,)),
            pltpu.SemaphoreType.DMA((n_copies,)),
            pltpu.SemaphoreType.DMA((5,)),
        ],
        compiler_params=pltpu.CompilerParams(
            collective_id=collective_id,
            has_side_effects=True,
            vmem_limit_bytes=52 * 2**20,
        ),
        name="exchange_%d_%d" % (slots, cell),
    )(ab, codes, act, bias, decoder)


def finish_kernel(
    recon_in, rows, own, grad_in, recon_out, dgrad_out, grad_out, dgrad, grad, sem
):
    copies = [pltpu.make_async_copy(recon_in, recon_out, sem.at[0])]
    copies[0].start()
    parts = sem.shape[0] - 2
    height = LATS // parts
    for n in range(parts):
        at = slice(n * height, (n + 1) * height)
        dgrad[at, :] = dot(own[:, at], rows[...], 0, 0).astype(BF16)
        copies.append(pltpu.make_async_copy(dgrad.at[at], dgrad_out.at[at], sem.at[2 + n]))
        copies[-1].start()
        if n == 0:
            grad[...] = grad_in[...].T
            copies.append(pltpu.make_async_copy(grad, grad_out, sem.at[1]))
            copies[-1].start()
    for copy in copies:
        copy.wait()


def finish(recon, rows, own, grad):
    slots, D = rows.shape
    CO, T = grad.shape
    whole = pl.BlockSpec(memory_space=pltpu.VMEM)
    far = pl.BlockSpec(memory_space=pl.ANY)
    return pl.pallas_call(
        finish_kernel,
        out_shape=(
            jax.ShapeDtypeStruct(recon.shape, BF16),
            jax.ShapeDtypeStruct((LATS, D), BF16),
            jax.ShapeDtypeStruct((T, CO), BF16),
        ),
        in_specs=[whole] * 4,
        out_specs=[far] * 3,
        scratch_shapes=[
            pltpu.VMEM((LATS, D), BF16),
            pltpu.VMEM((T, CO), BF16),
            pltpu.SemaphoreType.DMA((6,)),
        ],
        compiler_params=pltpu.CompilerParams(vmem_limit_bytes=32 * 2**20),
        cost_estimate=pl.CostEstimate(
            flops=2 * slots * LATS * D, bytes_accessed=2 * LATS * D, transcendentals=0
        ),
        name="finish_%d" % slots,
    )(recon, rows, own, grad)


def per_device(J, activations, latent_codes, active_blocks, decoder, decoder_bias):
    X = lax.axis_size("dp")
    Z = lax.axis_size("latent") // J
    T = activations.shape[0]
    args = (active_blocks.T, latent_codes, activations.T, decoder_bias[None, :], decoder)
    *fast, over = exchange(X, Z, J, 40, 64, 0, *args)

    def roomy():
        return finish(*exchange(X, Z, J, MOST_DEV, T, 1, *args)[:4])

    recon, decoder_grad, grad = lax.cond(over[0, 0] > 0, roomy, lambda: finish(*fast))
    return recon.T, decoder_grad, grad


def solution(mesh):
    in_specs = (
        P("dp", "latent"),
        P("dp", None),
        P("dp", None),
        P(("dp", "latent"), None),
        P("latent"),
    )
    out_specs = (P("dp", "latent"), P(("dp", "latent"), None), P("dp", None))
    J = 8 if mesh.shape["latent"] >= 16 else 4
    return jax.shard_map(
        functools.partial(per_device, J),
        mesh=mesh, in_specs=in_specs, out_specs=out_specs, check_vma=False,
    )
```

```python
import functools
import math

import jax
import jax.numpy as jnp
from jax import lax
from jax.experimental import pallas as pl
from jax.experimental.pallas import tpu as pltpu
from jax.sharding import PartitionSpec as P

MESH = pl.DeviceIdType.MESH
F32 = jnp.float32
BF16 = jnp.bfloat16
LAT_BLOCK = 64
BLK_DEV = 8
K_BLK = 4
MOST = 8
MOST_DEV = BLK_DEV * MOST
LATS = BLK_DEV * LAT_BLOCK
CODES = K_BLK * LAT_BLOCK


def dot(a, b, ca=1, cb=0):
    return lax.dot_general(a, b, (((ca,), (cb,)), ((), ())), preferred_element_type=F32)


def iota(shape, axis):
    return lax.broadcasted_iota(jnp.int32, shape, axis)


def ones(where):
    return jnp.where(where, 1.0, 0.0)


def onehot(place, rows):
    return ones(iota((rows, place.shape[1]), 0) == place).astype(BF16)


def twice_ids(rows, pack, width):
    ids = iota((rows * pack, width), 0)
    if pack == 2:
        ids = jnp.where(ids >= rows, ids - rows, ids)
    return ids


def onehot_twice(place, rows, pack):
    return ones(twice_ids(rows, pack, place.shape[1]) == place).astype(BF16)


def flat(key):
    return jnp.concatenate([key[k : k + 1] for k in range(K_BLK)], axis=1)


def exchange_kernel(
    X, Z, J, slots, cell,
    ab_hbm, codes_hbm, act_hbm, bias_hbm, dec_hbm,
    recon_ref, rows, own, grad_ref, over_ref,
    ab_my, codes, act, bias, dec, ab_all, c_all, q_all, zt, places, codes_out, codes_in,
    part, a_out, a_in, gpt, b_out, b_in, packed, recon_bf, b2_out, b2_in,
    a2_out, a2_in, yt, w_out, w_in, d_out, d_in, packed_d, pc_all, grads, g_in,
    send_sem, recv_sem, in_sem,
):
    T = ab_my.shape[1]
    NT = X * T
    G = X * Z
    pack = 128 // cell if cell < 128 else 1
    wide = cell * pack
    cw = act.shape[0]
    span = Z * cw
    cs = LAT_BLOCK // 2
    PT = K_BLK * T
    D = dec.shape[1]
    top = b_out.shape[1]
    top_d = d_out.shape[1]
    d = lax.axis_index("dp")
    lat = lax.axis_index("latent")
    z = lax.div(lat, J)
    j = lax.rem(lat, J)
    core = lax.rem(j, 2)
    g = d * Z + z

    def to(me, n, r):
        return lax.rem(me + r, n)

    def frm(me, n, r):
        return lax.rem(me + n - r, n)

    def near(n, r):
        return min(r, n - r)

    loads = [
        pltpu.make_async_copy(src, dst, in_sem.at[n])
        for n, (src, dst) in enumerate(
            ((ab_hbm, ab_my), (codes_hbm, codes), (act_hbm, act), (bias_hbm, bias), (dec_hbm, dec))
        )
    ]
    for load in loads:
        load.start()

    x_steps = sorted(range(1, X), key=lambda r: -near(X, r))
    j_steps = sorted(range(1, J), key=lambda r: -near(J, r))
    xz_steps = sorted(
        [(a, b) for a in range(X) for b in range(Z) if a + b > 0],
        key=lambda s: -near(X, s[0]) - near(Z, s[1]),
    )
    x_peers = [(to(d, X, r), lat) for r in x_steps]
    j_peers = [(d, z * J + to(j, J, r)) for r in j_steps]
    xz_peers = [(to(d, X, a), to(z, Z, b) * J + j) for a, b in xz_steps]
    barrier = pltpu.get_barrier_semaphore()
    for peer in j_peers + xz_peers:
        pl.semaphore_signal(barrier, inc=1, device_id=peer, device_id_type=MESH)

    sent = []

    def put(src, dst, device):
        at = len(sent)
        copy = pltpu.make_async_remote_copy(
            src_ref=src,
            dst_ref=dst,
            send_sem=send_sem.at[at],
            recv_sem=recv_sem.at[at],
            device_id=device,
            device_id_type=MESH,
        )
        copy.start()
        sent.append(copy)
        return copy

    lanes = min(128, T)
    per = PT // lanes
    upto = ones(iota((lanes, lanes), 0) <= iota((lanes, lanes), 1)).astype(BF16)

    def running(mem):
        n = mem.shape[0]
        chunks = mem.shape[1] // lanes
        stacked = jnp.concatenate(
            [mem[:, c * lanes : (c + 1) * lanes] for c in range(chunks)], axis=0
        )
        run = dot(stacked.astype(BF16), upto)
        return [run[c * n : (c + 1) * n] for c in range(chunks)]

    def placed(mem, run, restart):
        pieces = []
        base = jnp.zeros((mem.shape[0], 1), F32)
        for c, here in enumerate(run):
            if c % restart == 0:
                base = jnp.zeros_like(base)
            named = mem[:, c * lanes : (c + 1) * lanes]
            pieces.append(jnp.where(named > 0.5, here - 1.0 + base, -1.0))
            base = base + here[:, lanes - 1 : lanes]
        return jnp.concatenate(pieces, axis=1).astype(jnp.int32), base

    to_owner = int(math.log2(BLK_DEV))
    to_group = int(math.log2(J))
    for load in loads[:2]:
        load.wait()
    ab_here = ab_my[...]
    flat_here = flat(ab_here)
    owner_here = flat_here >> to_owner
    mem = ones(owner_here == (iota((X + (-X) % 8, 1), 0) * Z + z) * J + j)
    along, count = placed(mem, running(mem), per)
    block = jnp.broadcast_to((flat_here & (BLK_DEV - 1)) + 1, (8, PT)).astype(F32).astype(BF16)
    picks = [onehot(along[i : i + 1], slots) for i in range(X)]
    for i in range(X):
        pick = jnp.concatenate(
            [picks[i][:, k * T : (k + 1) * T] for k in range(K_BLK)], axis=0
        )
        got = dot(pick, codes[...])
        total = jnp.zeros((slots, LAT_BLOCK), F32)
        for k in range(K_BLK):
            total = total + got[
                k * slots : (k + 1) * slots, k * LAT_BLOCK : (k + 1) * LAT_BLOCK
            ]
        codes_out[i] = jnp.concatenate(
            [
                total,
                dot(picks[i], block, 1, 1),
                jnp.broadcast_to(count[i : i + 1], (slots, 128 - LAT_BLOCK - 8)),
            ],
            axis=1,
        ).astype(BF16)
    ab_all[d] = ab_here
    codes_in[d] = codes_out[d]
    pl.semaphore_wait(barrier, len(j_peers) + len(xz_peers))

    copies = []
    for r, peer in zip(x_steps, x_peers):
        copies.append(put(codes_out.at[to(d, X, r)], codes_in.at[d], peer))
    ab_copies = [put(ab_my, ab_all.at[d], peer) for peer in x_peers]
    loads[2].wait()
    loads[3].wait()
    column = jnp.broadcast_to(bias[...], (8, cw)).T[:, 0:1]
    offset = column - act[...].astype(F32)
    mem = ones((owner_here >> to_group) == iota((G, 1), 0))
    places[...] = placed(mem, running(mem), per)[0]
    for copy in copies:
        copy.wait_recv()

    mine = jnp.zeros((slots, 128), F32)
    first = jnp.zeros((slots, 1), F32)
    apart = (iota((slots, slots), 0) - iota((slots, slots), 1)).astype(F32)
    for i in range(X):
        here = codes_in[i]
        mine = mine + dot(ones(apart == first).astype(BF16), here)
        first = first + here[:, 127:128].astype(F32)
    by_row = mine[:, LAT_BLOCK : LAT_BLOCK + 1]
    one = mine[:, :LAT_BLOCK]
    twice = jnp.concatenate([one, one], axis=1)
    half = iota((slots, 2 * LAT_BLOCK), 1) >= LAT_BLOCK
    for m in range(BLK_DEV // 2):
        target = jnp.where(half, 2.0 * m + 2.0, 2.0 * m + 1.0)
        own[:, m * 2 * LAT_BLOCK : (m + 1) * 2 * LAT_BLOCK] = jnp.where(
            by_row == target, twice, 0.0
        ).astype(BF16)

    loads[4].wait()
    tile = 512 if D % 512 == 0 else D
    own_codes = own[...]

    for n in range(D // tile):
        at = slice(n * tile, (n + 1) * tile)
        part[:, at] = dot(own_codes, dec[:, at]).astype(BF16)
    for i in range(J):
        a_out[i] = jnp.concatenate(
            [part[:, (n * J + i) * cw : (n * J + i + 1) * cw] for n in range(Z)], axis=1
        )
    copies = []
    for r, peer in zip(j_steps, j_peers):
        copies.append(put(a_out.at[to(j, J, r)], a_in.at[j], peer))
    a_in[j] = a_out[j]
    for copy in ab_copies:
        copy.wait_recv()
    ab = jnp.concatenate([flat(ab_all[i]) for i in range(X)], axis=1)
    owner = ab >> to_owner
    group = owner >> to_group
    mem = jnp.concatenate(
        [
            ones(owner == g * J + iota((J + (-J) % 8, 1), 0)),
            ones(group == g + 0 * iota((8, 1), 0)),
        ],
        axis=0,
    )
    run = running(mem)
    in_owner = placed(mem, run, X * per)[0]
    anew = placed(mem, run, per)[0]
    for i in range(J):
        q_all[i] = onehot(in_owner[i : i + 1], slots)
    for i in range(X):
        at = slice(i * PT, (i + 1) * PT)
        pick = onehot_twice(anew[J + (-J) % 8 : J + (-J) % 8 + 1, at], cell, pack)
        zt[:, i * wide : (i + 1) * wide] = dot(
            q_all[:, :, at].reshape(J * slots, PT), pick, 1, 1
        ).astype(BF16)
    named = jnp.broadcast_to((ab & (BLK_DEV - 1)) + 1, (8, X * PT)).astype(F32).astype(BF16)
    by_col = dot(named, q_all[j], 1, 1)[0:1]
    for copy in copies:
        copy.wait_recv()

    left = lax.rem(iota((8, wide), 1), 128) < 64
    left_row = left[0:1]

    def packs(x, rows):
        if pack == 1:
            return x
        rest = x[rows:]
        if rest.shape[0] < rows:
            rest = jnp.concatenate([rest, rest[: rows - rest.shape[0]]], axis=0)
        return jnp.where(left_row, x[:rows], rest)

    def unpacks(x, rows):
        if pack == 1:
            return x
        x = x.astype(F32)
        first = jnp.where(left_row, x, 0.0)
        rest = jnp.where(left_row, 0.0, x[: rows - x.shape[0]])
        return jnp.concatenate([first, rest], axis=0).astype(BF16)

    arrived = a_in[...].reshape(J * slots, span)
    gpt[...] = dot(arrived, zt[...], 0, 0)
    for i in range(X):
        for n in range(Z):
            b_out[i * Z + n] = packs(
                gpt[n * cw : (n + 1) * cw, i * wide : (i + 1) * wide], top
            ).astype(BF16)
    copies = []
    for (a, b), peer in zip(xz_steps, xz_peers):
        copies.append(put(b_out.at[to(d, X, a) * Z + to(z, Z, b)], b_in.at[g], peer))
    b_in[g] = b_out[g]

    def fill_c(i, carry):
        place = places[pl.ds(i, 1), :]
        ids = twice_ids(cell, pack, T)
        hit = ids == place[:, 0:T]
        for k in range(1, K_BLK):
            hit = hit | (ids == place[:, k * T : (k + 1) * T])
        c_all[i] = ones(hit).astype(BF16)
        return carry

    lax.fori_loop(0, G, fill_c, 0)
    over = jnp.zeros((1, 1), F32)
    part_of = min(64, G * J)
    for i in range(G * J // part_of):
        mem = ones(owner == i * part_of + iota((part_of, 1), 0))
        here = jnp.sum(mem, axis=1, keepdims=True)
        over = over + jnp.max(ones(here > slots), axis=0, keepdims=True)
    for i in range(X):
        mem = ones(group[:, i * PT : (i + 1) * PT] == iota((G, 1), 0))
        here = jnp.sum(mem, axis=1, keepdims=True)
        over = over + jnp.max(ones(here > cell), axis=0, keepdims=True)
    over_ref[0, 0] = jnp.max(over).astype(jnp.int32)
    for copy in copies:
        copy.wait_recv()
    for i in range(G):
        packed[:, i * wide : (i + 1) * wide] = unpacks(b_in[i], cw)
    flat_c = c_all[...].reshape(G * wide, T)
    recon = (dot(packed[...], flat_c) + offset).astype(BF16)
    recon_ref[...] = recon
    recon_bf[...] = recon

    copies = []
    for a in sorted(range(X), key=lambda r: -near(X, r)):
        x = to(d, X, a)
        back_c = c_all[pl.ds(x * Z, Z)].reshape(Z * wide, T)
        sends = dot(recon_bf[...], back_c, 1, 1)
        for n in range(Z):
            b2_out[x * Z + n] = packs(sends[:, n * wide : (n + 1) * wide], top).astype(BF16)
        for (a2, b), peer in zip(xz_steps, xz_peers):
            if a2 == a:
                copies.append(put(b2_out.at[x * Z + to(z, Z, b)], b2_in.at[g], peer))
    b2_in[g] = b2_out[g]
    if pack == 2:

        def fill_pc(i, carry):
            pc_all[i] = onehot(places[pl.ds(i, 1), :], cell)
            return carry

        lax.fori_loop(0, G, fill_pc, 0)
    for copy in copies:
        copy.wait_recv()
    pieces = []
    for n in range(Z):
        pieces.append(
            jnp.concatenate([unpacks(b2_in[i * Z + n], cw) for i in range(X)], axis=1).astype(F32)
        )
    full = jnp.concatenate(pieces, axis=0).astype(BF16)
    a2_out[...] = dot(zt[...], full, 1, 1).astype(BF16).reshape(J, slots, span)
    copies = []
    for r, peer in zip(j_steps, j_peers):
        copies.append(put(a2_out.at[to(j, J, r)], a2_in.at[j], peer))
    a2_in[j] = a2_out[j]
    for copy in copies:
        copy.wait_recv()
    for m in range(Z // 2):
        pieces = [
            a2_in[i, :, n * cw : (n + 1) * cw]
            for n in (2 * m, 2 * m + 1)
            for i in range(J)
        ]
        width = 2 * J * cw
        rows[:, m * width : (m + 1) * width] = jnp.concatenate(pieces, axis=1)

    yt[...] = dot(dec[...], rows[...], 1, 1)
    total = jnp.zeros((LAT_BLOCK, slots), F32)
    for b in range(BLK_DEV):
        total = total + jnp.where(
            by_col == b + 1.0, yt[b * LAT_BLOCK : (b + 1) * LAT_BLOCK, :], 0.0
        )
    for n in range(2):
        w_out[n] = total[n * cs : (n + 1) * cs].astype(BF16)
    copies = []
    for r, peer in zip(j_steps, j_peers):
        copies.append(put(w_out.at[lax.rem(to(j, J, r), 2)], w_in.at[j], peer))
    w_in[j] = w_out[core]
    for copy in copies:
        copy.wait_recv()
    merged = dot(w_in[0], zt[0:slots, :])
    for i in range(1, J):
        merged = merged + dot(w_in[i], zt[i * slots : (i + 1) * slots, :])
    for i in range(X):
        d_out[i] = packs(merged[:, i * wide : (i + 1) * wide], top_d).astype(BF16)
    copies = []
    for (a, b), peer in zip(xz_steps, xz_peers):
        copies.append(put(d_out.at[to(d, X, a)], d_in.at[g], peer))
    d_in[g] = d_out[d]
    for copy in copies:
        copy.wait_recv()
    if pack == 2:
        for i in range(0, G, 2):
            here, after = d_in[i].astype(F32), d_in[i + 1].astype(F32)
            packed_d[:, i * cell : (i + 2) * cell] = jnp.concatenate(
                [
                    jnp.where(left_row, here, pltpu.roll(after, cell, 1)),
                    jnp.where(left_row, pltpu.roll(here, cell, 1), after),
                ],
                axis=0,
            ).astype(BF16)
        grads[...] = dot(packed_d[...], pc_all[...].reshape(G * cell, PT))
    else:
        grads[...] = jnp.zeros_like(grads)

        def gather(i, carry):
            grads[...] += dot(d_in[i], onehot(places[pl.ds(i, 1), :], cell))
            return carry

        lax.fori_loop(0, G, gather, 0)
    for k in range(K_BLK):
        g_in[core, k] = grads[:, k * T : (k + 1) * T].astype(BF16)
    copy = put(g_in.at[core], g_in.at[core], (d, z * J + j + 1 - 2 * core))
    copy.wait_recv()
    for k in range(K_BLK):
        for n in range(2):
            grad_ref[(2 * k + n) * cs : (2 * k + n + 1) * cs, :] = g_in[n, k]
    for copy in sent:
        copy.wait_send()


def exchange(X, Z, J, slots, cell, collective_id, ab, codes, act, bias, decoder):
    cw, T = act.shape
    D = decoder.shape[1]
    NT = X * T
    G = X * Z
    span = Z * cw
    cs = LAT_BLOCK // 2
    PT = K_BLK * T
    pack = 128 // cell if cell < 128 else 1
    wide = cell * pack
    top = cw if pack == 1 else -(-cw // 16) * 8
    top_d = cs if pack == 1 else cs // 2
    n_copies = 2 * (X - 1) + 3 * (G - 1) + 3 * (J - 1) + 1
    vmem = pltpu.VMEM
    whole = pl.BlockSpec(memory_space=pltpu.VMEM)
    far = pl.BlockSpec(memory_space=pl.ANY)
    return pl.pallas_call(
        functools.partial(exchange_kernel, X, Z, J, slots, cell),
        out_shape=(
            jax.ShapeDtypeStruct((cw, T), BF16),
            jax.ShapeDtypeStruct((slots, D), BF16),
            jax.ShapeDtypeStruct((slots, LATS), BF16),
            jax.ShapeDtypeStruct((CODES, T), BF16),
            jax.ShapeDtypeStruct((1, 1), jnp.int32),
        ),
        in_specs=[far] * 5,
        out_specs=[whole] * 4 + [pl.BlockSpec(memory_space=pltpu.SMEM)],
        scratch_shapes=[
            vmem((K_BLK, T), jnp.int32),
            vmem((T, CODES), BF16),
            vmem((cw, T), BF16),
            vmem((1, cw), F32),
            vmem((LATS, D), BF16),
            vmem((X, K_BLK, T), jnp.int32),
            vmem((G, wide, T), BF16),
            vmem((J, slots, X * PT), BF16),
            vmem((J * slots, X * wide), BF16),
            vmem((G, PT), jnp.int32),
            vmem((X, slots, 128), BF16),
            vmem((X, slots, 128), BF16),
            vmem((slots, D), BF16),
            vmem((J, slots, span), BF16),
            vmem((J, slots, span), BF16),
            vmem((span, X * wide), F32),
            vmem((G, top, wide), BF16),
            vmem((G, top, wide), BF16),
            vmem((cw, G * wide), BF16),
            vmem((cw, T), BF16),
            vmem((G, top, wide), BF16),
            vmem((G, top, wide), BF16),
            vmem((J, slots, span), BF16),
            vmem((J, slots, span), BF16),
            vmem((LATS, slots), F32),
            vmem((2, cs, slots), BF16),
            vmem((J, cs, slots), BF16),
            vmem((X, top_d, wide), BF16),
            vmem((G, top_d, wide), BF16),
            vmem((cs, G * cell), BF16),
            vmem((G if pack == 2 else 1, cell, PT), BF16),
            vmem((cs, PT), F32),
            vmem((2, K_BLK, cs, T), BF16),
            pltpu.SemaphoreType.DMA((n_copies,)),
            pltpu.SemaphoreType.DMA((n_copies,)),
            pltpu.SemaphoreType.DMA((5,)),
        ],
        compiler_params=pltpu.CompilerParams(
            collective_id=collective_id,
            has_side_effects=True,
            vmem_limit_bytes=52 * 2**20,
        ),
        name="exchange_%d_%d" % (slots, cell),
    )(ab, codes, act, bias, decoder)


def finish_kernel(
    recon_in, rows, own, grad_in, recon_out, dgrad_out, grad_out, dgrad, grad, sem
):
    copies = [pltpu.make_async_copy(recon_in, recon_out, sem.at[0])]
    copies[0].start()
    parts = sem.shape[0] - 2
    height = LATS // parts
    for n in range(parts):
        at = slice(n * height, (n + 1) * height)
        dgrad[at, :] = dot(own[:, at], rows[...], 0, 0).astype(BF16)
        copies.append(pltpu.make_async_copy(dgrad.at[at], dgrad_out.at[at], sem.at[2 + n]))
        copies[-1].start()
        if n == 0:
            grad[...] = grad_in[...].T
            copies.append(pltpu.make_async_copy(grad, grad_out, sem.at[1]))
            copies[-1].start()
    for copy in copies:
        copy.wait()


def finish(recon, rows, own, grad):
    slots, D = rows.shape
    CO, T = grad.shape
    whole = pl.BlockSpec(memory_space=pltpu.VMEM)
    far = pl.BlockSpec(memory_space=pl.ANY)
    return pl.pallas_call(
        finish_kernel,
        out_shape=(
            jax.ShapeDtypeStruct(recon.shape, BF16),
            jax.ShapeDtypeStruct((LATS, D), BF16),
            jax.ShapeDtypeStruct((T, CO), BF16),
        ),
        in_specs=[whole] * 4,
        out_specs=[far] * 3,
        scratch_shapes=[
            pltpu.VMEM((LATS, D), BF16),
            pltpu.VMEM((T, CO), BF16),
            pltpu.SemaphoreType.DMA((6,)),
        ],
        compiler_params=pltpu.CompilerParams(vmem_limit_bytes=32 * 2**20),
        cost_estimate=pl.CostEstimate(
            flops=2 * slots * LATS * D, bytes_accessed=2 * LATS * D, transcendentals=0
        ),
        name="finish_%d" % slots,
    )(recon, rows, own, grad)


def per_device(J, activations, latent_codes, active_blocks, decoder, decoder_bias):
    X = lax.axis_size("dp")
    Z = lax.axis_size("latent") // J
    T = activations.shape[0]
    args = (active_blocks.T, latent_codes, activations.T, decoder_bias[None, :], decoder)
    *fast, over = exchange(X, Z, J, 40, 64, 0, *args)

    def roomy():
        return finish(*exchange(X, Z, J, MOST_DEV, J * MOST_DEV, 1, *args)[:4])

    recon, decoder_grad, grad = lax.cond(over[0, 0] > 0, roomy, lambda: finish(*fast))
    return recon.T, decoder_grad, grad


def solution(mesh):
    in_specs = (
        P("dp", "latent"),
        P("dp", None),
        P("dp", None),
        P(("dp", "latent"), None),
        P("latent"),
    )
    out_specs = (P("dp", "latent"), P(("dp", "latent"), None), P("dp", None))
    J = 8 if mesh.shape["latent"] >= 16 else 4
    return jax.shard_map(
        functools.partial(per_device, J),
        mesh=mesh, in_specs=in_specs, out_specs=out_specs, check_vma=False,
    )
```

```python
import functools
import math

import jax
import jax.numpy as jnp
from jax import lax
from jax.experimental import pallas as pl
from jax.experimental.pallas import tpu as pltpu
from jax.sharding import PartitionSpec as P

MESH = pl.DeviceIdType.MESH
F32 = jnp.float32
BF16 = jnp.bfloat16
LAT_BLOCK = 64
BLK_DEV = 8
K_BLK = 4
MOST = 8
MOST_DEV = BLK_DEV * MOST
LATS = BLK_DEV * LAT_BLOCK
CODES = K_BLK * LAT_BLOCK


def dot(a, b, ca=1, cb=0):
    return lax.dot_general(a, b, (((ca,), (cb,)), ((), ())), preferred_element_type=F32)


def iota(shape, axis):
    return lax.broadcasted_iota(jnp.int32, shape, axis)


def ones(where):
    return jnp.where(where, 1.0, 0.0)


def onehot(place, rows):
    return ones(iota((rows, place.shape[1]), 0) == place).astype(BF16)


def twice_ids(rows, pack, width):
    ids = iota((rows * pack, width), 0)
    if pack == 2:
        ids = jnp.where(ids >= rows, ids - rows, ids)
    return ids


def onehot_twice(place, rows, pack):
    return ones(twice_ids(rows, pack, place.shape[1]) == place).astype(BF16)


def flat(key):
    return jnp.concatenate([key[k : k + 1] for k in range(K_BLK)], axis=1)


def exchange_kernel(
    X, Z, J, slots, cell,
    ab_hbm, codes_hbm, act_hbm, bias_hbm, dec_hbm,
    recon_ref, rows, own, grad_ref, over_ref,
    ab_my, codes, act, bias, dec, ab_all, c_all, q_all, zt, places, codes_out, codes_in,
    part, a_out, a_in, gpt, b_out, b_in, recon_bf, b2_out, b2_in,
    a2_out, a2_in, dec_by, yt, w_out, w_in, d_out, d_in, pc_all, grads, g_in,
    send_sem, recv_sem, in_sem,
):
    T = ab_my.shape[1]
    NT = X * T
    G = X * Z
    pack = 128 // cell if cell < 128 else 1
    wide = cell * pack
    cw = act.shape[0]
    span = Z * cw
    cs = LAT_BLOCK // 2
    PT = K_BLK * T
    D = dec.shape[1]
    top = b_out.shape[1]
    top_d = d_out.shape[1]
    d = lax.axis_index("dp")
    lat = lax.axis_index("latent")
    z = lax.div(lat, J)
    j = lax.rem(lat, J)
    core = lax.rem(j, 2)
    g = d * Z + z

    def to(me, n, r):
        return lax.rem(me + r, n)

    def frm(me, n, r):
        return lax.rem(me + n - r, n)

    def near(n, r):
        return min(r, n - r)

    loads = [
        pltpu.make_async_copy(src, dst, in_sem.at[n])
        for n, (src, dst) in enumerate(
            ((ab_hbm, ab_my), (codes_hbm, codes), (act_hbm, act), (bias_hbm, bias), (dec_hbm, dec))
        )
    ]
    for load in loads:
        load.start()

    x_steps = sorted(range(1, X), key=lambda r: -near(X, r))
    j_steps = sorted(range(1, J), key=lambda r: -near(J, r))
    xz_steps = sorted(
        [(a, b) for a in range(X) for b in range(Z) if a + b > 0],
        key=lambda s: -near(X, s[0]) - near(Z, s[1]),
    )
    x_peers = [(to(d, X, r), lat) for r in x_steps]
    j_peers = [(d, z * J + to(j, J, r)) for r in j_steps]
    xz_peers = [(to(d, X, a), to(z, Z, b) * J + j) for a, b in xz_steps]
    barrier = pltpu.get_barrier_semaphore()
    for peer in j_peers + xz_peers:
        pl.semaphore_signal(barrier, inc=1, device_id=peer, device_id_type=MESH)

    sent = []

    def put(src, dst, device):
        at = len(sent)
        copy = pltpu.make_async_remote_copy(
            src_ref=src,
            dst_ref=dst,
            send_sem=send_sem.at[at],
            recv_sem=recv_sem.at[at],
            device_id=device,
            device_id_type=MESH,
        )
        copy.start()
        sent.append(copy)
        return copy

    lanes = min(128, T)
    per = PT // lanes
    upto = ones(iota((lanes, lanes), 0) <= iota((lanes, lanes), 1)).astype(BF16)

    every = jnp.ones((lanes, lanes), BF16)

    def before(n, chunks, restart):
        shape = (n * chunks, n * chunks)
        here, there = iota(shape, 0), iota(shape, 1)
        same = (here & (n - 1)) == (there & (n - 1))
        step = int(math.log2(n))
        here, there = here >> step, there >> step
        rest = int(math.log2(restart))
        same = same & (there < here) & ((there >> rest) == (here >> rest))
        return ones(same).astype(BF16)

    def running(mem):
        n = mem.shape[0]
        chunks = mem.shape[1] // lanes
        stacked = jnp.concatenate(
            [mem[:, c * lanes : (c + 1) * lanes] for c in range(chunks)], axis=0
        )
        low = stacked.astype(BF16)
        return n, chunks, stacked, dot(low, upto), dot(low, every).astype(BF16)

    def placed(runs, prior):
        n, chunks, stacked, run, totals = runs
        place = jnp.where(stacked > 0.5, run - 1.0 + dot(prior, totals), -1.0)
        place = place.astype(jnp.int32)
        return jnp.concatenate([place[c * n : (c + 1) * n] for c in range(chunks)], axis=1)

    to_owner = int(math.log2(BLK_DEV))
    to_group = int(math.log2(J))
    for load in loads[:2]:
        load.wait()
    ab_here = ab_my[...]
    flat_here = flat(ab_here)
    owner_here = flat_here >> to_owner
    mem = ones(owner_here == (iota((X + (-X) % 8, 1), 0) * Z + z) * J + j)
    along = placed(running(mem), before(mem.shape[0], per, per))
    count = jnp.sum(mem, axis=1, keepdims=True)
    block = jnp.broadcast_to((flat_here & (BLK_DEV - 1)) + 1, (8, PT)).astype(F32).astype(BF16)
    picks = [onehot(along[i : i + 1], slots) for i in range(X)]
    for i in range(X):
        pick = jnp.concatenate(
            [picks[i][:, k * T : (k + 1) * T] for k in range(K_BLK)], axis=0
        )
        got = dot(pick, codes[...])
        total = jnp.zeros((slots, LAT_BLOCK), F32)
        for k in range(K_BLK):
            total = total + got[
                k * slots : (k + 1) * slots, k * LAT_BLOCK : (k + 1) * LAT_BLOCK
            ]
        codes_out[i] = jnp.concatenate(
            [
                total,
                dot(picks[i], block, 1, 1),
                jnp.broadcast_to(count[i : i + 1], (slots, 128 - LAT_BLOCK - 8)),
            ],
            axis=1,
        ).astype(BF16)
    ab_all[d] = ab_here
    codes_in[d] = codes_out[d]
    pl.semaphore_wait(barrier, len(j_peers) + len(xz_peers))

    copies = []
    for r, peer in zip(x_steps, x_peers):
        copies.append(put(codes_out.at[to(d, X, r)], codes_in.at[d], peer))
    ab_copies = [put(ab_my, ab_all.at[d], peer) for peer in x_peers]
    loads[2].wait()
    loads[3].wait()
    column = jnp.broadcast_to(bias[...], (8, cw)).T[:, 0:1]
    offset = column - act[...].astype(F32)
    mem = ones((owner_here >> to_group) == iota((G, 1), 0))
    places[...] = placed(running(mem), before(G, per, per))
    for copy in copies:
        copy.wait_recv()

    mine = jnp.zeros((slots, 128), F32)
    first = jnp.zeros((slots, 1), F32)
    apart = (iota((slots, slots), 0) - iota((slots, slots), 1)).astype(F32)
    for i in range(X):
        here = codes_in[i]
        mine = mine + dot(ones(apart == first).astype(BF16), here)
        first = first + here[:, 127:128].astype(F32)
    by_row = mine[:, LAT_BLOCK : LAT_BLOCK + 1]
    one = mine[:, :LAT_BLOCK]
    twice = jnp.concatenate([one, one], axis=1)
    half = iota((slots, 2 * LAT_BLOCK), 1) >= LAT_BLOCK
    for m in range(BLK_DEV // 2):
        target = jnp.where(half, 2.0 * m + 2.0, 2.0 * m + 1.0)
        own[:, m * 2 * LAT_BLOCK : (m + 1) * 2 * LAT_BLOCK] = jnp.where(
            by_row == target, twice, 0.0
        ).astype(BF16)

    loads[4].wait()
    tile = 512 if D % 512 == 0 else D
    own_codes = own[...]

    for n in range(D // tile):
        at = slice(n * tile, (n + 1) * tile)
        part[:, at] = dot(own_codes, dec[:, at]).astype(BF16)
    for i in range(J):
        a_out[i] = jnp.concatenate(
            [part[:, (n * J + i) * cw : (n * J + i + 1) * cw] for n in range(Z)], axis=1
        )
    copies = []
    for r, peer in zip(j_steps, j_peers):
        copies.append(put(a_out.at[to(j, J, r)], a_in.at[j], peer))
    a_in[j] = a_out[j]
    for copy in ab_copies:
        copy.wait_recv()
    ab = jnp.concatenate([flat(ab_all[i]) for i in range(X)], axis=1)
    owner = ab >> to_owner
    group = owner >> to_group
    mem = jnp.concatenate(
        [
            ones(owner == g * J + iota((J + (-J) % 8, 1), 0)),
            ones(group == g + 0 * iota((8, 1), 0)),
        ],
        axis=0,
    )
    run = running(mem)
    in_owner = placed(run, before(mem.shape[0], X * per, X * per))
    anew = placed(run, before(mem.shape[0], X * per, per))
    for i in range(J):
        q_all[i] = onehot(in_owner[i : i + 1], slots)
    for i in range(X):
        at = slice(i * PT, (i + 1) * PT)
        pick = onehot_twice(anew[J + (-J) % 8 : J + (-J) % 8 + 1, at], cell, pack)
        zt[:, i * wide : (i + 1) * wide] = dot(
            q_all[:, :, at].reshape(J * slots, PT), pick, 1, 1
        ).astype(BF16)
    named = jnp.broadcast_to((ab & (BLK_DEV - 1)) + 1, (8, X * PT)).astype(F32).astype(BF16)
    by_col = dot(named, q_all[j], 1, 1)[0:1]
    for copy in copies:
        copy.wait_recv()

    left = lax.rem(iota((8, wide), 1), 128) < 64
    left_row = left[0:1]

    def packs(x, rows):
        if pack == 1:
            return x
        rest = x[rows:]
        if rest.shape[0] < rows:
            rest = jnp.concatenate([rest, rest[: rows - rest.shape[0]]], axis=0)
        return jnp.where(left_row, x[:rows], rest)

    def unpacks(x, rows):
        if pack == 1:
            return x
        x = x.astype(F32)
        first = jnp.where(left_row, x, 0.0)
        rest = jnp.where(left_row, 0.0, x[: rows - x.shape[0]])
        return jnp.concatenate([first, rest], axis=0).astype(BF16)

    arrived = a_in[...].reshape(J * slots, span)
    gpt[...] = dot(arrived, zt[...], 0, 0)
    for i in range(X):
        for n in range(Z):
            b_out[i * Z + n] = packs(
                gpt[n * cw : (n + 1) * cw, i * wide : (i + 1) * wide], top
            ).astype(BF16)
    copies = []
    for (a, b), peer in zip(xz_steps, xz_peers):
        copies.append(put(b_out.at[to(d, X, a) * Z + to(z, Z, b)], b_in.at[g], peer))
    b_in[g] = b_out[g]

    def fill_c(i, carry):
        place = places[pl.ds(i, 1), :]
        ids = twice_ids(cell, pack, T)
        hit = ids == place[:, 0:T]
        for k in range(1, K_BLK):
            hit = hit | (ids == place[:, k * T : (k + 1) * T])
        c_all[i] = ones(hit).astype(BF16)
        return carry

    lax.fori_loop(0, G, fill_c, 0)
    over = jnp.zeros((1, 1), F32)
    part_of = min(64, G * J)
    for i in range(G * J // part_of):
        mem = ones(owner == i * part_of + iota((part_of, 1), 0))
        here = jnp.sum(mem, axis=1, keepdims=True)
        over = over + jnp.max(ones(here > slots), axis=0, keepdims=True)
    for i in range(X):
        mem = ones(group[:, i * PT : (i + 1) * PT] == iota((G, 1), 0))
        here = jnp.sum(mem, axis=1, keepdims=True)
        over = over + jnp.max(ones(here > cell), axis=0, keepdims=True)
    over_ref[0, 0] = jnp.max(over).astype(jnp.int32)

    def by_x(copies):
        for a in sorted(range(X), key=lambda r: near(X, r)):
            for (a2, b), copy in zip(xz_steps, copies):
                if a2 == (X - a) % X:
                    copy.wait_recv()
            yield to(d, X, a) * Z

    total = offset
    for first in by_x(copies):
        packed = jnp.concatenate([unpacks(b_in[first + n], cw) for n in range(Z)], axis=1)
        total = total + dot(packed, c_all[pl.ds(first, Z)].reshape(Z * wide, T))
    recon = total.astype(BF16)
    recon_ref[...] = recon
    recon_bf[...] = recon

    copies = []
    for a in sorted(range(X), key=lambda r: -near(X, r)):
        x = to(d, X, a)
        back_c = c_all[pl.ds(x * Z, Z)].reshape(Z * wide, T)
        sends = dot(recon_bf[...], back_c, 1, 1)
        for n in range(Z):
            b2_out[x * Z + n] = packs(sends[:, n * wide : (n + 1) * wide], top).astype(BF16)
        for (a2, b), peer in zip(xz_steps, xz_peers):
            if a2 == a:
                copies.append(put(b2_out.at[x * Z + to(z, Z, b)], b2_in.at[g], peer))
    b2_in[g] = b2_out[g]
    if pack == 2:

        def fill_pc(i, carry):
            pc_all[i] = onehot(places[pl.ds(i, 1), :], cell)
            return carry

        lax.fori_loop(0, G, fill_pc, 0)

    def order(n, carry):
        at = pl.ds(pl.multiple_of(n * LAT_BLOCK, LAT_BLOCK), LAT_BLOCK)
        for i in range(J):
            dec_by[i, at, :] = jnp.concatenate(
                [dec[at, (m * J + i) * cw : (m * J + i + 1) * cw] for m in range(Z)], axis=1
            )
        return carry

    lax.fori_loop(0, LATS // LAT_BLOCK, order, 0)
    for copy in copies:
        copy.wait_recv()
    pieces = []
    for n in range(Z):
        pieces.append(
            jnp.concatenate([unpacks(b2_in[i * Z + n], cw) for i in range(X)], axis=1).astype(F32)
        )
    full = jnp.concatenate(pieces, axis=0).astype(BF16)
    a2_out[...] = dot(zt[...], full, 1, 1).astype(BF16).reshape(J, slots, span)
    copies = []
    for r, peer in zip(j_steps, j_peers):
        copies.append(put(a2_out.at[to(j, J, r)], a2_in.at[j], peer))
    a2_in[j] = a2_out[j]
    yt[...] = dot(dec_by[j], a2_out[j], 1, 1)
    for r, copy in reversed(list(zip(j_steps, copies))):
        copy.wait_recv()
        i = frm(j, J, r)
        yt[...] += dot(dec_by[i], a2_in[i], 1, 1)
    total = jnp.zeros((LAT_BLOCK, slots), F32)
    for b in range(BLK_DEV):
        total = total + jnp.where(
            by_col == b + 1.0, yt[b * LAT_BLOCK : (b + 1) * LAT_BLOCK, :], 0.0
        )
    for n in range(2):
        w_out[n] = total[n * cs : (n + 1) * cs].astype(BF16)
    copies = []
    for r, peer in zip(j_steps, j_peers):
        copies.append(put(w_out.at[lax.rem(to(j, J, r), 2)], w_in.at[j], peer))
    w_in[j] = w_out[core]
    for m in range(Z // 2):
        pieces = [
            a2_in[i, :, n * cw : (n + 1) * cw]
            for n in (2 * m, 2 * m + 1)
            for i in range(J)
        ]
        width = 2 * J * cw
        rows[:, m * width : (m + 1) * width] = jnp.concatenate(pieces, axis=1)
    for copy in copies:
        copy.wait_recv()
    merged = dot(w_in[0], zt[0:slots, :])
    for i in range(1, J):
        merged = merged + dot(w_in[i], zt[i * slots : (i + 1) * slots, :])
    for i in range(X):
        d_out[i] = packs(merged[:, i * wide : (i + 1) * wide], top_d).astype(BF16)
    copies = []
    for (a, b), peer in zip(xz_steps, xz_peers):
        copies.append(put(d_out.at[to(d, X, a)], d_in.at[g], peer))
    d_in[g] = d_out[d]
    if pack == 2:
        for at, first in enumerate(by_x(copies)):
            pieces = []
            for n in range(0, Z, 2):
                here, after = d_in[first + n].astype(F32), d_in[first + n + 1].astype(F32)
                pieces.append(
                    jnp.concatenate(
                        [
                            jnp.where(left_row, here, pltpu.roll(after, cell, 1)),
                            jnp.where(left_row, pltpu.roll(here, cell, 1), after),
                        ],
                        axis=0,
                    ).astype(BF16)
                )
            more = dot(
                jnp.concatenate(pieces, axis=1), pc_all[pl.ds(first, Z)].reshape(Z * cell, PT)
            )
            grads[...] = more if at == 0 else grads[...] + more
    else:
        for copy in copies:
            copy.wait_recv()
        grads[...] = jnp.zeros_like(grads)

        def gather(i, carry):
            grads[...] += dot(d_in[i], onehot(places[pl.ds(i, 1), :], cell))
            return carry

        lax.fori_loop(0, G, gather, 0)
    for k in range(K_BLK):
        g_in[core, k] = grads[:, k * T : (k + 1) * T].astype(BF16)
    copy = put(g_in.at[core], g_in.at[core], (d, z * J + j + 1 - 2 * core))
    copy.wait_recv()
    for k in range(K_BLK):
        for n in range(2):
            grad_ref[(2 * k + n) * cs : (2 * k + n + 1) * cs, :] = g_in[n, k]
    for copy in sent:
        copy.wait_send()


def exchange(X, Z, J, slots, cell, collective_id, ab, codes, act, bias, decoder):
    cw, T = act.shape
    D = decoder.shape[1]
    NT = X * T
    G = X * Z
    span = Z * cw
    cs = LAT_BLOCK // 2
    PT = K_BLK * T
    pack = 128 // cell if cell < 128 else 1
    wide = cell * pack
    top = cw if pack == 1 else -(-cw // 16) * 8
    top_d = cs if pack == 1 else cs // 2
    n_copies = 2 * (X - 1) + 3 * (G - 1) + 3 * (J - 1) + 1
    vmem = pltpu.VMEM
    whole = pl.BlockSpec(memory_space=pltpu.VMEM)
    far = pl.BlockSpec(memory_space=pl.ANY)
    return pl.pallas_call(
        functools.partial(exchange_kernel, X, Z, J, slots, cell),
        out_shape=(
            jax.ShapeDtypeStruct((cw, T), BF16),
            jax.ShapeDtypeStruct((slots, D), BF16),
            jax.ShapeDtypeStruct((slots, LATS), BF16),
            jax.ShapeDtypeStruct((CODES, T), BF16),
            jax.ShapeDtypeStruct((1, 1), jnp.int32),
        ),
        in_specs=[far] * 5,
        out_specs=[whole] * 4 + [pl.BlockSpec(memory_space=pltpu.SMEM)],
        scratch_shapes=[
            vmem((K_BLK, T), jnp.int32),
            vmem((T, CODES), BF16),
            vmem((cw, T), BF16),
            vmem((1, cw), F32),
            vmem((LATS, D), BF16),
            vmem((X, K_BLK, T), jnp.int32),
            vmem((G, wide, T), BF16),
            vmem((J, slots, X * PT), BF16),
            vmem((J * slots, X * wide), BF16),
            vmem((G, PT), jnp.int32),
            vmem((X, slots, 128), BF16),
            vmem((X, slots, 128), BF16),
            vmem((slots, D), BF16),
            vmem((J, slots, span), BF16),
            vmem((J, slots, span), BF16),
            vmem((span, X * wide), F32),
            vmem((G, top, wide), BF16),
            vmem((G, top, wide), BF16),
            vmem((cw, T), BF16),
            vmem((G, top, wide), BF16),
            vmem((G, top, wide), BF16),
            vmem((J, slots, span), BF16),
            vmem((J, slots, span), BF16),
            vmem((J, LATS, span), BF16),
            vmem((LATS, slots), F32),
            vmem((2, cs, slots), BF16),
            vmem((J, cs, slots), BF16),
            vmem((X, top_d, wide), BF16),
            vmem((G, top_d, wide), BF16),
            vmem((G if pack == 2 else 1, cell, PT), BF16),
            vmem((cs, PT), F32),
            vmem((2, K_BLK, cs, T), BF16),
            pltpu.SemaphoreType.DMA((n_copies,)),
            pltpu.SemaphoreType.DMA((n_copies,)),
            pltpu.SemaphoreType.DMA((5,)),
        ],
        compiler_params=pltpu.CompilerParams(
            collective_id=collective_id,
            has_side_effects=True,
            vmem_limit_bytes=52 * 2**20,
        ),
        name="exchange_%d_%d" % (slots, cell),
    )(ab, codes, act, bias, decoder)


def finish_kernel(
    recon_in, rows, own, grad_in, recon_out, dgrad_out, grad_out, dgrad, grad, sem
):
    copies = [pltpu.make_async_copy(recon_in, recon_out, sem.at[0])]
    copies[0].start()
    parts = sem.shape[0] - 2
    height = LATS // parts
    for n in range(parts):
        at = slice(n * height, (n + 1) * height)
        dgrad[at, :] = dot(own[:, at], rows[...], 0, 0).astype(BF16)
        copies.append(pltpu.make_async_copy(dgrad.at[at], dgrad_out.at[at], sem.at[2 + n]))
        copies[-1].start()
        if n == 0:
            grad[...] = grad_in[...].T
            copies.append(pltpu.make_async_copy(grad, grad_out, sem.at[1]))
            copies[-1].start()
    for copy in copies:
        copy.wait()


def finish(recon, rows, own, grad):
    slots, D = rows.shape
    CO, T = grad.shape
    whole = pl.BlockSpec(memory_space=pltpu.VMEM)
    far = pl.BlockSpec(memory_space=pl.ANY)
    return pl.pallas_call(
        finish_kernel,
        out_shape=(
            jax.ShapeDtypeStruct(recon.shape, BF16),
            jax.ShapeDtypeStruct((LATS, D), BF16),
            jax.ShapeDtypeStruct((T, CO), BF16),
        ),
        in_specs=[whole] * 4,
        out_specs=[far] * 3,
        scratch_shapes=[
            pltpu.VMEM((LATS, D), BF16),
            pltpu.VMEM((T, CO), BF16),
            pltpu.SemaphoreType.DMA((10,)),
        ],
        compiler_params=pltpu.CompilerParams(vmem_limit_bytes=32 * 2**20),
        cost_estimate=pl.CostEstimate(
            flops=2 * slots * LATS * D, bytes_accessed=2 * LATS * D, transcendentals=0
        ),
        name="finish_%d" % slots,
    )(recon, rows, own, grad)


def per_device(J, activations, latent_codes, active_blocks, decoder, decoder_bias):
    X = lax.axis_size("dp")
    Z = lax.axis_size("latent") // J
    T = activations.shape[0]
    args = (active_blocks.T, latent_codes, activations.T, decoder_bias[None, :], decoder)
    *fast, over = exchange(X, Z, J, 40, 64, 0, *args)

    def roomy():
        return finish(*exchange(X, Z, J, MOST_DEV, J * MOST_DEV, 1, *args)[:4])

    recon, decoder_grad, grad = lax.cond(over[0, 0] > 0, roomy, lambda: finish(*fast))
    return recon.T, decoder_grad, grad


def solution(mesh):
    in_specs = (
        P("dp", "latent"),
        P("dp", None),
        P("dp", None),
        P(("dp", "latent"), None),
        P("latent"),
    )
    out_specs = (P("dp", "latent"), P(("dp", "latent"), None), P("dp", None))
    J = 8 if mesh.shape["latent"] >= 16 else 4
    return jax.shard_map(
        functools.partial(per_device, J),
        mesh=mesh, in_specs=in_specs, out_specs=out_specs, check_vma=False,
    )
```

```python
import functools
import math

import jax
import jax.numpy as jnp
from jax import lax
from jax.experimental import pallas as pl
from jax.experimental.pallas import tpu as pltpu
from jax.sharding import PartitionSpec as P

MESH = pl.DeviceIdType.MESH
F32 = jnp.float32
BF16 = jnp.bfloat16
LAT_BLOCK = 64
BLK_DEV = 8
K_BLK = 4
MOST = 8
MOST_DEV = BLK_DEV * MOST
LATS = BLK_DEV * LAT_BLOCK
CODES = K_BLK * LAT_BLOCK


def dot(a, b, ca=1, cb=0):
    return lax.dot_general(a, b, (((ca,), (cb,)), ((), ())), preferred_element_type=F32)


def iota(shape, axis):
    return lax.broadcasted_iota(jnp.int32, shape, axis)


def ones(where):
    return jnp.where(where, 1.0, 0.0)


def onehot(place, rows):
    return ones(iota((rows, place.shape[1]), 0) == place).astype(BF16)


def twice_ids(rows, pack, width):
    ids = iota((rows * pack, width), 0)
    if pack == 2:
        ids = jnp.where(ids >= rows, ids - rows, ids)
    return ids


def onehot_twice(place, rows, pack):
    return ones(twice_ids(rows, pack, place.shape[1]) == place).astype(BF16)


def flat(key):
    return jnp.concatenate([key[k : k + 1] for k in range(K_BLK)], axis=1)


def exchange_kernel(
    X, Z, J, slots, cell,
    ab_hbm, codes_hbm, act_hbm, bias_hbm, dec_hbm,
    recon_ref, rows, own, grad_ref, over_ref,
    ab_my, codes, act, bias, dec, ab_all, c_all, q_all, zt, places, codes_out, codes_in,
    part, a_out, a_in, gpt, b_out, b_in, recon_bf, b2_out, b2_in,
    a2_out, a2_in, dec_by, yt, w_out, w_in, d_out, d_in, pc_all, grads, g_in,
    send_sem, recv_sem, in_sem,
):
    T = ab_my.shape[1]
    NT = X * T
    G = X * Z
    pack = 128 // cell if cell < 128 else 1
    wide = cell * pack
    cw = act.shape[0]
    span = Z * cw
    cs = LAT_BLOCK // 2
    PT = K_BLK * T
    D = dec.shape[1]
    top = b_out.shape[1]
    top_d = d_out.shape[1]
    d = lax.axis_index("dp")
    lat = lax.axis_index("latent")
    z = lax.div(lat, J)
    j = lax.rem(lat, J)
    core = lax.rem(j, 2)
    g = d * Z + z

    def to(me, n, r):
        return lax.rem(me + r, n)

    def frm(me, n, r):
        return lax.rem(me + n - r, n)

    def near(n, r):
        return min(r, n - r)

    loads = [
        pltpu.make_async_copy(src, dst, in_sem.at[n])
        for n, (src, dst) in enumerate(
            ((ab_hbm, ab_my), (codes_hbm, codes), (act_hbm, act), (bias_hbm, bias), (dec_hbm, dec))
        )
    ]
    for load in loads:
        load.start()

    x_steps = sorted(range(1, X), key=lambda r: -near(X, r))
    j_steps = sorted(range(1, J), key=lambda r: -near(J, r))
    xz_steps = sorted(
        [(a, b) for a in range(X) for b in range(Z) if a + b > 0],
        key=lambda s: -near(X, s[0]) - near(Z, s[1]),
    )
    x_peers = [(to(d, X, r), lat) for r in x_steps]
    j_peers = [(d, z * J + to(j, J, r)) for r in j_steps]
    xz_peers = [(to(d, X, a), to(z, Z, b) * J + j) for a, b in xz_steps]
    barrier = pltpu.get_barrier_semaphore()
    for peer in j_peers + xz_peers:
        pl.semaphore_signal(barrier, inc=1, device_id=peer, device_id_type=MESH)

    taken = [0]
    sent = []

    def copy_of(src, dst, device, at):
        return pltpu.make_async_remote_copy(
            src_ref=src,
            dst_ref=dst,
            send_sem=send_sem.at[at],
            recv_sem=recv_sem.at[at],
            device_id=device,
            device_id_type=MESH,
        )

    def send(messages, like):
        at = taken[0]
        taken[0] += 1
        for src, dst, device in messages:
            copy_of(src, dst, device, at).start()
        all_of = like.at[0 : len(messages)]
        whole = copy_of(all_of, all_of, messages[0][2], at)
        sent.append(whole)
        return whole

    def drain():
        while sent:
            sent.pop().wait_send()

    def send_xz(message, like):
        copies = {}
        for a in sorted(range(X), key=lambda r: -near(X, r)):
            copies[a] = send(
                [message(a, b) + (peer,) for (a2, b), peer in zip(xz_steps, xz_peers) if a2 == a],
                like,
            )
        return copies

    def by_x(copies):
        for a in sorted(range(X), key=lambda r: near(X, r)):
            copies[(X - a) % X].wait_recv()
            yield to(d, X, a) * Z

    lanes = min(128, T)
    per = PT // lanes
    upto = ones(iota((lanes, lanes), 0) <= iota((lanes, lanes), 1)).astype(BF16)

    every = jnp.ones((lanes, lanes), BF16)

    def before(n, chunks, restart):
        shape = (n * chunks, n * chunks)
        here, there = iota(shape, 0), iota(shape, 1)
        same = (here & (n - 1)) == (there & (n - 1))
        step = int(math.log2(n))
        here, there = here >> step, there >> step
        rest = int(math.log2(restart))
        same = same & (there < here) & ((there >> rest) == (here >> rest))
        return ones(same).astype(BF16)

    def running(mem):
        n = mem.shape[0]
        chunks = mem.shape[1] // lanes
        stacked = jnp.concatenate(
            [mem[:, c * lanes : (c + 1) * lanes] for c in range(chunks)], axis=0
        )
        low = stacked.astype(BF16)
        return n, chunks, stacked, dot(low, upto), dot(low, every).astype(BF16)

    def placed(runs, prior):
        n, chunks, stacked, run, totals = runs
        place = jnp.where(stacked > 0.5, run - 1.0 + dot(prior, totals), -1.0)
        place = place.astype(jnp.int32)
        return jnp.concatenate([place[c * n : (c + 1) * n] for c in range(chunks)], axis=1)

    to_owner = int(math.log2(BLK_DEV))
    to_group = int(math.log2(J))
    for load in loads[:2]:
        load.wait()
    ab_here = ab_my[...]
    flat_here = flat(ab_here)
    owner_here = flat_here >> to_owner
    mem = ones(owner_here == (iota((X + (-X) % 8, 1), 0) * Z + z) * J + j)
    along = placed(running(mem), before(mem.shape[0], per, per))
    count = jnp.sum(mem, axis=1, keepdims=True)
    block = jnp.broadcast_to((flat_here & (BLK_DEV - 1)) + 1, (8, PT)).astype(F32).astype(BF16)
    picks = [onehot(along[i : i + 1], slots) for i in range(X)]
    for i in range(X):
        pick = jnp.concatenate(
            [picks[i][:, k * T : (k + 1) * T] for k in range(K_BLK)], axis=0
        )
        got = dot(pick, codes[...])
        total = jnp.zeros((slots, LAT_BLOCK), F32)
        for k in range(K_BLK):
            total = total + got[
                k * slots : (k + 1) * slots, k * LAT_BLOCK : (k + 1) * LAT_BLOCK
            ]
        codes_out[i] = jnp.concatenate(
            [
                total,
                dot(picks[i], block, 1, 1),
                jnp.broadcast_to(count[i : i + 1], (slots, 128 - LAT_BLOCK - 8)),
            ],
            axis=1,
        ).astype(BF16)
    ab_all[d] = ab_here
    codes_in[d] = codes_out[d]
    pl.semaphore_wait(barrier, len(j_peers) + len(xz_peers))

    copies = send(
        [
            (codes_out.at[to(d, X, r)], codes_in.at[d], peer)
            for r, peer in zip(x_steps, x_peers)
        ],
        codes_in,
    )
    ab_copies = send([(ab_my, ab_all.at[d], peer) for peer in x_peers], ab_all)
    loads[2].wait()
    loads[3].wait()
    column = jnp.broadcast_to(bias[...], (8, cw)).T[:, 0:1]
    offset = column - act[...].astype(F32)
    mem = ones((owner_here >> to_group) == iota((G, 1), 0))
    places[...] = placed(running(mem), before(G, per, per))
    copies.wait_recv()

    mine = jnp.zeros((slots, 128), F32)
    first = jnp.zeros((slots, 1), F32)
    apart = (iota((slots, slots), 0) - iota((slots, slots), 1)).astype(F32)
    for i in range(X):
        here = codes_in[i]
        mine = mine + dot(ones(apart == first).astype(BF16), here)
        first = first + here[:, 127:128].astype(F32)
    by_row = mine[:, LAT_BLOCK : LAT_BLOCK + 1]
    one = mine[:, :LAT_BLOCK]
    twice = jnp.concatenate([one, one], axis=1)
    half = iota((slots, 2 * LAT_BLOCK), 1) >= LAT_BLOCK
    for m in range(BLK_DEV // 2):
        target = jnp.where(half, 2.0 * m + 2.0, 2.0 * m + 1.0)
        own[:, m * 2 * LAT_BLOCK : (m + 1) * 2 * LAT_BLOCK] = jnp.where(
            by_row == target, twice, 0.0
        ).astype(BF16)

    loads[4].wait()
    tile = 512 if D % 512 == 0 else D
    own_codes = own[...]

    for n in range(D // tile):
        at = slice(n * tile, (n + 1) * tile)
        part[:, at] = dot(own_codes, dec[:, at]).astype(BF16)
    for i in range(J):
        a_out[i] = jnp.concatenate(
            [part[:, (n * J + i) * cw : (n * J + i + 1) * cw] for n in range(Z)], axis=1
        )
    copies = send(
        [(a_out.at[to(j, J, r)], a_in.at[j], peer) for r, peer in zip(j_steps, j_peers)], a_in
    )
    a_in[j] = a_out[j]
    ab_copies.wait_recv()
    ab = jnp.concatenate([flat(ab_all[i]) for i in range(X)], axis=1)
    owner = ab >> to_owner
    group = owner >> to_group
    mem = jnp.concatenate(
        [
            ones(owner == g * J + iota((J + (-J) % 8, 1), 0)),
            ones(group == g + 0 * iota((8, 1), 0)),
        ],
        axis=0,
    )
    run = running(mem)
    in_owner = placed(run, before(mem.shape[0], X * per, X * per))
    anew = placed(run, before(mem.shape[0], X * per, per))
    for i in range(J):
        q_all[i] = onehot(in_owner[i : i + 1], slots)
    for i in range(X):
        at = slice(i * PT, (i + 1) * PT)
        pick = onehot_twice(anew[J + (-J) % 8 : J + (-J) % 8 + 1, at], cell, pack)
        zt[:, i * wide : (i + 1) * wide] = dot(
            q_all[:, :, at].reshape(J * slots, PT), pick, 1, 1
        ).astype(BF16)
    named = jnp.broadcast_to((ab & (BLK_DEV - 1)) + 1, (8, X * PT)).astype(F32).astype(BF16)
    by_col = dot(named, q_all[j], 1, 1)[0:1]
    copies.wait_recv()

    left = lax.rem(iota((8, wide), 1), 128) < 64
    left_row = left[0:1]

    def packs(x, rows):
        if pack == 1:
            return x
        rest = x[rows:]
        if rest.shape[0] < rows:
            rest = jnp.concatenate([rest, rest[: rows - rest.shape[0]]], axis=0)
        return jnp.where(left_row, x[:rows], rest)

    def unpacks(x, rows):
        if pack == 1:
            return x
        x = x.astype(F32)
        first = jnp.where(left_row, x, 0.0)
        rest = jnp.where(left_row, 0.0, x[: rows - x.shape[0]])
        return jnp.concatenate([first, rest], axis=0).astype(BF16)

    arrived = a_in[...].reshape(J * slots, span)
    gpt[...] = dot(arrived, zt[...], 0, 0)
    for i in range(X):
        for n in range(Z):
            b_out[i * Z + n] = packs(
                gpt[n * cw : (n + 1) * cw, i * wide : (i + 1) * wide], top
            ).astype(BF16)
    copies = send_xz(
        lambda a, b: (b_out.at[to(d, X, a) * Z + to(z, Z, b)], b_in.at[g]), b_in
    )
    b_in[g] = b_out[g]

    def fill_c(i, carry):
        place = places[pl.ds(i, 1), :]
        ids = twice_ids(cell, pack, T)
        hit = ids == place[:, 0:T]
        for k in range(1, K_BLK):
            hit = hit | (ids == place[:, k * T : (k + 1) * T])
        c_all[i] = ones(hit).astype(BF16)
        return carry

    lax.fori_loop(0, G, fill_c, 0)

    def order(n, carry):
        at = pl.ds(pl.multiple_of(n * LAT_BLOCK, LAT_BLOCK), LAT_BLOCK)
        for i in range(J):
            dec_by[i, at, :] = jnp.concatenate(
                [dec[at, (m * J + i) * cw : (m * J + i + 1) * cw] for m in range(Z)], axis=1
            )
        return carry

    lax.fori_loop(0, LATS // LAT_BLOCK, order, 0)
    over = jnp.zeros((1, 1), F32)
    part_of = min(64, G * J)
    for i in range(G * J // part_of):
        mem = ones(owner == i * part_of + iota((part_of, 1), 0))
        here = jnp.sum(mem, axis=1, keepdims=True)
        over = over + jnp.max(ones(here > slots), axis=0, keepdims=True)
    for i in range(X):
        mem = ones(group[:, i * PT : (i + 1) * PT] == iota((G, 1), 0))
        here = jnp.sum(mem, axis=1, keepdims=True)
        over = over + jnp.max(ones(here > cell), axis=0, keepdims=True)
    over_ref[0, 0] = jnp.max(over).astype(jnp.int32)

    drain()
    total = offset
    for first in by_x(copies):
        packed = jnp.concatenate([unpacks(b_in[first + n], cw) for n in range(Z)], axis=1)
        total = total + dot(packed, c_all[pl.ds(first, Z)].reshape(Z * wide, T))
    recon = total.astype(BF16)
    recon_ref[...] = recon
    recon_bf[...] = recon

    copies = []
    for a in sorted(range(X), key=lambda r: -near(X, r)):
        x = to(d, X, a)
        back_c = c_all[pl.ds(x * Z, Z)].reshape(Z * wide, T)
        sends = dot(recon_bf[...], back_c, 1, 1)
        for n in range(Z):
            b2_out[x * Z + n] = packs(sends[:, n * wide : (n + 1) * wide], top).astype(BF16)
        copies.append(
            send(
                [
                    (b2_out.at[x * Z + to(z, Z, b)], b2_in.at[g], peer)
                    for (a2, b), peer in zip(xz_steps, xz_peers)
                    if a2 == a
                ],
                b2_in,
            )
        )
    b2_in[g] = b2_out[g]
    if pack == 2:

        def fill_pc(i, carry):
            pc_all[i] = onehot(places[pl.ds(i, 1), :], cell)
            return carry

        lax.fori_loop(0, G, fill_pc, 0)
    for copy in copies:
        copy.wait_recv()
    pieces = []
    for n in range(Z):
        pieces.append(
            jnp.concatenate([unpacks(b2_in[i * Z + n], cw) for i in range(X)], axis=1).astype(F32)
        )
    full = jnp.concatenate(pieces, axis=0).astype(BF16)
    a2_out[...] = dot(zt[...], full, 1, 1).astype(BF16).reshape(J, slots, span)
    copies = [
        send([(a2_out.at[to(j, J, r)], a2_in.at[j], peer)], a2_in)
        for r, peer in zip(j_steps, j_peers)
    ]
    a2_in[j] = a2_out[j]
    yt[...] = dot(dec_by[j], a2_out[j], 1, 1)
    for r, copy in reversed(list(zip(j_steps, copies))):
        copy.wait_recv()
        i = frm(j, J, r)
        yt[...] += dot(dec_by[i], a2_in[i], 1, 1)
    total = jnp.zeros((LAT_BLOCK, slots), F32)
    for b in range(BLK_DEV):
        total = total + jnp.where(
            by_col == b + 1.0, yt[b * LAT_BLOCK : (b + 1) * LAT_BLOCK, :], 0.0
        )
    for n in range(2):
        w_out[n] = total[n * cs : (n + 1) * cs].astype(BF16)
    copies = send(
        [
            (w_out.at[lax.rem(to(j, J, r), 2)], w_in.at[j], peer)
            for r, peer in zip(j_steps, j_peers)
        ],
        w_in,
    )
    w_in[j] = w_out[core]
    for m in range(Z // 2):
        pieces = [
            a2_in[i, :, n * cw : (n + 1) * cw]
            for n in (2 * m, 2 * m + 1)
            for i in range(J)
        ]
        width = 2 * J * cw
        rows[:, m * width : (m + 1) * width] = jnp.concatenate(pieces, axis=1)
    copies.wait_recv()
    merged = dot(w_in[0], zt[0:slots, :])
    for i in range(1, J):
        merged = merged + dot(w_in[i], zt[i * slots : (i + 1) * slots, :])
    for i in range(X):
        d_out[i] = packs(merged[:, i * wide : (i + 1) * wide], top_d).astype(BF16)
    copies = send_xz(lambda a, b: (d_out.at[to(d, X, a)], d_in.at[g]), d_in)
    drain()
    d_in[g] = d_out[d]
    if pack == 2:
        for at, first in enumerate(by_x(copies)):
            pieces = []
            for n in range(0, Z, 2):
                here, after = d_in[first + n].astype(F32), d_in[first + n + 1].astype(F32)
                pieces.append(
                    jnp.concatenate(
                        [
                            jnp.where(left_row, here, pltpu.roll(after, cell, 1)),
                            jnp.where(left_row, pltpu.roll(here, cell, 1), after),
                        ],
                        axis=0,
                    ).astype(BF16)
                )
            more = dot(
                jnp.concatenate(pieces, axis=1), pc_all[pl.ds(first, Z)].reshape(Z * cell, PT)
            )
            grads[...] = more if at == 0 else grads[...] + more
    else:
        for copy in copies.values():
            copy.wait_recv()
        grads[...] = jnp.zeros_like(grads)

        def gather(i, carry):
            grads[...] += dot(d_in[i], onehot(places[pl.ds(i, 1), :], cell))
            return carry

        lax.fori_loop(0, G, gather, 0)
    for k in range(K_BLK):
        g_in[core, k] = grads[:, k * T : (k + 1) * T].astype(BF16)
    copy = send([(g_in.at[core], g_in.at[core], (d, z * J + j + 1 - 2 * core))], g_in)
    copy.wait_recv()
    for k in range(K_BLK):
        for n in range(2):
            grad_ref[(2 * k + n) * cs : (2 * k + n + 1) * cs, :] = g_in[n, k]
    drain()


def exchange(X, Z, J, slots, cell, collective_id, ab, codes, act, bias, decoder):
    cw, T = act.shape
    D = decoder.shape[1]
    NT = X * T
    G = X * Z
    span = Z * cw
    cs = LAT_BLOCK // 2
    PT = K_BLK * T
    pack = 128 // cell if cell < 128 else 1
    wide = cell * pack
    top = cw if pack == 1 else -(-cw // 16) * 8
    top_d = cs if pack == 1 else cs // 2
    n_copies = 3 * X + (J - 1) + 5
    vmem = pltpu.VMEM
    whole = pl.BlockSpec(memory_space=pltpu.VMEM)
    far = pl.BlockSpec(memory_space=pl.ANY)
    return pl.pallas_call(
        functools.partial(exchange_kernel, X, Z, J, slots, cell),
        out_shape=(
            jax.ShapeDtypeStruct((cw, T), BF16),
            jax.ShapeDtypeStruct((slots, D), BF16),
            jax.ShapeDtypeStruct((slots, LATS), BF16),
            jax.ShapeDtypeStruct((CODES, T), BF16),
            jax.ShapeDtypeStruct((1, 1), jnp.int32),
        ),
        in_specs=[far] * 5,
        out_specs=[whole] * 4 + [pl.BlockSpec(memory_space=pltpu.SMEM)],
        scratch_shapes=[
            vmem((K_BLK, T), jnp.int32),
            vmem((T, CODES), BF16),
            vmem((cw, T), BF16),
            vmem((1, cw), F32),
            vmem((LATS, D), BF16),
            vmem((X, K_BLK, T), jnp.int32),
            vmem((G, wide, T), BF16),
            vmem((J, slots, X * PT), BF16),
            vmem((J * slots, X * wide), BF16),
            vmem((G, PT), jnp.int32),
            vmem((X, slots, 128), BF16),
            vmem((X, slots, 128), BF16),
            vmem((slots, D), BF16),
            vmem((J, slots, span), BF16),
            vmem((J, slots, span), BF16),
            vmem((span, X * wide), F32),
            vmem((G, top, wide), BF16),
            vmem((G, top, wide), BF16),
            vmem((cw, T), BF16),
            vmem((G, top, wide), BF16),
            vmem((G, top, wide), BF16),
            vmem((J, slots, span), BF16),
            vmem((J, slots, span), BF16),
            vmem((J, LATS, span), BF16),
            vmem((LATS, slots), F32),
            vmem((2, cs, slots), BF16),
            vmem((J, cs, slots), BF16),
            vmem((X, top_d, wide), BF16),
            vmem((G, top_d, wide), BF16),
            vmem((G if pack == 2 else 1, cell, PT), BF16),
            vmem((cs, PT), F32),
            vmem((2, K_BLK, cs, T), BF16),
            pltpu.SemaphoreType.DMA((n_copies,)),
            pltpu.SemaphoreType.DMA((n_copies,)),
            pltpu.SemaphoreType.DMA((5,)),
        ],
        compiler_params=pltpu.CompilerParams(
            collective_id=collective_id,
            has_side_effects=True,
            vmem_limit_bytes=52 * 2**20,
        ),
        name="exchange_%d_%d" % (slots, cell),
    )(ab, codes, act, bias, decoder)


def finish_kernel(
    recon_in, rows, own, grad_in, recon_out, dgrad_out, grad_out, dgrad, grad, sem
):
    copies = [pltpu.make_async_copy(recon_in, recon_out, sem.at[0])]
    copies[0].start()
    parts = sem.shape[0] - 2
    height = LATS // parts
    for n in range(parts):
        at = slice(n * height, (n + 1) * height)
        dgrad[at, :] = dot(own[:, at], rows[...], 0, 0).astype(BF16)
        copies.append(pltpu.make_async_copy(dgrad.at[at], dgrad_out.at[at], sem.at[2 + n]))
        copies[-1].start()
        if n == 0:
            grad[...] = grad_in[...].T
            copies.append(pltpu.make_async_copy(grad, grad_out, sem.at[1]))
            copies[-1].start()
    for copy in copies:
        copy.wait()


def finish(recon, rows, own, grad):
    slots, D = rows.shape
    CO, T = grad.shape
    whole = pl.BlockSpec(memory_space=pltpu.VMEM)
    far = pl.BlockSpec(memory_space=pl.ANY)
    return pl.pallas_call(
        finish_kernel,
        out_shape=(
            jax.ShapeDtypeStruct(recon.shape, BF16),
            jax.ShapeDtypeStruct((LATS, D), BF16),
            jax.ShapeDtypeStruct((T, CO), BF16),
        ),
        in_specs=[whole] * 4,
        out_specs=[far] * 3,
        scratch_shapes=[
            pltpu.VMEM((LATS, D), BF16),
            pltpu.VMEM((T, CO), BF16),
            pltpu.SemaphoreType.DMA((10,)),
        ],
        compiler_params=pltpu.CompilerParams(vmem_limit_bytes=32 * 2**20),
        cost_estimate=pl.CostEstimate(
            flops=2 * slots * LATS * D, bytes_accessed=2 * LATS * D, transcendentals=0
        ),
        name="finish_%d" % slots,
    )(recon, rows, own, grad)


def per_device(J, activations, latent_codes, active_blocks, decoder, decoder_bias):
    X = lax.axis_size("dp")
    Z = lax.axis_size("latent") // J
    T = activations.shape[0]
    args = (active_blocks.T, latent_codes, activations.T, decoder_bias[None, :], decoder)
    *fast, over = exchange(X, Z, J, 40, 64, 0, *args)

    def roomy():
        return finish(*exchange(X, Z, J, MOST_DEV, J * MOST_DEV, 1, *args)[:4])

    recon, decoder_grad, grad = lax.cond(over[0, 0] > 0, roomy, lambda: finish(*fast))
    return recon.T, decoder_grad, grad


def solution(mesh):
    in_specs = (
        P("dp", "latent"),
        P("dp", None),
        P("dp", None),
        P(("dp", "latent"), None),
        P("latent"),
    )
    out_specs = (P("dp", "latent"), P(("dp", "latent"), None), P("dp", None))
    J = 8 if mesh.shape["latent"] >= 16 else 4
    return jax.shard_map(
        functools.partial(per_device, J),
        mesh=mesh, in_specs=in_specs, out_specs=out_specs, check_vma=False,
    )
```

```python
import functools
import math

import jax
import jax.numpy as jnp
from jax import lax
from jax.experimental import pallas as pl
from jax.experimental.pallas import tpu as pltpu
from jax.sharding import PartitionSpec as P

MESH = pl.DeviceIdType.MESH
F32 = jnp.float32
BF16 = jnp.bfloat16
LAT_BLOCK = 64
BLK_DEV = 8
K_BLK = 4
MOST = 8
MOST_DEV = BLK_DEV * MOST
LATS = BLK_DEV * LAT_BLOCK
CODES = K_BLK * LAT_BLOCK


def dot(a, b, ca=1, cb=0):
    return lax.dot_general(a, b, (((ca,), (cb,)), ((), ())), preferred_element_type=F32)


def iota(shape, axis):
    return lax.broadcasted_iota(jnp.int32, shape, axis)


def ones(where):
    return jnp.where(where, 1.0, 0.0)


def onehot(place, rows):
    return ones(iota((rows, place.shape[1]), 0) == place).astype(BF16)


def twice_ids(rows, pack, width):
    ids = iota((rows * pack, width), 0)
    if pack == 2:
        ids = jnp.where(ids >= rows, ids - rows, ids)
    return ids


def onehot_twice(place, rows, pack):
    return ones(twice_ids(rows, pack, place.shape[1]) == place).astype(BF16)


def flat(key):
    return jnp.concatenate([key[k : k + 1] for k in range(K_BLK)], axis=1)


def exchange_kernel(
    X, Z, J, slots, cell,
    ab_hbm, codes_hbm, act_hbm, bias_hbm, dec_hbm,
    recon_ref, rows, own, grad_ref, over_ref,
    ab_my, codes, act, bias, dec, ab_all, c_all, q_all, zt, places, codes_out, codes_in,
    part, a_out, a_in, gpt, b_out, b_in, recon_bf, ba_out, ba_in, bb_out, bb_in,
    aa_out, aa_in, ab_out, ab_in, dec_a, dec_b, yt, w_out, w_in, d_out, d_in, pc_all, grads, g_in,
    send_sem, recv_sem, in_sem,
):
    T = ab_my.shape[1]
    NT = X * T
    G = X * Z
    pack = 128 // cell if cell < 128 else 1
    wide = cell * pack
    cw = act.shape[0]
    span = Z * cw
    cs = LAT_BLOCK // 2
    fa = -(-cw // 16) * 8
    fb = cw - fa
    PT = K_BLK * T
    D = dec.shape[1]
    top = b_out.shape[1]
    top_d = d_out.shape[1]
    d = lax.axis_index("dp")
    lat = lax.axis_index("latent")
    z = lax.div(lat, J)
    j = lax.rem(lat, J)
    core = lax.rem(j, 2)
    g = d * Z + z

    def to(me, n, r):
        return lax.rem(me + r, n)

    def frm(me, n, r):
        return lax.rem(me + n - r, n)

    def near(n, r):
        return min(r, n - r)

    loads = [
        pltpu.make_async_copy(src, dst, in_sem.at[n])
        for n, (src, dst) in enumerate(
            ((ab_hbm, ab_my), (codes_hbm, codes), (act_hbm, act), (bias_hbm, bias), (dec_hbm, dec))
        )
    ]
    for load in loads:
        load.start()

    x_steps = sorted(range(1, X), key=lambda r: -near(X, r))
    j_steps = sorted(range(1, J), key=lambda r: -near(J, r))
    xz_steps = sorted(
        [(a, b) for a in range(X) for b in range(Z) if a + b > 0],
        key=lambda s: -near(X, s[0]) - near(Z, s[1]),
    )
    x_peers = [(to(d, X, r), lat) for r in x_steps]
    j_peers = [(d, z * J + to(j, J, r)) for r in j_steps]
    xz_peers = [(to(d, X, a), to(z, Z, b) * J + j) for a, b in xz_steps]
    barrier = pltpu.get_barrier_semaphore()
    for peer in j_peers + xz_peers:
        pl.semaphore_signal(barrier, inc=1, device_id=peer, device_id_type=MESH)

    taken = [0]
    sent = []

    def copy_of(src, dst, device, at):
        return pltpu.make_async_remote_copy(
            src_ref=src,
            dst_ref=dst,
            send_sem=send_sem.at[at],
            recv_sem=recv_sem.at[at],
            device_id=device,
            device_id_type=MESH,
        )

    def send(messages, like):
        at = taken[0]
        taken[0] += 1
        for src, dst, device in messages:
            copy_of(src, dst, device, at).start()
        all_of = like.at[0 : len(messages)]
        whole = copy_of(all_of, all_of, messages[0][2], at)
        sent.append(whole)
        return whole

    def drain():
        while sent:
            sent.pop().wait_send()

    def send_xz(message, like):
        copies = {}
        for a in sorted(range(X), key=lambda r: -near(X, r)):
            copies[a] = send(
                [message(a, b) + (peer,) for (a2, b), peer in zip(xz_steps, xz_peers) if a2 == a],
                like,
            )
        return copies

    def by_x(copies):
        for a in sorted(range(X), key=lambda r: near(X, r)):
            copies[(X - a) % X].wait_recv()
            yield to(d, X, a) * Z

    lanes = min(128, T)
    per = PT // lanes
    upto = ones(iota((lanes, lanes), 0) <= iota((lanes, lanes), 1)).astype(BF16)

    every = jnp.ones((lanes, lanes), BF16)

    def before(n, chunks, restart):
        shape = (n * chunks, n * chunks)
        here, there = iota(shape, 0), iota(shape, 1)
        same = (here & (n - 1)) == (there & (n - 1))
        step = int(math.log2(n))
        here, there = here >> step, there >> step
        rest = int(math.log2(restart))
        same = same & (there < here) & ((there >> rest) == (here >> rest))
        return ones(same).astype(BF16)

    def running(mem):
        n = mem.shape[0]
        chunks = mem.shape[1] // lanes
        stacked = jnp.concatenate(
            [mem[:, c * lanes : (c + 1) * lanes] for c in range(chunks)], axis=0
        )
        low = stacked.astype(BF16)
        return n, chunks, stacked, dot(low, upto), dot(low, every).astype(BF16)

    def placed(runs, prior):
        n, chunks, stacked, run, totals = runs
        place = jnp.where(stacked > 0.5, run - 1.0 + dot(prior, totals), -1.0)
        place = place.astype(jnp.int32)
        return jnp.concatenate([place[c * n : (c + 1) * n] for c in range(chunks)], axis=1)

    to_owner = int(math.log2(BLK_DEV))
    to_group = int(math.log2(J))
    for load in loads[:2]:
        load.wait()
    ab_here = ab_my[...]
    flat_here = flat(ab_here)
    owner_here = flat_here >> to_owner
    mem = ones(owner_here == (iota((X + (-X) % 8, 1), 0) * Z + z) * J + j)
    along = placed(running(mem), before(mem.shape[0], per, per))
    count = jnp.sum(mem, axis=1, keepdims=True)
    block = jnp.broadcast_to((flat_here & (BLK_DEV - 1)) + 1, (8, PT)).astype(F32).astype(BF16)
    picks = [onehot(along[i : i + 1], slots) for i in range(X)]
    for i in range(X):
        pick = jnp.concatenate(
            [picks[i][:, k * T : (k + 1) * T] for k in range(K_BLK)], axis=0
        )
        got = dot(pick, codes[...])
        total = jnp.zeros((slots, LAT_BLOCK), F32)
        for k in range(K_BLK):
            total = total + got[
                k * slots : (k + 1) * slots, k * LAT_BLOCK : (k + 1) * LAT_BLOCK
            ]
        codes_out[i] = jnp.concatenate(
            [
                total,
                dot(picks[i], block, 1, 1),
                jnp.broadcast_to(count[i : i + 1], (slots, 128 - LAT_BLOCK - 8)),
            ],
            axis=1,
        ).astype(BF16)
    ab_all[d] = ab_here
    codes_in[d] = codes_out[d]
    pl.semaphore_wait(barrier, len(j_peers) + len(xz_peers))

    copies = send(
        [
            (codes_out.at[to(d, X, r)], codes_in.at[d], peer)
            for r, peer in zip(x_steps, x_peers)
        ],
        codes_in,
    )
    ab_copies = send([(ab_my, ab_all.at[d], peer) for peer in x_peers], ab_all)
    loads[2].wait()
    loads[3].wait()
    column = jnp.broadcast_to(bias[...], (8, cw)).T[:, 0:1]
    offset = column - act[...].astype(F32)
    mem = ones((owner_here >> to_group) == iota((G, 1), 0))
    places[...] = placed(running(mem), before(G, per, per))
    copies.wait_recv()

    mine = jnp.zeros((slots, 128), F32)
    first = jnp.zeros((slots, 1), F32)
    apart = (iota((slots, slots), 0) - iota((slots, slots), 1)).astype(F32)
    for i in range(X):
        here = codes_in[i]
        mine = mine + dot(ones(apart == first).astype(BF16), here)
        first = first + here[:, 127:128].astype(F32)
    by_row = mine[:, LAT_BLOCK : LAT_BLOCK + 1]
    one = mine[:, :LAT_BLOCK]
    twice = jnp.concatenate([one, one], axis=1)
    half = iota((slots, 2 * LAT_BLOCK), 1) >= LAT_BLOCK
    for m in range(BLK_DEV // 2):
        target = jnp.where(half, 2.0 * m + 2.0, 2.0 * m + 1.0)
        own[:, m * 2 * LAT_BLOCK : (m + 1) * 2 * LAT_BLOCK] = jnp.where(
            by_row == target, twice, 0.0
        ).astype(BF16)

    loads[4].wait()
    tile = 512 if D % 512 == 0 else D
    own_codes = own[...]

    for n in range(D // tile):
        at = slice(n * tile, (n + 1) * tile)
        part[:, at] = dot(own_codes, dec[:, at]).astype(BF16)
    for i in range(J):
        a_out[i] = jnp.concatenate(
            [part[:, (n * J + i) * cw : (n * J + i + 1) * cw] for n in range(Z)], axis=1
        )
    copies = send(
        [(a_out.at[to(j, J, r)], a_in.at[j], peer) for r, peer in zip(j_steps, j_peers)], a_in
    )
    a_in[j] = a_out[j]
    ab_copies.wait_recv()
    ab = jnp.concatenate([flat(ab_all[i]) for i in range(X)], axis=1)
    owner = ab >> to_owner
    group = owner >> to_group
    mem = jnp.concatenate(
        [
            ones(owner == g * J + iota((J + (-J) % 8, 1), 0)),
            ones(group == g + 0 * iota((8, 1), 0)),
        ],
        axis=0,
    )
    run = running(mem)
    in_owner = placed(run, before(mem.shape[0], X * per, X * per))
    anew = placed(run, before(mem.shape[0], X * per, per))
    for i in range(J):
        q_all[i] = onehot(in_owner[i : i + 1], slots)
    for i in range(X):
        at = slice(i * PT, (i + 1) * PT)
        pick = onehot_twice(anew[J + (-J) % 8 : J + (-J) % 8 + 1, at], cell, pack)
        zt[:, i * wide : (i + 1) * wide] = dot(
            q_all[:, :, at].reshape(J * slots, PT), pick, 1, 1
        ).astype(BF16)
    named = jnp.broadcast_to((ab & (BLK_DEV - 1)) + 1, (8, X * PT)).astype(F32).astype(BF16)
    by_col = dot(named, q_all[j], 1, 1)[0:1]
    copies.wait_recv()

    left = lax.rem(iota((8, wide), 1), 128) < 64
    left_row = left[0:1]

    def packs(x, rows):
        if pack == 1:
            return x
        rest = x[rows:]
        if rest.shape[0] < rows:
            rest = jnp.concatenate([rest, rest[: rows - rest.shape[0]]], axis=0)
        return jnp.where(left_row, x[:rows], rest)

    def unpacks(x, rows):
        if pack == 1:
            return x
        x = x.astype(F32)
        first = jnp.where(left_row, x, 0.0)
        rest = jnp.where(left_row, 0.0, x[: rows - x.shape[0]])
        return jnp.concatenate([first, rest], axis=0).astype(BF16)

    arrived = a_in[...].reshape(J * slots, span)
    gpt[...] = dot(arrived, zt[...], 0, 0)
    for i in range(X):
        for n in range(Z):
            b_out[i * Z + n] = packs(
                gpt[n * cw : (n + 1) * cw, i * wide : (i + 1) * wide], top
            ).astype(BF16)
    copies = send_xz(
        lambda a, b: (b_out.at[to(d, X, a) * Z + to(z, Z, b)], b_in.at[g]), b_in
    )
    b_in[g] = b_out[g]

    def fill_c(i, carry):
        place = places[pl.ds(i, 1), :]
        ids = twice_ids(cell, pack, T)
        hit = ids == place[:, 0:T]
        for k in range(1, K_BLK):
            hit = hit | (ids == place[:, k * T : (k + 1) * T])
        c_all[i] = ones(hit).astype(BF16)
        return carry

    lax.fori_loop(0, G, fill_c, 0)

    def order(n, carry):
        at = pl.ds(pl.multiple_of(n * LAT_BLOCK, LAT_BLOCK), LAT_BLOCK)
        for i in range(J):
            starts = [(m * J + i) * cw for m in range(Z)]
            dec_a[i, at, :] = jnp.concatenate([dec[at, f : f + fa] for f in starts], axis=1)
            dec_b[i, at, :] = jnp.concatenate([dec[at, f + fa : f + cw] for f in starts], axis=1)
        return carry

    lax.fori_loop(0, LATS // LAT_BLOCK, order, 0)
    over = jnp.zeros((1, 1), F32)
    part_of = min(64, G * J)
    for i in range(G * J // part_of):
        mem = ones(owner == i * part_of + iota((part_of, 1), 0))
        here = jnp.sum(mem, axis=1, keepdims=True)
        over = over + jnp.max(ones(here > slots), axis=0, keepdims=True)
    for i in range(X):
        mem = ones(group[:, i * PT : (i + 1) * PT] == iota((G, 1), 0))
        here = jnp.sum(mem, axis=1, keepdims=True)
        over = over + jnp.max(ones(here > cell), axis=0, keepdims=True)
    over_ref[0, 0] = jnp.max(over).astype(jnp.int32)

    drain()
    total = offset
    for first in by_x(copies):
        packed = jnp.concatenate([unpacks(b_in[first + n], cw) for n in range(Z)], axis=1)
        total = total + dot(packed, c_all[pl.ds(first, Z)].reshape(Z * wide, T))
    recon = total.astype(BF16)
    recon_ref[...] = recon
    recon_bf[...] = recon

    first_copies, later = [], []
    for a in sorted(range(X), key=lambda r: -near(X, r)):
        x = to(d, X, a)
        back_c = c_all[pl.ds(x * Z, Z)].reshape(Z * wide, T)
        sends = dot(recon_bf[...], back_c, 1, 1)
        for n in range(Z):
            piece = sends[:, n * wide : (n + 1) * wide]
            ba_out[x * Z + n] = packs(piece[:fa], ba_out.shape[1]).astype(BF16)
            bb_out[x * Z + n] = packs(piece[fa:], bb_out.shape[1]).astype(BF16)
        ways = [
            (x * Z + to(z, Z, b), peer)
            for (a2, b), peer in zip(xz_steps, xz_peers)
            if a2 == a
        ]
        first_copies.append(send([(ba_out.at[i], ba_in.at[g], peer) for i, peer in ways], ba_in))
        later.append([(bb_out.at[i], bb_in.at[g], peer) for i, peer in ways])
    later_copies = [send(messages, bb_in) for messages in later]
    ba_in[g] = ba_out[g]
    bb_in[g] = bb_out[g]
    if pack == 2:

        def fill_pc(i, carry):
            pc_all[i] = onehot(places[pl.ds(i, 1), :], cell)
            return carry

        lax.fori_loop(0, G, fill_pc, 0)

    def returned(copies, src, rows):
        for copy in copies:
            copy.wait_recv()
        pieces = [
            jnp.concatenate([unpacks(src[i * Z + n], rows) for i in range(X)], axis=1).astype(F32)
            for n in range(Z)
        ]
        return jnp.concatenate(pieces, axis=0).astype(BF16)

    def to_owners(full, out, dst):
        out[...] = dot(zt[...], full, 1, 1).astype(BF16).reshape(out.shape)
        copies = [
            send([(out.at[to(j, J, r)], dst.at[j], peer)], dst)
            for r, peer in zip(j_steps, j_peers)
        ]
        dst[j] = out[j]
        return copies

    a_copies = to_owners(returned(first_copies, ba_in, fa), aa_out, aa_in)
    b_copies = to_owners(returned(later_copies, bb_in, fb), ab_out, ab_in)
    yt[...] = dot(dec_a[j], aa_out[j], 1, 1) + dot(dec_b[j], ab_out[j], 1, 1)
    for r, copy in reversed(list(zip(j_steps, a_copies))):
        copy.wait_recv()
        i = frm(j, J, r)
        yt[...] += dot(dec_a[i], aa_in[i], 1, 1)
    for r, copy in reversed(list(zip(j_steps, b_copies))):
        copy.wait_recv()
        i = frm(j, J, r)
        yt[...] += dot(dec_b[i], ab_in[i], 1, 1)
    total = jnp.zeros((LAT_BLOCK, slots), F32)
    for b in range(BLK_DEV):
        total = total + jnp.where(
            by_col == b + 1.0, yt[b * LAT_BLOCK : (b + 1) * LAT_BLOCK, :], 0.0
        )
    for n in range(2):
        w_out[n] = total[n * cs : (n + 1) * cs].astype(BF16)
    copies = send(
        [
            (w_out.at[lax.rem(to(j, J, r), 2)], w_in.at[j], peer)
            for r, peer in zip(j_steps, j_peers)
        ],
        w_in,
    )
    w_in[j] = w_out[core]
    for m in range(Z // 2):
        pieces = [
            half_in[i, :, n * rows_of : (n + 1) * rows_of]
            for n in (2 * m, 2 * m + 1)
            for i in range(J)
            for half_in, rows_of in ((aa_in, fa), (ab_in, fb))
        ]
        width = 2 * J * cw
        rows[:, m * width : (m + 1) * width] = jnp.concatenate(pieces, axis=1)
    copies.wait_recv()
    merged = dot(w_in[0], zt[0:slots, :])
    for i in range(1, J):
        merged = merged + dot(w_in[i], zt[i * slots : (i + 1) * slots, :])
    for i in range(X):
        d_out[i] = packs(merged[:, i * wide : (i + 1) * wide], top_d).astype(BF16)
    copies = send_xz(lambda a, b: (d_out.at[to(d, X, a)], d_in.at[g]), d_in)
    drain()
    d_in[g] = d_out[d]
    if pack == 2:
        for at, first in enumerate(by_x(copies)):
            pieces = []
            for n in range(0, Z, 2):
                here, after = d_in[first + n].astype(F32), d_in[first + n + 1].astype(F32)
                pieces.append(
                    jnp.concatenate(
                        [
                            jnp.where(left_row, here, pltpu.roll(after, cell, 1)),
                            jnp.where(left_row, pltpu.roll(here, cell, 1), after),
                        ],
                        axis=0,
                    ).astype(BF16)
                )
            more = dot(
                jnp.concatenate(pieces, axis=1), pc_all[pl.ds(first, Z)].reshape(Z * cell, PT)
            )
            grads[...] = more if at == 0 else grads[...] + more
    else:
        for copy in copies.values():
            copy.wait_recv()
        grads[...] = jnp.zeros_like(grads)

        def gather(i, carry):
            grads[...] += dot(d_in[i], onehot(places[pl.ds(i, 1), :], cell))
            return carry

        lax.fori_loop(0, G, gather, 0)
    for k in range(K_BLK):
        g_in[core, k] = grads[:, k * T : (k + 1) * T].astype(BF16)
    copy = send([(g_in.at[core], g_in.at[core], (d, z * J + j + 1 - 2 * core))], g_in)
    copy.wait_recv()
    for k in range(K_BLK):
        for n in range(2):
            grad_ref[(2 * k + n) * cs : (2 * k + n + 1) * cs, :] = g_in[n, k]
    drain()


def exchange(X, Z, J, slots, cell, collective_id, ab, codes, act, bias, decoder):
    cw, T = act.shape
    D = decoder.shape[1]
    NT = X * T
    G = X * Z
    span = Z * cw
    cs = LAT_BLOCK // 2
    fa = -(-cw // 16) * 8
    fb = cw - fa
    PT = K_BLK * T
    pack = 128 // cell if cell < 128 else 1
    wide = cell * pack
    top = cw if pack == 1 else -(-cw // 16) * 8
    top_d = cs if pack == 1 else cs // 2
    n_copies = 4 * X + 2 * (J - 1) + 5
    vmem = pltpu.VMEM
    whole = pl.BlockSpec(memory_space=pltpu.VMEM)
    far = pl.BlockSpec(memory_space=pl.ANY)
    return pl.pallas_call(
        functools.partial(exchange_kernel, X, Z, J, slots, cell),
        out_shape=(
            jax.ShapeDtypeStruct((cw, T), BF16),
            jax.ShapeDtypeStruct((slots, D), BF16),
            jax.ShapeDtypeStruct((slots, LATS), BF16),
            jax.ShapeDtypeStruct((CODES, T), BF16),
            jax.ShapeDtypeStruct((1, 1), jnp.int32),
        ),
        in_specs=[far] * 5,
        out_specs=[whole] * 4 + [pl.BlockSpec(memory_space=pltpu.SMEM)],
        scratch_shapes=[
            vmem((K_BLK, T), jnp.int32),
            vmem((T, CODES), BF16),
            vmem((cw, T), BF16),
            vmem((1, cw), F32),
            vmem((LATS, D), BF16),
            vmem((X, K_BLK, T), jnp.int32),
            vmem((G, wide, T), BF16),
            vmem((J, slots, X * PT), BF16),
            vmem((J * slots, X * wide), BF16),
            vmem((G, PT), jnp.int32),
            vmem((X, slots, 128), BF16),
            vmem((X, slots, 128), BF16),
            vmem((slots, D), BF16),
            vmem((J, slots, span), BF16),
            vmem((J, slots, span), BF16),
            vmem((span, X * wide), F32),
            vmem((G, top, wide), BF16),
            vmem((G, top, wide), BF16),
            vmem((cw, T), BF16),
            vmem((G, fa // pack + (-(fa // pack)) % 8, wide), BF16),
            vmem((G, fa // pack + (-(fa // pack)) % 8, wide), BF16),
            vmem((G, fb // pack, wide), BF16),
            vmem((G, fb // pack, wide), BF16),
            vmem((J, slots, Z * fa), BF16),
            vmem((J, slots, Z * fa), BF16),
            vmem((J, slots, Z * fb), BF16),
            vmem((J, slots, Z * fb), BF16),
            vmem((J, LATS, Z * fa), BF16),
            vmem((J, LATS, Z * fb), BF16),
            vmem((LATS, slots), F32),
            vmem((2, cs, slots), BF16),
            vmem((J, cs, slots), BF16),
            vmem((X, top_d, wide), BF16),
            vmem((G, top_d, wide), BF16),
            vmem((G if pack == 2 else 1, cell, PT), BF16),
            vmem((cs, PT), F32),
            vmem((2, K_BLK, cs, T), BF16),
            pltpu.SemaphoreType.DMA((n_copies,)),
            pltpu.SemaphoreType.DMA((n_copies,)),
            pltpu.SemaphoreType.DMA((5,)),
        ],
        compiler_params=pltpu.CompilerParams(
            collective_id=collective_id,
            has_side_effects=True,
            vmem_limit_bytes=52 * 2**20,
        ),
        name="exchange_%d_%d" % (slots, cell),
    )(ab, codes, act, bias, decoder)


def finish_kernel(
    recon_in, rows, own, grad_in, recon_out, dgrad_out, grad_out, dgrad, grad, sem
):
    copies = [pltpu.make_async_copy(recon_in, recon_out, sem.at[0])]
    copies[0].start()
    parts = sem.shape[0] - 2
    height = LATS // parts
    for n in range(parts):
        at = slice(n * height, (n + 1) * height)
        dgrad[at, :] = dot(own[:, at], rows[...], 0, 0).astype(BF16)
        copies.append(pltpu.make_async_copy(dgrad.at[at], dgrad_out.at[at], sem.at[2 + n]))
        copies[-1].start()
        if n == 0:
            grad[...] = grad_in[...].T
            copies.append(pltpu.make_async_copy(grad, grad_out, sem.at[1]))
            copies[-1].start()
    for copy in copies:
        copy.wait()


def finish(recon, rows, own, grad):
    slots, D = rows.shape
    CO, T = grad.shape
    whole = pl.BlockSpec(memory_space=pltpu.VMEM)
    far = pl.BlockSpec(memory_space=pl.ANY)
    return pl.pallas_call(
        finish_kernel,
        out_shape=(
            jax.ShapeDtypeStruct(recon.shape, BF16),
            jax.ShapeDtypeStruct((LATS, D), BF16),
            jax.ShapeDtypeStruct((T, CO), BF16),
        ),
        in_specs=[whole] * 4,
        out_specs=[far] * 3,
        scratch_shapes=[
            pltpu.VMEM((LATS, D), BF16),
            pltpu.VMEM((T, CO), BF16),
            pltpu.SemaphoreType.DMA((10,)),
        ],
        compiler_params=pltpu.CompilerParams(vmem_limit_bytes=32 * 2**20),
        cost_estimate=pl.CostEstimate(
            flops=2 * slots * LATS * D, bytes_accessed=2 * LATS * D, transcendentals=0
        ),
        name="finish_%d" % slots,
    )(recon, rows, own, grad)


def per_device(J, activations, latent_codes, active_blocks, decoder, decoder_bias):
    X = lax.axis_size("dp")
    Z = lax.axis_size("latent") // J
    T = activations.shape[0]
    args = (active_blocks.T, latent_codes, activations.T, decoder_bias[None, :], decoder)
    *fast, over = exchange(X, Z, J, 40, 64, 0, *args)

    def roomy():
        return finish(*exchange(X, Z, J, MOST_DEV, J * MOST_DEV, 1, *args)[:4])

    recon, decoder_grad, grad = lax.cond(over[0, 0] > 0, roomy, lambda: finish(*fast))
    return recon.T, decoder_grad, grad


def solution(mesh):
    in_specs = (
        P("dp", "latent"),
        P("dp", None),
        P("dp", None),
        P(("dp", "latent"), None),
        P("latent"),
    )
    out_specs = (P("dp", "latent"), P(("dp", "latent"), None), P("dp", None))
    J = 8 if mesh.shape["latent"] >= 16 else 4
    return jax.shard_map(
        functools.partial(per_device, J),
        mesh=mesh, in_specs=in_specs, out_specs=out_specs, check_vma=False,
    )
```

```python
import functools
import math

import jax
import jax.numpy as jnp
from jax import lax
from jax.experimental import pallas as pl
from jax.experimental.pallas import tpu as pltpu
from jax.sharding import PartitionSpec as P

MESH = pl.DeviceIdType.MESH
F32 = jnp.float32
BF16 = jnp.bfloat16
LAT_BLOCK = 64
BLK_DEV = 8
K_BLK = 4
MOST = 8
MOST_DEV = BLK_DEV * MOST
LATS = BLK_DEV * LAT_BLOCK
CODES = K_BLK * LAT_BLOCK


def dot(a, b, ca=1, cb=0):
    return lax.dot_general(a, b, (((ca,), (cb,)), ((), ())), preferred_element_type=F32)


def iota(shape, axis):
    return lax.broadcasted_iota(jnp.int32, shape, axis)


def ones(where):
    return jnp.where(where, 1.0, 0.0)


def onehot(place, rows):
    return ones(iota((rows, place.shape[1]), 0) == place).astype(BF16)


def twice_ids(rows, pack, width):
    ids = iota((rows * pack, width), 0)
    if pack == 2:
        ids = jnp.where(ids >= rows, ids - rows, ids)
    return ids


def onehot_twice(place, rows, pack):
    return ones(twice_ids(rows, pack, place.shape[1]) == place).astype(BF16)


def flat(key):
    return jnp.concatenate([key[k : k + 1] for k in range(K_BLK)], axis=1)


def exchange_kernel(
    X, Z, J, slots, cell,
    ab_hbm, codes_hbm, act_hbm, bias_hbm, dec_hbm,
    recon_ref, rows, own, grad_ref, over_ref,
    ab_my, codes, act, bias, dec, ab_all, c_all, q_all, zt, places, codes_out, codes_in,
    part, a_out, a_in, gpt, b_out, b_in, recon_bf, ba_out, ba_in, bb_out, bb_in,
    aa_out, aa_in, ab_out, ab_in, dec_a, dec_b, yt, w_out, w_in, d_out, d_in, pc_all, grads, g_in,
    send_sem, recv_sem, in_sem,
):
    T = ab_my.shape[1]
    NT = X * T
    G = X * Z
    pack = 128 // cell if cell < 128 else 1
    wide = cell * pack
    cw = act.shape[0]
    span = Z * cw
    cs = LAT_BLOCK // 2
    fa = -(-cw // 16) * 8
    fb = cw - fa
    PT = K_BLK * T
    D = dec.shape[1]
    top = b_out.shape[1]
    top_d = d_out.shape[1]
    d = lax.axis_index("dp")
    lat = lax.axis_index("latent")
    z = lax.div(lat, J)
    j = lax.rem(lat, J)
    core = lax.rem(j, 2)
    g = d * Z + z

    def to(me, n, r):
        return lax.rem(me + r, n)

    def frm(me, n, r):
        return lax.rem(me + n - r, n)

    def near(n, r):
        return min(r, n - r)

    loads = [
        pltpu.make_async_copy(src, dst, in_sem.at[n])
        for n, (src, dst) in enumerate(
            ((ab_hbm, ab_my), (codes_hbm, codes), (act_hbm, act), (bias_hbm, bias), (dec_hbm, dec))
        )
    ]
    for load in loads:
        load.start()

    x_steps = sorted(range(1, X), key=lambda r: -near(X, r))
    j_steps = sorted(range(1, J), key=lambda r: -near(J, r))
    xz_steps = sorted(
        [(a, b) for a in range(X) for b in range(Z) if a + b > 0],
        key=lambda s: -near(X, s[0]) - near(Z, s[1]),
    )
    x_peers = [(to(d, X, r), lat) for r in x_steps]
    j_peers = [(d, z * J + to(j, J, r)) for r in j_steps]
    xz_peers = [(to(d, X, a), to(z, Z, b) * J + j) for a, b in xz_steps]
    barrier = pltpu.get_barrier_semaphore()
    for peer in j_peers + xz_peers:
        pl.semaphore_signal(barrier, inc=1, device_id=peer, device_id_type=MESH)

    taken = [0]
    sent = []

    def copy_of(src, dst, device, at):
        return pltpu.make_async_remote_copy(
            src_ref=src,
            dst_ref=dst,
            send_sem=send_sem.at[at],
            recv_sem=recv_sem.at[at],
            device_id=device,
            device_id_type=MESH,
        )

    def send(messages, like):
        at = taken[0]
        taken[0] += 1
        for src, dst, device in messages:
            copy_of(src, dst, device, at).start()
        all_of = like.at[0 : len(messages)]
        whole = copy_of(all_of, all_of, messages[0][2], at)
        sent.append(whole)
        return whole

    def drain():
        while sent:
            sent.pop().wait_send()

    def send_xz(message, like):
        copies = {}
        for a in sorted(range(X), key=lambda r: -near(X, r)):
            copies[a] = send(
                [message(a, b) + (peer,) for (a2, b), peer in zip(xz_steps, xz_peers) if a2 == a],
                like,
            )
        return copies

    def by_x(copies):
        for a in sorted(range(X), key=lambda r: near(X, r)):
            copies[(X - a) % X].wait_recv()
            yield to(d, X, a) * Z

    lanes = min(128, T)
    per = PT // lanes
    upto = ones(iota((lanes, lanes), 0) <= iota((lanes, lanes), 1)).astype(BF16)

    every = jnp.ones((lanes, lanes), BF16)

    def before(n, chunks, restart):
        shape = (n * chunks, n * chunks)
        here, there = iota(shape, 0), iota(shape, 1)
        same = (here & (n - 1)) == (there & (n - 1))
        step = int(math.log2(n))
        here, there = here >> step, there >> step
        rest = int(math.log2(restart))
        same = same & (there < here) & ((there >> rest) == (here >> rest))
        return ones(same).astype(BF16)

    def running(mem):
        n = mem.shape[0]
        chunks = mem.shape[1] // lanes
        stacked = jnp.concatenate(
            [mem[:, c * lanes : (c + 1) * lanes] for c in range(chunks)], axis=0
        )
        low = stacked.astype(BF16)
        return n, chunks, stacked, dot(low, upto), dot(low, every).astype(BF16)

    def placed(runs, prior):
        n, chunks, stacked, run, totals = runs
        place = jnp.where(stacked > 0.5, run - 1.0 + dot(prior, totals), -1.0)
        place = place.astype(jnp.int32)
        return jnp.concatenate([place[c * n : (c + 1) * n] for c in range(chunks)], axis=1)

    to_owner = int(math.log2(BLK_DEV))
    to_group = int(math.log2(J))
    for load in loads[:2]:
        load.wait()
    ab_here = ab_my[...]
    flat_here = flat(ab_here)
    owner_here = flat_here >> to_owner
    mem = ones(owner_here == (iota((X + (-X) % 8, 1), 0) * Z + z) * J + j)
    along = placed(running(mem), before(mem.shape[0], per, per))
    count = jnp.sum(mem, axis=1, keepdims=True)
    block = jnp.broadcast_to((flat_here & (BLK_DEV - 1)) + 1, (8, PT)).astype(F32).astype(BF16)
    picks = [onehot(along[i : i + 1], slots) for i in range(X)]
    for i in range(X):
        pick = jnp.concatenate(
            [picks[i][:, k * T : (k + 1) * T] for k in range(K_BLK)], axis=0
        )
        got = dot(pick, codes[...])
        total = jnp.zeros((slots, LAT_BLOCK), F32)
        for k in range(K_BLK):
            total = total + got[
                k * slots : (k + 1) * slots, k * LAT_BLOCK : (k + 1) * LAT_BLOCK
            ]
        codes_out[i] = jnp.concatenate(
            [
                total,
                dot(picks[i], block, 1, 1),
                jnp.broadcast_to(count[i : i + 1], (slots, 128 - LAT_BLOCK - 8)),
            ],
            axis=1,
        ).astype(BF16)
    ab_all[d] = ab_here
    codes_in[d] = codes_out[d]
    pl.semaphore_wait(barrier, len(j_peers) + len(xz_peers))

    copies = send(
        [
            (codes_out.at[to(d, X, r)], codes_in.at[d], peer)
            for r, peer in zip(x_steps, x_peers)
        ],
        codes_in,
    )
    ab_copies = send([(ab_my, ab_all.at[d], peer) for peer in x_peers], ab_all)
    loads[2].wait()
    loads[3].wait()
    column = jnp.broadcast_to(bias[...], (8, cw)).T[:, 0:1]
    offset = column - act[...].astype(F32)
    mem = ones((owner_here >> to_group) == iota((G, 1), 0))
    places[...] = placed(running(mem), before(G, per, per))
    copies.wait_recv()

    mine = jnp.zeros((slots, 128), F32)
    first = jnp.zeros((slots, 1), F32)
    apart = (iota((slots, slots), 0) - iota((slots, slots), 1)).astype(F32)
    for i in range(X):
        here = codes_in[i]
        mine = mine + dot(ones(apart == first).astype(BF16), here)
        first = first + here[:, 127:128].astype(F32)
    by_row = mine[:, LAT_BLOCK : LAT_BLOCK + 1]
    one = mine[:, :LAT_BLOCK]
    twice = jnp.concatenate([one, one], axis=1)
    half = iota((slots, 2 * LAT_BLOCK), 1) >= LAT_BLOCK
    for m in range(BLK_DEV // 2):
        target = jnp.where(half, 2.0 * m + 2.0, 2.0 * m + 1.0)
        own[:, m * 2 * LAT_BLOCK : (m + 1) * 2 * LAT_BLOCK] = jnp.where(
            by_row == target, twice, 0.0
        ).astype(BF16)

    loads[4].wait()
    tile = 512 if D % 512 == 0 else D
    own_codes = own[...]

    for n in range(D // tile):
        at = slice(n * tile, (n + 1) * tile)
        part[:, at] = dot(own_codes, dec[:, at]).astype(BF16)
    for i in range(J):
        a_out[i] = jnp.concatenate(
            [part[:, (n * J + i) * cw : (n * J + i + 1) * cw] for n in range(Z)], axis=1
        )
    copies = send(
        [(a_out.at[to(j, J, r)], a_in.at[j], peer) for r, peer in zip(j_steps, j_peers)], a_in
    )
    a_in[j] = a_out[j]
    ab_copies.wait_recv()
    ab = jnp.concatenate([flat(ab_all[i]) for i in range(X)], axis=1)
    owner = ab >> to_owner
    group = owner >> to_group
    mem = jnp.concatenate(
        [
            ones(owner == g * J + iota((J + (-J) % 8, 1), 0)),
            ones(group == g + 0 * iota((8, 1), 0)),
        ],
        axis=0,
    )
    run = running(mem)
    in_owner = placed(run, before(mem.shape[0], X * per, X * per))
    anew = placed(run, before(mem.shape[0], X * per, per))
    for i in range(J):
        q_all[i] = onehot(in_owner[i : i + 1], slots)
    for i in range(X):
        at = slice(i * PT, (i + 1) * PT)
        pick = onehot_twice(anew[J + (-J) % 8 : J + (-J) % 8 + 1, at], cell, pack)
        zt[:, i * wide : (i + 1) * wide] = dot(
            q_all[:, :, at].reshape(J * slots, PT), pick, 1, 1
        ).astype(BF16)
    named = jnp.broadcast_to((ab & (BLK_DEV - 1)) + 1, (8, X * PT)).astype(F32).astype(BF16)
    by_col = dot(named, q_all[j], 1, 1)[0:1]
    copies.wait_recv()

    left = lax.rem(iota((8, wide), 1), 128) < 64
    left_row = left[0:1]

    def packs(x, rows):
        if pack == 1:
            return x
        rest = x[rows:]
        if rest.shape[0] < rows:
            rest = jnp.concatenate([rest, rest[: rows - rest.shape[0]]], axis=0)
        return jnp.where(left_row, x[:rows], rest)

    def unpacks(x, rows):
        if pack == 1:
            return x
        x = x.astype(F32)
        first = jnp.where(left_row, x, 0.0)
        rest = jnp.where(left_row, 0.0, x[: rows - x.shape[0]])
        return jnp.concatenate([first, rest], axis=0).astype(BF16)

    arrived = a_in[...].reshape(J * slots, span)
    gpt[...] = dot(arrived, zt[...], 0, 0)
    for i in range(X):
        for n in range(Z):
            b_out[i * Z + n] = packs(
                gpt[n * cw : (n + 1) * cw, i * wide : (i + 1) * wide], top
            ).astype(BF16)
    copies = send_xz(
        lambda a, b: (b_out.at[to(d, X, a) * Z + to(z, Z, b)], b_in.at[g]), b_in
    )
    b_in[g] = b_out[g]

    def fill_c(i, carry):
        place = places[pl.ds(i, 1), :]
        ids = twice_ids(cell, pack, T)
        hit = ids == place[:, 0:T]
        for k in range(1, K_BLK):
            hit = hit | (ids == place[:, k * T : (k + 1) * T])
        c_all[i] = ones(hit).astype(BF16)
        return carry

    lax.fori_loop(0, G, fill_c, 0)

    def order(n, carry):
        at = pl.ds(pl.multiple_of(n * LAT_BLOCK, LAT_BLOCK), LAT_BLOCK)
        for i in range(J):
            starts = [(m * J + i) * cw for m in range(Z)]
            dec_a[i, at, :] = jnp.concatenate([dec[at, f : f + fa] for f in starts], axis=1)
            dec_b[i, at, :] = jnp.concatenate([dec[at, f + fa : f + cw] for f in starts], axis=1)
        return carry

    lax.fori_loop(0, LATS // LAT_BLOCK, order, 0)
    over = jnp.zeros((1, 1), F32)
    part_of = min(64, G * J)
    for i in range(G * J // part_of):
        mem = ones(owner == i * part_of + iota((part_of, 1), 0))
        here = jnp.sum(mem, axis=1, keepdims=True)
        over = over + jnp.max(ones(here > slots), axis=0, keepdims=True)
    for i in range(X):
        mem = ones(group[:, i * PT : (i + 1) * PT] == iota((G, 1), 0))
        here = jnp.sum(mem, axis=1, keepdims=True)
        over = over + jnp.max(ones(here > cell), axis=0, keepdims=True)
    over_ref[0, 0] = jnp.max(over).astype(jnp.int32)

    drain()
    total = offset
    for first in by_x(copies):
        packed = jnp.concatenate([unpacks(b_in[first + n], cw) for n in range(Z)], axis=1)
        total = total + dot(packed, c_all[pl.ds(first, Z)].reshape(Z * wide, T))
    recon = total.astype(BF16)
    recon_ref[...] = recon
    recon_bf[...] = recon

    first_copies, later = [], []
    for a in sorted(range(X), key=lambda r: -near(X, r)):
        x = to(d, X, a)
        back_c = c_all[pl.ds(x * Z, Z)].reshape(Z * wide, T)
        sends = dot(recon_bf[...], back_c, 1, 1)
        for n in range(Z):
            piece = sends[:, n * wide : (n + 1) * wide]
            ba_out[x * Z + n] = packs(piece[:fa], ba_out.shape[1]).astype(BF16)
            bb_out[x * Z + n] = packs(piece[fa:], bb_out.shape[1]).astype(BF16)
        ways = [
            (x * Z + to(z, Z, b), peer)
            for (a2, b), peer in zip(xz_steps, xz_peers)
            if a2 == a
        ]
        first_copies.append(send([(ba_out.at[i], ba_in.at[g], peer) for i, peer in ways], ba_in))
        later.append([(bb_out.at[i], bb_in.at[g], peer) for i, peer in ways])
    later_copies = [send(messages, bb_in) for messages in later]
    ba_in[g] = ba_out[g]
    bb_in[g] = bb_out[g]
    if pack == 2:

        def fill_pc(i, carry):
            pc_all[i] = onehot(places[pl.ds(i, 1), :], cell)
            return carry

        lax.fori_loop(0, G, fill_pc, 0)

    def returned(copies, src, rows):
        for copy in copies:
            copy.wait_recv()
        pieces = [
            jnp.concatenate([unpacks(src[i * Z + n], rows) for i in range(X)], axis=1).astype(F32)
            for n in range(Z)
        ]
        return jnp.concatenate(pieces, axis=0).astype(BF16)

    def to_owners(full, out, dst, together):
        out[...] = dot(zt[...], full, 1, 1).astype(BF16).reshape(out.shape)
        messages = [
            (out.at[to(j, J, r)], dst.at[j], peer) for r, peer in zip(j_steps, j_peers)
        ]
        copies = [send(messages, dst)] if together else [send([m], dst) for m in messages]
        dst[j] = out[j]
        return copies

    a_copies = to_owners(returned(first_copies, ba_in, fa), aa_out, aa_in, True)
    b_copies = to_owners(returned(later_copies, bb_in, fb), ab_out, ab_in, False)
    yt[...] = dot(dec_a[j], aa_out[j], 1, 1) + dot(dec_b[j], ab_out[j], 1, 1)
    a_copies[0].wait_recv()
    for r in j_steps:
        i = frm(j, J, r)
        yt[...] += dot(dec_a[i], aa_in[i], 1, 1)
    for r, copy in reversed(list(zip(j_steps, b_copies))):
        copy.wait_recv()
        i = frm(j, J, r)
        yt[...] += dot(dec_b[i], ab_in[i], 1, 1)
    total = jnp.zeros((LAT_BLOCK, slots), F32)
    for b in range(BLK_DEV):
        total = total + jnp.where(
            by_col == b + 1.0, yt[b * LAT_BLOCK : (b + 1) * LAT_BLOCK, :], 0.0
        )
    for n in range(2):
        w_out[n] = total[n * cs : (n + 1) * cs].astype(BF16)
    copies = send(
        [
            (w_out.at[lax.rem(to(j, J, r), 2)], w_in.at[j], peer)
            for r, peer in zip(j_steps, j_peers)
        ],
        w_in,
    )
    w_in[j] = w_out[core]
    for m in range(Z // 2):
        pieces = [
            half_in[i, :, n * rows_of : (n + 1) * rows_of]
            for n in (2 * m, 2 * m + 1)
            for i in range(J)
            for half_in, rows_of in ((aa_in, fa), (ab_in, fb))
        ]
        width = 2 * J * cw
        rows[:, m * width : (m + 1) * width] = jnp.concatenate(pieces, axis=1)
    copies.wait_recv()
    merged = dot(w_in[0], zt[0:slots, :])
    for i in range(1, J):
        merged = merged + dot(w_in[i], zt[i * slots : (i + 1) * slots, :])
    for i in range(X):
        d_out[i] = packs(merged[:, i * wide : (i + 1) * wide], top_d).astype(BF16)
    copies = send_xz(lambda a, b: (d_out.at[to(d, X, a)], d_in.at[g]), d_in)
    drain()
    d_in[g] = d_out[d]
    if pack == 2:
        for at, first in enumerate(by_x(copies)):
            pieces = []
            for n in range(0, Z, 2):
                here, after = d_in[first + n].astype(F32), d_in[first + n + 1].astype(F32)
                pieces.append(
                    jnp.concatenate(
                        [
                            jnp.where(left_row, here, pltpu.roll(after, cell, 1)),
                            jnp.where(left_row, pltpu.roll(here, cell, 1), after),
                        ],
                        axis=0,
                    ).astype(BF16)
                )
            more = dot(
                jnp.concatenate(pieces, axis=1), pc_all[pl.ds(first, Z)].reshape(Z * cell, PT)
            )
            grads[...] = more if at == 0 else grads[...] + more
    else:
        for copy in copies.values():
            copy.wait_recv()
        grads[...] = jnp.zeros_like(grads)

        def gather(i, carry):
            grads[...] += dot(d_in[i], onehot(places[pl.ds(i, 1), :], cell))
            return carry

        lax.fori_loop(0, G, gather, 0)
    for k in range(K_BLK):
        g_in[core, k] = grads[:, k * T : (k + 1) * T].astype(BF16)
    copy = send([(g_in.at[core], g_in.at[core], (d, z * J + j + 1 - 2 * core))], g_in)
    copy.wait_recv()
    for k in range(K_BLK):
        for n in range(2):
            grad_ref[(2 * k + n) * cs : (2 * k + n + 1) * cs, :] = g_in[n, k]
    drain()


def exchange(X, Z, J, slots, cell, collective_id, ab, codes, act, bias, decoder):
    cw, T = act.shape
    D = decoder.shape[1]
    NT = X * T
    G = X * Z
    span = Z * cw
    cs = LAT_BLOCK // 2
    fa = -(-cw // 16) * 8
    fb = cw - fa
    PT = K_BLK * T
    pack = 128 // cell if cell < 128 else 1
    wide = cell * pack
    top = cw if pack == 1 else -(-cw // 16) * 8
    top_d = cs if pack == 1 else cs // 2
    n_copies = 4 * X + 2 * (J - 1) + 5
    vmem = pltpu.VMEM
    whole = pl.BlockSpec(memory_space=pltpu.VMEM)
    far = pl.BlockSpec(memory_space=pl.ANY)
    return pl.pallas_call(
        functools.partial(exchange_kernel, X, Z, J, slots, cell),
        out_shape=(
            jax.ShapeDtypeStruct((cw, T), BF16),
            jax.ShapeDtypeStruct((slots, D), BF16),
            jax.ShapeDtypeStruct((slots, LATS), BF16),
            jax.ShapeDtypeStruct((CODES, T), BF16),
            jax.ShapeDtypeStruct((1, 1), jnp.int32),
        ),
        in_specs=[far] * 5,
        out_specs=[whole] * 4 + [pl.BlockSpec(memory_space=pltpu.SMEM)],
        scratch_shapes=[
            vmem((K_BLK, T), jnp.int32),
            vmem((T, CODES), BF16),
            vmem((cw, T), BF16),
            vmem((1, cw), F32),
            vmem((LATS, D), BF16),
            vmem((X, K_BLK, T), jnp.int32),
            vmem((G, wide, T), BF16),
            vmem((J, slots, X * PT), BF16),
            vmem((J * slots, X * wide), BF16),
            vmem((G, PT), jnp.int32),
            vmem((X, slots, 128), BF16),
            vmem((X, slots, 128), BF16),
            vmem((slots, D), BF16),
            vmem((J, slots, span), BF16),
            vmem((J, slots, span), BF16),
            vmem((span, X * wide), F32),
            vmem((G, top, wide), BF16),
            vmem((G, top, wide), BF16),
            vmem((cw, T), BF16),
            vmem((G, fa // pack + (-(fa // pack)) % 8, wide), BF16),
            vmem((G, fa // pack + (-(fa // pack)) % 8, wide), BF16),
            vmem((G, fb // pack, wide), BF16),
            vmem((G, fb // pack, wide), BF16),
            vmem((J, slots, Z * fa), BF16),
            vmem((J, slots, Z * fa), BF16),
            vmem((J, slots, Z * fb), BF16),
            vmem((J, slots, Z * fb), BF16),
            vmem((J, LATS, Z * fa), BF16),
            vmem((J, LATS, Z * fb), BF16),
            vmem((LATS, slots), F32),
            vmem((2, cs, slots), BF16),
            vmem((J, cs, slots), BF16),
            vmem((X, top_d, wide), BF16),
            vmem((G, top_d, wide), BF16),
            vmem((G if pack == 2 else 1, cell, PT), BF16),
            vmem((cs, PT), F32),
            vmem((2, K_BLK, cs, T), BF16),
            pltpu.SemaphoreType.DMA((n_copies,)),
            pltpu.SemaphoreType.DMA((n_copies,)),
            pltpu.SemaphoreType.DMA((5,)),
        ],
        compiler_params=pltpu.CompilerParams(
            collective_id=collective_id,
            has_side_effects=True,
            vmem_limit_bytes=52 * 2**20,
        ),
        name="exchange_%d_%d" % (slots, cell),
    )(ab, codes, act, bias, decoder)


def finish_kernel(
    recon_in, rows, own, grad_in, recon_out, dgrad_out, grad_out, dgrad, grad, sem
):
    copies = [pltpu.make_async_copy(recon_in, recon_out, sem.at[0])]
    copies[0].start()
    parts = sem.shape[0] - 2
    height = LATS // parts
    for n in range(parts):
        at = slice(n * height, (n + 1) * height)
        dgrad[at, :] = dot(own[:, at], rows[...], 0, 0).astype(BF16)
        copies.append(pltpu.make_async_copy(dgrad.at[at], dgrad_out.at[at], sem.at[2 + n]))
        copies[-1].start()
        if n == 0:
            grad[...] = grad_in[...].T
            copies.append(pltpu.make_async_copy(grad, grad_out, sem.at[1]))
            copies[-1].start()
    for copy in copies:
        copy.wait()


def finish(recon, rows, own, grad):
    slots, D = rows.shape
    CO, T = grad.shape
    whole = pl.BlockSpec(memory_space=pltpu.VMEM)
    far = pl.BlockSpec(memory_space=pl.ANY)
    return pl.pallas_call(
        finish_kernel,
        out_shape=(
            jax.ShapeDtypeStruct(recon.shape, BF16),
            jax.ShapeDtypeStruct((LATS, D), BF16),
            jax.ShapeDtypeStruct((T, CO), BF16),
        ),
        in_specs=[whole] * 4,
        out_specs=[far] * 3,
        scratch_shapes=[
            pltpu.VMEM((LATS, D), BF16),
            pltpu.VMEM((T, CO), BF16),
            pltpu.SemaphoreType.DMA((10,)),
        ],
        compiler_params=pltpu.CompilerParams(vmem_limit_bytes=32 * 2**20),
        cost_estimate=pl.CostEstimate(
            flops=2 * slots * LATS * D, bytes_accessed=2 * LATS * D, transcendentals=0
        ),
        name="finish_%d" % slots,
    )(recon, rows, own, grad)


def per_device(J, activations, latent_codes, active_blocks, decoder, decoder_bias):
    X = lax.axis_size("dp")
    Z = lax.axis_size("latent") // J
    T = activations.shape[0]
    args = (active_blocks.T, latent_codes, activations.T, decoder_bias[None, :], decoder)
    *fast, over = exchange(X, Z, J, 40, 64, 0, *args)

    def roomy():
        return finish(*exchange(X, Z, J, MOST_DEV, J * MOST_DEV, 1, *args)[:4])

    recon, decoder_grad, grad = lax.cond(over[0, 0] > 0, roomy, lambda: finish(*fast))
    return recon.T, decoder_grad, grad


def solution(mesh):
    in_specs = (
        P("dp", "latent"),
        P("dp", None),
        P("dp", None),
        P(("dp", "latent"), None),
        P("latent"),
    )
    out_specs = (P("dp", "latent"), P(("dp", "latent"), None), P("dp", None))
    J = 8 if mesh.shape["latent"] >= 16 else 4
    return jax.shard_map(
        functools.partial(per_device, J),
        mesh=mesh, in_specs=in_specs, out_specs=out_specs, check_vma=False,
    )
```
